256 devices in a mesh: row: 8 (over y_hi, x), col: 32 (over y_lo, z, core).
Axes of the slice: x: 4, y: 4 (y_hi: 2, y_lo: 2; y = y_hi * 2 + y_lo), z: 8, core: 2. Of those that a mesh axis runs over, the one named last changes fastest.
Arguments:
- features: bfloat16 [1, 512, 1024, 128], P(None, 'row', 'col'), may hold values from -6 to 6
- conv_mid: bfloat16 [3, 3, 128, 128], replicated, may hold values from -0.1875 to 0.1875
- conv_out: bfloat16 [3, 3, 128, 3], replicated, may hold values from -0.5 to 0.5
- target: bfloat16 [1, 512, 1024, 3], P(None, 'row', 'col'), may hold values from -6 to 6
- vgg_first: bfloat16 [3, 3, 3, 64], replicated, may hold values from -1.25 to 1.25
- vgg_second: bfloat16 [3, 3, 64, 64], replicated, may hold values from -0.25 to 0.25
- perceptual_weights: float32 [64], replicated, may hold values from 0.2 to 2
- crop_anchors: int32 [1, 64, 2], replicated, may hold values from 0 to 768, as said below
- crop_owner: int32 [1, 64, 1], replicated, may hold values from 0 to 31; in each aligned block of 64 rows (0 to 63, 64 to 127, ..., all dimensions but the last counted through in order) at most 5 rows name the same one
- critic_first: bfloat16 [32, 4, 4, 3, 64], P('col'), may hold values from -0.875 to 0.875
- critic_second: bfloat16 [32, 4, 4, 64, 128], P('col'), may hold values from -0.1875 to 0.1875
- critic_score: bfloat16 [32, 128], P('col'), may hold values from -0.5 to 0.5
Outputs:
- decoder_grad: bfloat16 [1, 512, 1024, 128], P(None, 'row', 'col')
The draws below stay inside these ranges and needn't reach their ends.
Inputs may be any that keep to these rules, and one draw needn't show every extreme that they name: `crop_anchors`: [..., 0] is a top row, at most 256; [..., 1] a left column, at most 768; both reach 0 and their largest value. `crop_owner`: every critic scores at least one crop and none more than 5; one scores exactly 5.
All inputs are finite; a program needn't handle non-finite values.
Results may differ from the reference program's by a relative error of at most 0.017.
Values may be sent and summed in bfloat16 or wider, within the bound.
No kernel may reach another device: no remote copies, remote signals or barrier semaphores. Data moves between devices by JAX's collectives and lax.ppermute only.
A program may use at most 128 MiB of HBM per device.

```python
import math
import jax
import jax.numpy as jnp
import numpy as np
from jax import lax

C = 128
VGG_C = 64
D1 = 64
D2 = 128
B = 1
CROP = 256
H = 512
W = 1024
CROPS = 64
CPI = 64
CAP = 5
DISCS = 32
N_COL = 32


def draw_crop_anchors(key, part):
    key = jax.random.fold_in(key, 7)
    subkeys = jax.random.split(key, 4)
    count = B * CPI
    top_rows = jax.random.randint(subkeys[0], (count,), 0, H - CROP + 1)
    left_cols = jax.random.randint(subkeys[1], (count,), 0, W - CROP + 1)
    row_order = jax.random.permutation(subkeys[2], count)
    col_order = jax.random.permutation(subkeys[3], count)
    top_rows = top_rows.at[row_order[0]].set(H - CROP)
    top_rows = top_rows.at[row_order[1]].set(0)
    top_rows = top_rows.at[row_order[2]].set((H - CROP) // 2)
    left_cols = left_cols.at[col_order[0]].set(W - CROP)
    left_cols = left_cols.at[col_order[1]].set(0)
    return jnp.stack([top_rows, left_cols], -1).reshape(B, CPI, 2).astype(jnp.int32)


def level_of(rng, dims, cuts, least, top_value):
    loudness = 1.0
    for position, shards_of in cuts:
        steps = jax.random.uniform(jax.random.fold_in(jax.random.fold_in(rng, 6), position), (shards_of,), jnp.float32, least / len(cuts), top_value / len(cuts))
        loudness = loudness * jnp.repeat(jnp.exp(steps), dims[position] // shards_of).reshape((-1,) + (1,) * (len(dims) - 1 - position))
    return loudness


def assign_block(key, own, number, rows, amount, top, limit, lean):
    order = jax.random.permutation(key, amount)
    crowded, common = shares(amount, rows * top, limit, lean, True), shares(amount, rows * top, limit, lean, False)
    places = jnp.arange(amount)

    def named(tallies, rotation):
        used = int((tallies > 0).sum())
        fixed = max(1, used // 4)
        moved = fixed + (places - fixed + rotation * (used - fixed)) % max(1, amount - fixed)
        return jnp.zeros((amount,), jnp.int32).at[order[jnp.where(places < fixed, places, moved)]].set(jnp.asarray(tallies, jnp.int32))

    tallies = jnp.where(number % 4 == 0, named(crowded, number // 4), named(common, number - number // 4 - 1))
    mixed = jax.random.permutation(jax.random.fold_in(own, 3), amount)
    donor, receiver = mixed[0:amount // 2 * 2:2], mixed[1:amount // 2 * 2:2]
    slack = jnp.minimum(tallies[donor] - 1, limit - tallies[receiver]) // 2
    slack = jnp.where((donor == order[0]) | (receiver == order[0]) | (tallies[receiver] == 0), 0, jnp.maximum(slack, 0))
    moved = jax.random.randint(jax.random.fold_in(own, 4), (amount // 2,), 0, 1 << 20) % (slack + 1)
    tallies = tallies.at[donor].add(-moved).at[receiver].add(moved)
    labels = jnp.searchsorted(jnp.cumsum(tallies), jnp.arange(rows * top), side="right").astype(jnp.int32)
    grid = labels.reshape(top, rows).T
    grid = grid[jax.random.permutation(jax.random.fold_in(own, 1), rows)]
    rotation = jax.random.randint(jax.random.fold_in(own, 2), (rows, 1), 0, top)
    return jnp.take_along_axis(grid, (jnp.arange(top)[None, :] + rotation) % top, axis=1)


def shares(number_of, total, bound, slope, full):
    weights = [(1 << 20) // math.isqrt(standing ** slope) + 1 for standing in range(1, number_of + 1)]
    largest = bound if full else min(bound, max(-(-total // number_of), total * weights[0] // sum(weights)))
    least = 1 if total - largest >= number_of - 1 else 0
    counts, surplus = [largest] + [least] * (number_of - 1), total - largest - least * (number_of - 1)
    while surplus > 0:
        movable = [i for i in range(1, number_of) if counts[i] < largest] or [i for i in range(1, number_of) if counts[i] < bound]
        pool, left = sum([weights[i] for i in movable]), surplus
        for i in movable:
            more = min(bound - counts[i], max(1, left * weights[i] // pool), surplus)
            counts[i] = counts[i] + more
            surplus = surplus - more
    return np.array(counts)


def scatter_about(stream_key, dims, width, reach, cuts=(), kind=jnp.bfloat16):
    array = jax.random.normal(stream_key, dims, jnp.float32) * width
    if len(cuts) > 0:
        array = level_of(stream_key, dims, cuts, -0.22, 0.18) * array
    return jnp.clip(array, min=-reach, max=reach).astype(kind)


def setup_inputs(seed: int = 0) -> dict:
    seeds = jax.random.split(jax.random.key(seed), 13)
    features = scatter_about(seeds[0], (B, H, W, C), 1.0, 6.0, ((1, 8), (2, 32)))
    conv_mid = scatter_about(seeds[1], (3, 3, C, C), (9 * C) ** -0.5, 0.1875)
    conv_out = scatter_about(seeds[2], (3, 3, C, 3), C ** -0.5, 0.5)
    target = scatter_about(seeds[3], (B, H, W, 3), 1.0, 6.0, ((1, 8), (2, 32)))
    vgg_first = scatter_about(seeds[4], (3, 3, 3, VGG_C), 27 ** -0.5, 1.25)
    vgg_second = scatter_about(seeds[5], (3, 3, VGG_C, VGG_C), (9 * VGG_C) ** -0.5, 0.25)
    perceptual_weights = jnp.clip(jnp.exp(jax.random.uniform(seeds[6], (VGG_C,), jnp.float32, math.log(0.2), math.log(2.0))), 0.2, 2.0)
    crop_anchors = draw_crop_anchors(jax.random.fold_in(seeds[12], 71), 0)
    crop_owner_keys = jax.random.split(jax.random.fold_in(seeds[8], 1), B * CPI // CROPS)
    crop_owner_turns = jax.random.permutation(jax.random.fold_in(seeds[8], 3), B * CPI // CROPS)
    crop_owner = jax.vmap(lambda own, number: assign_block(jax.random.fold_in(seeds[8], 2), own, number, CROPS, N_COL, 1, CAP, 2))(crop_owner_keys, crop_owner_turns).reshape((B, CPI, 1))
    critic_first = scatter_about(seeds[9], (DISCS, 4, 4, 3, D1), 48 ** -0.5, 0.875, ((0, 32),))
    critic_second = scatter_about(seeds[10], (DISCS, 4, 4, D1, D2), (16 * D1) ** -0.5, 0.1875, ((0, 32),))
    critic_score = scatter_about(seeds[11], (DISCS, D2), D2 ** -0.5, 0.5, ((0, 32),))
    return {"features": features, "conv_mid": conv_mid, "conv_out": conv_out, "target": target, "vgg_first": vgg_first, "vgg_second": vgg_second, "perceptual_weights": perceptual_weights, "crop_anchors": crop_anchors, "crop_owner": crop_owner, "critic_first": critic_first, "critic_second": critic_second, "critic_score": critic_score}


LOSS_SCALE = 32.0
EPSILON = 1e-06
CONV_LAYOUT = ('NHWC', 'HWIO', 'NHWC')

def conv_same(inputs, weight):
    return lax.conv_general_dilated(inputs, weight, (1, 1), ((1, 1), (1, 1)), dimension_numbers=CONV_LAYOUT, preferred_element_type=jnp.float32)

def flipped(weight):
    return jnp.swapaxes(jnp.flip(weight, (0, 1)), 2, 3)

def conv_down(inputs, weight):
    return lax.conv_general_dilated(inputs, weight, (2, 2), ((1, 1), (1, 1)), dimension_numbers=CONV_LAYOUT, preferred_element_type=jnp.float32)

def conv_up(grads, weight):
    return lax.conv_general_dilated(grads, flipped(weight), (1, 1), ((2, 2), (2, 2)), lhs_dilation=(2, 2), dimension_numbers=CONV_LAYOUT, preferred_element_type=jnp.float32)

def silu_slope(value):
    sigma = jax.nn.sigmoid(value)
    return sigma * (1.0 + value * (1.0 - sigma))

def perceptual_grad(pre_x, pre_y, weights):
    feat_x = jax.nn.silu(pre_x)
    feat_y = jax.nn.silu(pre_y)
    scale_x = lax.rsqrt(lax.optimization_barrier(jnp.sum(feat_x * feat_x, -1, keepdims=True)) + EPSILON)
    scale_y = lax.rsqrt(lax.optimization_barrier(jnp.sum(feat_y * feat_y, -1, keepdims=True)) + EPSILON)
    unit_x = feat_x * scale_x
    unit_y = feat_y * scale_y
    weighted = 2.0 * LOSS_SCALE * weights * (unit_x - unit_y)
    grads = scale_x * (weighted - unit_x * lax.optimization_barrier(jnp.sum(weighted * unit_x, -1, keepdims=True)))
    return (grads * silu_slope(pre_x)).astype(jnp.bfloat16)

def critic_grad(crop, first, second, score):
    pre_one = conv_down(crop, first)
    act_one = jax.nn.silu(pre_one).astype(jnp.bfloat16)
    pre_two = conv_down(act_one, second)
    score_f = score.astype(jnp.float32)
    logit = lax.optimization_barrier(jnp.sum(jax.nn.silu(pre_two) * score_f, -1, keepdims=True))
    logit_grad = -LOSS_SCALE * jax.nn.sigmoid(-logit)
    back_two = (logit_grad * score_f * silu_slope(pre_two)).astype(jnp.bfloat16)
    back_one = (conv_up(back_two, second) * silu_slope(pre_one)).astype(jnp.bfloat16)
    return conv_up(back_one, first)

def reference(features, conv_mid, conv_out, target, vgg_first, vgg_second, perceptual_weights, crop_anchors, crop_owner, critic_first, critic_second, critic_score):
    feature_float = features.astype(jnp.float32)
    silu_in = jax.nn.silu(feature_float).astype(jnp.bfloat16)
    middle = conv_same(silu_in, conv_mid)
    decoded = conv_same(jax.nn.silu(middle).astype(jnp.bfloat16), conv_out).astype(jnp.bfloat16)
    stacked = jnp.concatenate([decoded, target], 0)
    vgg_pre = conv_same(stacked, vgg_first)
    vgg_one = jax.nn.silu(vgg_pre).astype(jnp.bfloat16)
    vgg_pre_two = conv_same(vgg_one, vgg_second)
    back_feat = perceptual_grad(vgg_pre_two[:B], vgg_pre_two[B:], perceptual_weights)
    back_vgg = (conv_same(back_feat, flipped(vgg_second)) * silu_slope(vgg_pre[:B])).astype(jnp.bfloat16)
    lpips_back = conv_same(back_vgg, flipped(vgg_first))
    flat_anchor = crop_anchors.reshape(-1, 2)
    flat_owner = crop_owner.reshape(-1)
    per_image = crop_anchors.shape[1]
    zero_index = jnp.zeros((), jnp.int32)

    def one_crop(total_grad, crop_index):
        image = (crop_index // per_image).astype(jnp.int32)
        top_row = flat_anchor[crop_index, 0].astype(jnp.int32)
        left_col = flat_anchor[crop_index, 1].astype(jnp.int32)
        owner = flat_owner[crop_index]
        corner = (image, top_row, left_col, zero_index)
        crop = lax.dynamic_slice(decoded, corner, (1, CROP, CROP, 3))
        grads = critic_grad(crop, critic_first[owner], critic_second[owner], critic_score[owner])
        previous = lax.dynamic_slice(total_grad, corner, (1, CROP, CROP, 3))
        return (lax.dynamic_update_slice(total_grad, previous + grads, corner), None)
    start = jnp.zeros((B, H, W, 3), jnp.float32)
    gan_back, _ = lax.scan(one_crop, start, jnp.arange(flat_owner.shape[0], dtype=jnp.int32))
    image_back = (lpips_back + gan_back).astype(jnp.bfloat16)
    back_mid = (conv_same(image_back, flipped(conv_out)) * silu_slope(middle)).astype(jnp.bfloat16)
    decoder_grad = conv_same(back_mid, flipped(conv_mid)) * silu_slope(feature_float)
    return decoder_grad.astype(jnp.bfloat16)
```

```python
import jax
import jax.numpy as jnp
import numpy as np
from jax import lax
from jax.experimental import pallas as pl
from jax.experimental.pallas import tpu as pltpu
from jax.sharding import PartitionSpec as P

BF = jnp.bfloat16
F32 = jnp.float32

LOSS_SCALE = 32.0
EPSILON = 1e-06
CROP = 256
TH, TW = 64, 32
IMG_H, IMG_W = 512, 1024
ROWS, COLS = 8, 32
CROPS = 64
DEC_HALO = 11
FEAT_HALO = 13
COL_HALO = 8
WIDE = TW + 2 * COL_HALO
TGT_HALO = 6
GRAD_PAD = 10
VMEM = 56 * 1024 * 1024


def sigmoid(v):
    return 0.5 * jnp.tanh(0.5 * v) + 0.5


def silu_parts(v):
    sig = sigmoid(v)
    act = v * sig
    return act, sig + act * (1.0 - sig)


def mm(a, b, ca=1, cb=0):
    return lax.dot_general(a, b, (((ca,), (cb,)), ((), ())), preferred_element_type=F32)


def iota(shape, dim):
    return lax.broadcasted_iota(jnp.int32, shape, dim)


def aligned(start, unit):
    return pl.multiple_of(start, unit) if not isinstance(start, int) else start


def conv_rows(src, row0, rows, weight, transposed=False, shift=0):
    n = rows * WIDE
    lhs = jnp.concatenate(
        [src[pl.ds(aligned((row0 + dy) * WIDE, 16), n), :] for dy in range(3)], axis=1
    )
    z = mm(lhs, weight, 1, 1 if transposed else 0)
    parts = []
    for dx in range(3):
        amount = (1 - dx - shift) % n
        part = z[:, dx * 128 : (dx + 1) * 128]
        parts.append(pltpu.roll(part, amount, 0) if amount else part)
    return parts[0] + parts[1] + parts[2]


def inside(row_first, col_first, rows):
    y = row_first + iota((rows, WIDE, 1), 0)
    x = col_first + iota((rows, WIDE, 1), 1)
    ok = (y >= 0) & (y < IMG_H) & (x >= 0) & (x < IMG_W)
    return ok.astype(F32).reshape(rows * WIDE, 1) > 0.0


def lanes_inside(row, col_first, low, high):
    lane = iota((8, 128), 1)
    x = col_first + lane
    return (x >= 0) & (x < IMG_W) & (lane >= low) & (lane < high) & (row >= 0) & (row < IMG_H)


def fold_taps(z, first, shift):
    total = None
    for dx in range(3):
        part = None
        for dy in range(3):
            k = (dx * 3 + dy) * 8
            piece = z[first + dy, k : k + 8, :]
            part = piece if part is None else part + piece
        amount = (1 - dx - shift) % 128
        part = pltpu.roll(part, amount, 1) if amount else part
        total = part if total is None else total + part
    return total


def three_shifts(v):
    return jnp.concatenate(
        [pltpu.roll(v, 1, 1), v, pltpu.roll(v, 127, 1), jnp.zeros_like(v)], axis=0
    ).astype(BF)


def decode_kernel(
    where, top, mid, bot, left, right, w_mid, w_out, pay, dec, slope_out, s1, s2, z, w
):
    r, c = where[0], where[1]
    for dy in range(3):
        for dx in range(3):
            w[dy * 128 : (dy + 1) * 128, dx * 128 : (dx + 1) * 128] = w_mid[dy, dx]

    def fill(first, rows, centre):
        n = rows * WIDE
        parts = [left[pl.ds(first, rows)], centre, right[pl.ds(first, rows)]]
        v = jnp.concatenate([p.astype(F32) for p in parts], axis=1).reshape(n, 128)
        s1[pl.ds(aligned(first * WIDE, 16), n), :] = (v * sigmoid(v)).astype(BF)

    fill(0, FEAT_HALO, top[...])
    fill(FEAT_HALO + TH, FEAT_HALO, bot[...])

    def fill_mid(i, carry):
        fill(FEAT_HALO + i * 8, 8, mid[pl.ds(i * 8, 8)])
        return carry

    lax.fori_loop(0, TH // 8, fill_mid, 0)

    def middle(i, carry):
        v = conv_rows(s1, i * 8, 8, w[...])
        act, slope = silu_parts(v)
        ok = inside(r * TH - 12 + i * 8, c * TW - COL_HALO, 8)
        s2[pl.ds(aligned(i * 8 * WIDE, 16), 8 * WIDE), :] = jnp.where(ok, act, 0.0).astype(BF)
        slope_out[pl.ds(i * 8, 8)] = (
            pltpu.roll(slope, 8 * WIDE - 6, 0).reshape(8, WIDE, 128).astype(BF)
        )
        return carry

    lax.fori_loop(0, 11, middle, 0)

    def taps(i, carry):
        for k in range(4):
            m = i * 4 + k
            z[m, :, 0:WIDE] = mm(w_out[...], s2[pl.ds(aligned(m * WIDE, 16), WIDE), :], 1, 1)
        return carry

    lax.fori_loop(0, 22, taps, 0)
    dec[86 * 8 :, :] = jnp.zeros((1024 - 86 * 8, 128), F32)

    def fold(i, carry):
        for k in range(2):
            d = i * 2 + k
            ok = lanes_inside(r * TH - DEC_HALO + d, c * TW - COL_HALO, 2, WIDE - 2)
            v = jnp.where(ok, fold_taps(z, d, 0), 0.0)
            dec[pl.ds(aligned(d * 8, 8), 8), :] = v.astype(BF).astype(F32)
        return carry

    lax.fori_loop(0, 43, fold, 0)
    planes = [
        dec[pl.ds(k, 128, stride=8), :].T[COL_HALO : COL_HALO + TW, :].astype(BF) for k in range(3)
    ]
    packed = jnp.concatenate(planes, axis=1)
    for k in range(COLS):
        pay[k] = packed


def percept_kernel(
    where, dec, tgt, w_first, w_second, w_back, w_last, weights, out, d3, pre, one, feat, bv, z
):
    r, c = where[0], where[1]
    col_first = c * TW - COL_HALO

    def gather(i, carry):
        for k in range(2):
            q = i * 2 + k
            v = dec[pl.ds(aligned((q + 5) * 8, 8), 8), :] + tgt[pl.ds(aligned(q * 8, 8), 8), :]
            d3[pl.ds(aligned(q * 32, 32), 32), :] = three_shifts(v)
        return carry

    lax.fori_loop(0, 38, gather, 0)

    def first(i, carry):
        for k in range(2):
            p = i * 2 + k
            v = mm(d3[pl.ds(aligned(p * 32, 32), 96), 0:WIDE], w_first[...], 0, 0)
            act = v * sigmoid(v)
            ok = inside(r * TH - 5 + p, col_first, 1)
            pre[pl.ds(aligned(p * WIDE, 16), WIDE), :] = v
            one[pl.ds(aligned(p * WIDE, 16), WIDE), :] = jnp.where(ok, act, 0.0).astype(BF)
        return carry

    lax.fori_loop(0, 37, first, 0)
    ones = ((iota((128, 128), 0) >> 6) == (iota((128, 128), 1) >> 6)).astype(F32).astype(BF)

    def half_sum(v):
        high = v.astype(BF)
        low = (v - high.astype(F32)).astype(BF)
        return mm(high, ones) + mm(low, ones)

    def second(i, carry):
        v = conv_rows(one, i * 8, 8, w_second[...])
        f, slope = silu_parts(v)
        scale = lax.rsqrt(half_sum(f * f) + EPSILON)
        unit = f * scale
        weighted = weights[...] * (unit - pltpu.roll(unit, 64, 1))
        g = scale * (weighted - unit * half_sum(weighted * unit)) * slope
        ok = inside(r * TH - 4 + i * 8, col_first, 8)
        feat[pl.ds(aligned(i * 8 * WIDE, 16), 8 * WIDE), :] = jnp.where(ok, g, 0.0).astype(BF)
        return carry

    lax.fori_loop(0, 9, second, 0)

    def back(i, carry):
        v = conv_rows(feat, i * 10, 10, w_back[...])
        x = pre[pl.ds(aligned((i * 10 + 2) * WIDE, 16), 10 * WIDE), :]
        v = v * silu_parts(x)[1]
        ok = inside(r * TH - 3 + i * 10, col_first, 10)
        bv[pl.ds(aligned(i * 10 * WIDE, 16), 10 * WIDE), :] = jnp.where(ok, v, 0.0).astype(BF)
        return carry

    lax.fori_loop(0, 7, back, 0)

    def taps(i, carry):
        for k in range(5):
            m = i * 5 + k
            z[m, :, 0:WIDE] = mm(w_last[...], bv[pl.ds(aligned(m * WIDE, 16), WIDE), :], 1, 1)
        return carry

    lax.fori_loop(0, 14, taps, 0)

    def fold(i, carry):
        for k in range(2):
            m = i * 2 + k
            out[pl.ds(aligned(m * 8, 8), 8), :] = fold_taps(z, m, 6)
        return carry

    lax.fori_loop(0, 34, fold, 0)


TILES = 22
LANES = TILES * 128


def critic_kernel(
    where, anchors, owners, strip, pick, rows_of, rows_back, w_first, w_second, score, out,
    strip32, grads, w_back, x_all, pre, act, two, cols,
):
    r, me = where[0], where[1]
    strip32[0:IMG_W, :] = strip[...].astype(F32)
    strip32[IMG_W:, :] = jnp.zeros((8, 384), F32)
    grads[...] = jnp.zeros(grads.shape, F32)
    w_back[...] = jnp.zeros(w_back.shape, BF)
    for par in range(2):
        for p in range(2):
            for t in range(2):
                i = par + 2 * t
                for kind, j in ((0, 1 + p), (1 + p, 3 - 3 * p)):
                    w_back[
                        (par * 2 + p) * 64 : (par * 2 + p + 1) * 64,
                        (t * 3 + kind) * 128 : (t * 3 + kind + 1) * 128,
                    ] = w_second[i, j * 64 : (j + 1) * 64, :]
    two[:, 0:128] = jnp.zeros((384, 128), BF)
    two[:, 11 * 128 :] = jnp.zeros((384, 128), BF)
    lane = iota((1, 128), 1)
    upper = lane >= 64
    first_x = (lane & 63) == 0
    last_x = (lane & 63) == 63
    wide_lane = iota((1, 384), 1) & 127

    def score_crop(top, left):
        y0 = r * TH - 2 - top
        v0 = lax.shift_right_arithmetic(y0 - 3, 2)
        e = 4 * v0 - y0 + 6
        crop_row = y0 - 9 + wide_lane
        in_crop = (crop_row >= 0) & (crop_row < CROP)
        window = strip32[pl.ds(aligned((left >> 3) * 8, 8), CROP + 8), :]
        window = pltpu.roll(window, lax.rem((CROP + 8) - (left & 7), CROP + 8), 0)[0:CROP]
        window = jnp.where(in_crop, window, 0.0).astype(BF)
        cols_of = mm(window, pick[...], 0, 0)
        halves = [
            jnp.concatenate(
                [cols_of[k * 128 + 40 * h : k * 128 + 40 * h + 64, :] for k in range(3)], axis=0
            )
            for h in range(2)
        ]
        mixed = []
        for m in range(6):
            tile = slice((m // 2) * 128, (m // 2 + 1) * 128)
            low, high = halves[0][:, tile], halves[1][:, tile]
            if m % 2 == 0:
                high = pltpu.roll(high, 64, 1)
            else:
                low = pltpu.roll(low, 64, 1)
            mixed.append(jnp.where(upper, high, low))
        patches = mm(rows_of[e], jnp.concatenate(mixed, axis=1).astype(BF)).astype(BF)
        for t in range(TILES):
            for m in range(6):
                x_all[m * 16 : (m + 1) * 16, t * 128 : (t + 1) * 128] = patches[
                    t * 16 : (t + 1) * 16, m * 128 : (m + 1) * 128
                ]
        pre[...] = mm(w_first[...], x_all[...], 0, 0)

        def activate(s, carry):
            for par in range(2):
                at = pl.ds(aligned((par * 11 + s) * 128, 128), 128)
                n = 2 * s + par + jnp.where(upper, 20, 0)
                u = 2 * v0 - 1 + n
                ok = (u >= 0) & (u < CROP // 2)
                a, slope = silu_parts(pre[:, at])
                a = jnp.where(ok, a, 0.0)
                pre[:, at] = jnp.where(ok, slope, 0.0)
                even, odd = a[:64], a[64:]
                act[0:64, at] = jnp.where(first_x, 0.0, pltpu.roll(odd, 1, 1)).astype(BF)
                act[64:128, at] = even.astype(BF)
                act[128:192, at] = odd.astype(BF)
                act[192:256, at] = jnp.where(last_x, 0.0, pltpu.roll(even, 127, 1)).astype(BF)
            return carry

        lax.fori_loop(0, 11, activate, 0)
        pre_two = mm(w_second[0], act[:, 0:1280], 0, 0)
        pre_two = pre_two + mm(w_second[1], act[:, 1408 : 1408 + 1280], 0, 0)
        pre_two = pre_two + mm(w_second[2], act[:, 128 : 128 + 1280], 0, 0)
        pre_two = pre_two + mm(w_second[3], act[:, 1408 + 128 : 1408 + 1408], 0, 0)
        for t in range(10):
            f, slope = silu_parts(pre_two[:, t * 128 : (t + 1) * 128])
            logit = jnp.sum(f * score[...], axis=0, keepdims=True)
            v = v0 + t + jnp.where(upper, 10, 0)
            ok = (v >= 0) & (v < CROP // 4)
            grad = jnp.where(ok, -LOSS_SCALE * sigmoid(-logit), 0.0)
            b = grad * score[...] * slope
            at = slice((t + 1) * 128, (t + 2) * 128)
            two[0:128, at] = b.astype(BF)
            two[128:256, at] = jnp.where(first_x, 0.0, pltpu.roll(b, 1, 1)).astype(BF)
            two[256:384, at] = jnp.where(last_x, 0.0, pltpu.roll(b, 127, 1)).astype(BF)
        up = mm(w_back[...], jnp.concatenate([two[:, 128:], two[:, 0 : 11 * 128]], axis=0))
        one = jnp.concatenate(
            [(up[0:128] * pre[:, 0:1408]).astype(BF), (up[128:256] * pre[:, 1408:]).astype(BF)],
            axis=1,
        )
        x_all[...] = mm(w_first[...], one).astype(BF)
        spread = jnp.concatenate(
            [
                jnp.concatenate(
                    [
                        x_all[m * 16 : (m + 1) * 16, t * 128 : (t + 1) * 128]
                        for t in range(TILES)
                    ],
                    axis=0,
                )
                for m in range(6)
            ],
            axis=1,
        )
        back = mm(rows_back[e], spread)
        cols[...] = jnp.zeros(cols.shape, F32)
        for h in range(2):
            tiles = []
            for k in range(3):
                low = back[:, 2 * k * 128 : (2 * k + 1) * 128]
                high = back[:, (2 * k + 1) * 128 : (2 * k + 2) * 128]
                if h == 0:
                    high = pltpu.roll(high, 64, 1)
                else:
                    low = pltpu.roll(low, 64, 1)
                tiles.append(jnp.where(upper, high, low))
            part = jnp.concatenate(tiles, axis=1)
            for k in range(3):
                at = slice(k * 128 + 40 * h, k * 128 + 40 * h + 64)
                cols[at, :] = cols[at, :] + part[k * 64 : (k + 1) * 64, :]
        placed = mm(pick[...], cols[...].astype(BF), 1, 1)
        keep = in_crop & (wide_lane >= 9) & (wide_lane < 77)
        placed = jnp.concatenate([jnp.where(keep, placed, 0.0), jnp.zeros((8, 384), F32)], axis=0)
        start = left + GRAD_PAD
        here = pl.ds(aligned((start >> 3) * 8, 8), CROP + 8)
        grads[here, :] = grads[here, :] + pltpu.roll(placed, start & 7, 0)

    def one_crop(q, carry):
        top, left = anchors[q, 0], anchors[q, 1]
        y0 = r * TH - 2 - top

        @pl.when((owners[q] == me) & (y0 < CROP) & (y0 + TH + 4 > 0))
        def _():
            score_crop(top, left)

        return carry

    lax.fori_loop(0, CROPS, one_crop, 0)

    def pack(k, carry):
        block = grads[pl.ds(aligned(k * TW + 8, 8), 40), :]
        a = pltpu.roll(block[:, 0:128], 128 - 9, 1)
        b = pltpu.roll(block[:, 128:256], 63, 1)
        d = pltpu.roll(block[:, 256:384], 7, 1)
        out[k] = jnp.concatenate(
            [jnp.where(lane < 72, a, b), jnp.where(lane < 16, b, d)], axis=1
        ).astype(BF)
        return carry

    lax.fori_loop(0, COLS, pack, 0)


def finish_kernel(
    where, parts, lpips, slope, feats, w_mid, w_out, out, square, turned, planes, ib, bm, w
):
    r, c = where[0], where[1]
    for dy in range(3):
        for dx in range(3):
            w[dx * 128 : (dx + 1) * 128, dy * 128 : (dy + 1) * 128] = w_mid[2 - dy, 2 - dx]
    total = parts[0].astype(F32)
    for k in range(1, COLS):
        total = total + parts[k].astype(F32)
    square[...] = jnp.zeros(square.shape, F32)
    square[0:40, :] = total
    turned[...] = square[...].T
    planes[...] = jnp.zeros(planes.shape, F32)
    for k in range(3):
        planes[pl.ds(k, 72, stride=8), :] = turned[k * 72 : (k + 1) * 72, :]

    def gather(i, carry):
        for k in range(2):
            m = i * 2 + k
            at = pl.ds(aligned(m * 8, 8), 8)
            ok = lanes_inside(r * TH - 2 + m, c * TW - 2, 0, 36)
            v = jnp.where(ok, lpips[at, :] + planes[at, :], 0.0)
            ib[pl.ds(aligned(m * 32, 32), 32), :] = three_shifts(v)
        return carry

    lax.fori_loop(0, 34, gather, 0)

    def middle(i, carry):
        for k in range(2):
            n = i * 2 + k
            v = mm(ib[pl.ds(aligned(n * 32, 32), 96), 0:WIDE], w_out[...], 0, 0)
            v = v * slope[n + 11].astype(F32)
            ok = inside(r * TH - 1 + n, c * TW - 2, 1)
            bm[pl.ds(aligned(n * WIDE, 16), WIDE), :] = jnp.where(ok, v, 0.0).astype(BF)
        return carry

    lax.fori_loop(0, 33, middle, 0)

    def last(i, carry):
        v = conv_rows(bm, i * 8, 8, w[...], transposed=True, shift=2)
        v = v.reshape(8, WIDE, 128)[:, 0:TW, :]
        x = feats[pl.ds(i * 8, 8)].astype(F32)
        out[pl.ds(i * 8, 8)] = (v * silu_parts(x)[1]).astype(BF)
        return carry

    lax.fori_loop(0, TH // 8, last, 0)


def call(kernel, outs, scratch, args, scalars=1):
    specs = [pl.BlockSpec(memory_space=pltpu.SMEM)] * scalars
    specs += [pl.BlockSpec(memory_space=pltpu.VMEM)] * (len(args) - scalars)
    return pl.pallas_call(
        kernel,
        in_specs=specs,
        out_specs=jax.tree.map(lambda _: pl.BlockSpec(memory_space=pltpu.VMEM), outs),
        out_shape=outs,
        scratch_shapes=[pltpu.VMEM(s, t) for s, t in scratch],
        compiler_params=pltpu.CompilerParams(vmem_limit_bytes=VMEM),
        interpret=INTERPRET,
    )(*args)


INTERPRET = False


def shape(dims, kind):
    return jax.ShapeDtypeStruct(dims, kind)


def row_tables():
    table = np.zeros((4, TILES, 16, 3, 64), np.float32)
    for e in range(4):
        for t in range(TILES):
            u = 2 * (t % 11) + t // 11
            for i in range(4):
                for k in range(3):
                    table[e, t, i * 4 + k, k, 2 * u + i + e] = 1.0
    return table.reshape(4, TILES * 16, 192)


def column_table():
    table = np.zeros((CROP, 6, 64), np.float32)
    for m in range(6):
        for x in range(64):
            if 0 <= 4 * x + m - 1 < CROP:
                table[4 * x + m - 1, m, x] = 1.0
    return table.reshape(CROP, 384)


def decode(where, top, mid, bot, left, right, conv_mid, conv_out):
    w = jnp.transpose(conv_out, (1, 0, 3, 2))
    w = jnp.pad(w, ((0, 0), (0, 0), (0, 5), (0, 0))).reshape(72, 128)
    w = jnp.pad(w, ((0, 8), (0, 0)))
    return call(
        decode_kernel,
        (
            shape((COLS, TW, 384), BF),
            shape((1024, 128), F32),
            shape((88, WIDE, 128), BF),
        ),
        [((90 * WIDE, 128), BF), ((88 * WIDE, 128), BF), ((88, 80, 128), F32), ((384, 384), BF)],
        (where, top, mid, bot, left, right, conv_mid, w),
    )


def percept(where, dec, tgt, vgg_first, vgg_second, weights):
    none = jnp.zeros((3, 3, 3, 64), BF)
    w_first = jnp.concatenate(
        [jnp.concatenate([vgg_first, none], -1), jnp.concatenate([none, vgg_first], -1)], 2
    )
    w_first = jnp.pad(w_first, ((0, 0), (0, 1), (0, 2), (0, 0))).reshape(96, 128)
    both = jnp.eye(2, dtype=BF)[None, :, None, None, :, None]
    w_second = (jnp.transpose(vgg_second, (0, 2, 1, 3))[:, None, :, :, None, :] * both).reshape(
        384, 384
    )
    w_back = jnp.transpose(jnp.flip(vgg_second, (0, 1)), (0, 3, 1, 2))
    w_back = jnp.pad(w_back, ((0, 0), (0, 64), (0, 0), (0, 64))).reshape(384, 384)
    w_last = jnp.transpose(jnp.flip(vgg_first, (0, 1)), (1, 0, 2, 3))
    w_last = jnp.pad(w_last, ((0, 0), (0, 0), (0, 5), (0, 64))).reshape(72, 128)
    w_last = jnp.pad(w_last, ((0, 8), (0, 0)))
    scaled = jnp.pad(2.0 * LOSS_SCALE * weights, (0, 64)).reshape(1, 128)
    return call(
        percept_kernel,
        shape((68 * 8, 128), F32),
        [
            ((76 * 32, 128), BF),
            ((74 * WIDE, 128), F32),
            ((74 * WIDE, 128), BF),
            ((72 * WIDE, 128), BF),
            ((70 * WIDE, 128), BF),
            ((70, 80, 128), F32),
        ],
        (where, dec, tgt, w_first, w_second, w_back, w_last, scaled),
    )


def critics(where, anchors, owners, strip, first, second, score):
    w = jnp.pad(first, ((0, 0), (0, 0), (0, 1), (0, 0)))
    w = jnp.transpose(w, (1, 0, 2, 3)).reshape(4, 16, 64)
    w = jnp.concatenate(
        [jnp.pad(w, ((0, 2), (0, 0), (0, 0))), jnp.pad(w, ((2, 0), (0, 0), (0, 0)))], -1
    ).reshape(96, 128)
    rows_of = row_tables()
    return call(
        critic_kernel,
        shape((COLS, 40, 256), BF),
        [
            ((IMG_W + 8, 384), F32),
            ((IMG_W + 24, 384), F32),
            ((256, 768), BF),
            ((96, LANES), BF),
            ((128, LANES), F32),
            ((256, LANES), BF),
            ((384, 12 * 128), BF),
            ((384, 384), F32),
        ],
        (
            where,
            anchors,
            owners,
            strip,
            jnp.asarray(column_table(), BF),
            jnp.asarray(rows_of, BF),
            jnp.asarray(np.swapaxes(rows_of, 1, 2), BF),
            w,
            second.reshape(4, 256, 128),
            score.astype(F32).reshape(128, 1),
        ),
        scalars=3,
    )


def finish(where, parts, lpips, slope, feats, conv_mid, conv_out):
    w = jnp.transpose(jnp.flip(conv_out, (0, 1)), (0, 1, 3, 2))
    w = jnp.pad(w, ((0, 0), (0, 1), (0, 5), (0, 0))).reshape(96, 128)
    return call(
        finish_kernel,
        shape((TH, TW, 128), BF),
        [
            ((128, 256), F32),
            ((256, 128), F32),
            ((72 * 8, 128), F32),
            ((68 * 32, 128), BF),
            ((66 * WIDE, 128), BF),
            ((384, 384), BF),
        ],
        (where, parts, lpips, slope, feats, conv_mid, w),
    )


def neighbours(block, axis, dim, width):
    count = lax.axis_size(axis)
    forward = [(i, i + 1) for i in range(count - 1)]
    backward = [(target, source) for source, target in forward]
    size = block.shape[dim]
    low = lax.ppermute(lax.slice_in_dim(block, size - width, size, axis=dim), axis, forward)
    high = lax.ppermute(lax.slice_in_dim(block, 0, width, axis=dim), axis, backward)
    return low, high


def local(
    features, conv_mid, conv_out, target, vgg_first, vgg_second, perceptual_weights,
    crop_anchors, crop_owner, critic_first, critic_second, critic_score,
):
    where = jnp.stack([lax.axis_index("row"), lax.axis_index("col")]).astype(jnp.int32)
    feats = features[0]
    planar = jnp.transpose(target[0], (0, 2, 1))
    top, bot = neighbours(feats, "row", 0, FEAT_HALO)
    t_top, t_bot = neighbours(planar, "row", 0, TGT_HALO)

    def edge(first, last):
        return jnp.concatenate([a[:, first:last] for a in (top, feats, bot)], 0)

    count = lax.axis_size("col")
    forward = [(i, i + 1) for i in range(count - 1)]
    backward = [(t, s) for s, t in forward]
    left = lax.ppermute(edge(TW - COL_HALO, TW), "col", forward)
    right = lax.ppermute(edge(0, COL_HALO), "col", backward)
    tall = jnp.concatenate([t_top, planar, t_bot], 0)
    t_left, t_right = neighbours(tall, "col", 2, TGT_HALO)
    tgt = jnp.concatenate([t_left, tall, t_right], 2).astype(F32)
    tgt = jnp.pad(tgt, ((0, 0), (3, 2), (2, 128 - 2 - TW - 2 * TGT_HALO))).reshape(76 * 8, 128)
    pay, dec, slope = decode(where, top, feats, bot, left, right, conv_mid, conv_out)
    strip = lax.all_to_all(pay, "col", split_axis=0, concat_axis=0, tiled=True)
    lpips = percept(where, dec, tgt, vgg_first, vgg_second, perceptual_weights)
    grads = critics(
        where,
        crop_anchors.reshape(CROPS, 2),
        crop_owner.reshape(CROPS),
        strip.reshape(IMG_W, 384),
        critic_first[0],
        critic_second[0],
        critic_score[0],
    )
    parts = lax.all_to_all(grads, "col", split_axis=0, concat_axis=0, tiled=True)
    return finish(where, parts, lpips, slope, feats, conv_mid, conv_out)[None]


def solution(mesh):
    placed = (
        P(None, "row", "col", None),
        P(),
        P(),
        P(None, "row", "col", None),
        P(),
        P(),
        P(),
        P(),
        P(),
        P("col", None, None, None, None),
        P("col", None, None, None, None),
        P("col", None),
    )
    return jax.shard_map(
        local, mesh=mesh, in_specs=placed, out_specs=P(None, "row", "col", None), check_vma=False
    )
```

```python
import jax
import jax.numpy as jnp
import numpy as np
from jax import lax
from jax.experimental import pallas as pl
from jax.experimental.pallas import tpu as pltpu
from jax.sharding import PartitionSpec as P

BF = jnp.bfloat16
F32 = jnp.float32

LOSS_SCALE = 32.0
EPSILON = 1e-06
CROP = 256
TH, TW = 64, 32
IMG_H, IMG_W = 512, 1024
ROWS, COLS = 8, 32
CROPS = 64
DEC_HALO = 11
FEAT_HALO = 13
COL_HALO = 8
WIDE = TW + 2 * COL_HALO
TGT_HALO = 6
GRAD_PAD = 10
SHARE = 34
VMEM = 56 * 1024 * 1024


def sigmoid(v):
    return 0.5 * jnp.tanh(0.5 * v) + 0.5


def silu_parts(v):
    sig = sigmoid(v)
    act = v * sig
    return act, sig + act * (1.0 - sig)


def mm(a, b, ca=1, cb=0):
    return lax.dot_general(a, b, (((ca,), (cb,)), ((), ())), preferred_element_type=F32)


def iota(shape, dim):
    return lax.broadcasted_iota(jnp.int32, shape, dim)


def aligned(start, unit):
    return pl.multiple_of(start, unit) if not isinstance(start, int) else start


def conv_rows(src, row0, rows, weight, transposed=False, shift=0):
    n = rows * WIDE
    lhs = jnp.concatenate(
        [src[pl.ds(aligned((row0 + dy) * WIDE, 16), n), :] for dy in range(3)], axis=1
    )
    z = mm(lhs, weight, 1, 1 if transposed else 0)
    parts = []
    for dx in range(3):
        amount = (1 - dx - shift) % n
        part = z[:, dx * 128 : (dx + 1) * 128]
        parts.append(pltpu.roll(part, amount, 0) if amount else part)
    return parts[0] + parts[1] + parts[2]


def column_mask(col_first):
    x = col_first + iota((1, WIDE, 128), 1)
    return ((x >= 0) & (x < IMG_W)).astype(F32)


def keep_inside(v, row_first, rows, col_ok):
    y = row_first + iota((rows, 1, 128), 0)
    row_ok = ((y >= 0) & (y < IMG_H)).astype(F32)
    return (v.reshape(rows, WIDE, 128) * (col_ok * row_ok)).reshape(rows * WIDE, 128)


def planar_inside(row_first, col_first, low, high, rows, limit):
    lane = iota((rows * 8, 128), 1)
    row = iota((rows * 8, 128), 0) >> 3
    x = col_first + lane
    y = row_first + row
    ok = (x >= 0) & (x < IMG_W) & (lane >= low) & (lane < high) & (y >= 0) & (y < IMG_H)
    return ok & (row < limit)


def taller(v):
    return jnp.concatenate([v, jnp.zeros((128 - v.shape[0], 128), F32)], axis=0)


def colour_weights(w, small):
    k = iota((32, 384), 0)
    n = iota((32, 384), 1)
    copies = (((n >> 7) * 8 + (n & 7)) == k).astype(F32).astype(BF)
    for dy in range(3):
        w[dy * 128 : (dy + 1) * 128, :] = mm(small(dy).astype(BF), copies, 0, 0).astype(BF)


def to_colours(src, first, w):
    group = iota((WIDE, 128), 1) >> 3
    tile = jnp.zeros((WIDE, 128), F32)
    for half in range(2):
        v = conv_rows(src, first + half * 8, 8, w[...])
        for k in range(8):
            tile = jnp.where(group == half * 8 + k, v[k * WIDE : (k + 1) * WIDE], tile)
    return taller(tile).T


def patch_tile(v):
    after, before = pltpu.roll(v, 1, 1), pltpu.roll(v, 127, 1)
    none = jnp.zeros((8, 128), F32)
    parts = []
    for k in range(4):
        at = slice(k * 8, (k + 1) * 8)
        parts += [after[at], v[at], before[at], none]
    return jnp.concatenate(parts, axis=0).T[0:WIDE].astype(BF)


def patch_weights(w, small):
    w[...] = jnp.zeros(w.shape, BF)
    for k in range(4):
        for dy in range(3):
            w[(k + dy) * 32 : (k + dy + 1) * 32, k * 128 : (k + 1) * 128] = small(dy).astype(BF)


def from_colours(px, tile, count, w):
    at = [pl.ds(aligned((tile + k) * WIDE, 16), count * WIDE) for k in range(2)]
    return mm(jnp.concatenate([px[at[0], :], px[at[1], :]], axis=1), w[...])


def decode_kernel(
    where, top, mid, bot, left, right, w_mid, w_out, pay, dec, slope_out, s1, s2, w, w3
):
    r, c = where[0], where[1]
    for dy in range(3):
        for dx in range(3):
            w[dy * 128 : (dy + 1) * 128, dx * 128 : (dx + 1) * 128] = w_mid[dy, dx]
    colour_weights(w3, lambda dy: w_out[dy])

    def fill(first, rows, centre):
        n = rows * WIDE
        parts = [left[pl.ds(first, rows)], centre, right[pl.ds(first, rows)]]
        v = jnp.concatenate([p.astype(F32) for p in parts], axis=1).reshape(n, 128)
        s1[pl.ds(aligned(first * WIDE, 16), n), :] = (v * sigmoid(v)).astype(BF)

    fill(0, FEAT_HALO, top[0:FEAT_HALO])
    fill(FEAT_HALO + TH, FEAT_HALO, bot[0:FEAT_HALO])

    def fill_mid(i, carry):
        fill(FEAT_HALO + i * 8, 8, mid[pl.ds(i * 8, 8)])
        return carry

    lax.fori_loop(0, TH // 8, fill_mid, 0, unroll=2)
    col_ok = column_mask(c * TW - COL_HALO)

    def middle(i, carry):
        v = conv_rows(s1, i * 8, 8, w[...])
        act, slope = silu_parts(v)
        act = keep_inside(act, r * TH - 12 + i * 8, 8, col_ok)
        s2[pl.ds(aligned(i * 8 * WIDE, 16), 8 * WIDE), :] = act.astype(BF)
        slope_out[pl.ds(i * 8, 8)] = (
            pltpu.roll(slope, 8 * WIDE - 6, 0).reshape(8, WIDE, 128).astype(BF)
        )
        return carry

    lax.fori_loop(0, 11, middle, 0, unroll=True)
    s2[88 * WIDE :, :] = jnp.zeros((10 * WIDE, 128), BF)
    dec[768:, :] = jnp.zeros((256, 128), F32)

    def colours(i, carry):
        v = to_colours(s2, i * 16, w3)
        ok = planar_inside(
            r * TH - DEC_HALO + i * 16, c * TW - COL_HALO, 2, WIDE - 2, 16, 86 - i * 16
        )
        dec[pl.ds(aligned(i * 128, 128), 128), :] = jnp.where(ok, v, 0.0).astype(BF).astype(F32)
        return carry

    lax.fori_loop(0, 6, colours, 0, unroll=True)
    planes = [
        dec[pl.ds(k, 128, stride=8), :].T[COL_HALO : COL_HALO + TW, :] for k in range(3)
    ]
    upper = iota((16, 128), 1) >= 64
    for half in range(2):
        low, high = [], []
        for x in range(2):
            for p in planes:
                p = p[x * 16 : (x + 1) * 16]
                start = half * SHARE
                low.append(pltpu.roll(p, 128 - start, 1) if start else p)
                high.append(pltpu.roll(p, 64 - start, 1))
        packed = [jnp.where(upper, high[k + 1], low[k]) for k in (0, 2, 4)]
        packed = jnp.concatenate(packed, axis=1).astype(BF)
        for k in range(COLS // 2):
            pay[2 * k + half] = packed


def percept_kernel(
    where, dec, tall, left, right, v_first, v_second, weights, feat, slope_one,
    planes, px, one, w1, w2,
):
    r, c = where[0], where[1]
    col_first = c * TW - COL_HALO
    col_ok = column_mask(col_first)

    def first_small(dy):
        v = v_first[dy]
        return v + pltpu.roll(pltpu.roll(v, 3, 0), 64, 1)

    patch_weights(w1, first_small)
    for dy in range(3):
        for dx in range(3):
            v = v_second[dy, dx].astype(F32)
            v = jnp.concatenate([v, jnp.zeros((64, 64), F32)], axis=1)
            u = pltpu.roll(v, 64, 1)
            w2[dy * 128 : (dy + 1) * 128, dx * 128 : (dx + 1) * 128] = jnp.concatenate(
                [v, u], axis=0
            ).astype(BF)

    planes[...] = jnp.zeros(planes.shape, F32)
    for k in range(3):
        v = jnp.concatenate(
            [a.astype(F32) for a in (left[90 + k], tall[k], right[90 + k])], axis=0
        )
        planes[pl.ds(3 + k, 80, stride=8), :] = taller(v).T[0:80]

    def gather(i, carry):
        v = dec[pl.ds(aligned(i * 32 + 40, 8), 32), :] + planes[pl.ds(aligned(i * 32, 32), 32), :]
        px[pl.ds(aligned(i * WIDE, 16), WIDE), :] = patch_tile(v)
        return carry

    lax.fori_loop(0, 19, gather, 0, unroll=True)
    px[19 * WIDE :, :] = jnp.zeros((WIDE, 128), BF)

    def first(tile, count):
        v = from_colours(px, tile, count, w1)
        for j in range(count):
            for k in range(4):
                p = (tile + j) * 4 + k
                x = v[j * WIDE : (j + 1) * WIDE, k * 128 : (k + 1) * 128]
                act, slope = silu_parts(x)
                act = keep_inside(act, r * TH - 5 + p, 1, col_ok)
                slope_one[pl.ds(aligned(p * WIDE, 16), WIDE), :] = slope.astype(BF)
                one[pl.ds(aligned(p * WIDE, 16), WIDE), :] = act.astype(BF)

    def first_group(i, carry):
        first(i * 4, 4)
        return carry

    lax.fori_loop(0, 4, first_group, 0, unroll=True)
    first(16, 3)
    ones = ((iota((128, 128), 0) >> 6) == (iota((128, 128), 1) >> 6)).astype(F32).astype(BF)

    def half_sum(v):
        high = v.astype(BF)
        low = (v - high.astype(F32)).astype(BF)
        return mm(high, ones) + mm(low, ones)

    def second(i, carry):
        v = conv_rows(one, i * 8, 8, w2[...])
        f, slope = silu_parts(v)
        scale = lax.rsqrt(half_sum(f * f) + EPSILON)
        unit = f * scale
        weighted = weights[...] * (unit - pltpu.roll(unit, 64, 1))
        g = scale * (weighted - unit * half_sum(weighted * unit)) * slope
        g = keep_inside(g, r * TH - 4 + i * 8, 8, col_ok)
        feat[pl.ds(aligned(i * 8 * WIDE, 16), 8 * WIDE), :] = g.astype(BF)
        return carry

    lax.fori_loop(0, 9, second, 0, unroll=3)


def percept_back_kernel(where, feat, slope_one, v_first, v_second, out, bv, w3, w4):
    r, c = where[0], where[1]
    col_ok = column_mask(c * TW - COL_HALO)

    def last_small(dy):
        parts = [v_first[2 - dy, (2 - dx) * 8 : (3 - dx) * 8, :] for dx in range(3)]
        return jnp.concatenate(parts + [jnp.zeros((8, 128), F32)], axis=0)

    colour_weights(w4, last_small)
    for dy in range(3):
        for dx in range(3):
            v = v_second[dy, dx].astype(F32)
            v = jnp.concatenate([v, jnp.zeros((64, 64), F32)], axis=1)
            w3[(2 - dx) * 128 : (3 - dx) * 128, (2 - dy) * 128 : (3 - dy) * 128] = jnp.concatenate(
                [v, jnp.zeros((64, 128), F32)], axis=0
            ).astype(BF)

    def back(i, carry):
        v = conv_rows(feat, i * 10, 10, w3[...], transposed=True)
        x = slope_one[pl.ds(aligned((i * 10 + 2) * WIDE, 16), 10 * WIDE), :]
        v = keep_inside(v * x.astype(F32), r * TH - 3 + i * 10, 10, col_ok)
        bv[pl.ds(aligned(i * 10 * WIDE, 16), 10 * WIDE), :] = v.astype(BF)
        return carry

    lax.fori_loop(0, 7, back, 0, unroll=True)
    bv[70 * WIDE :, :] = jnp.zeros((12 * WIDE, 128), BF)

    def colours(i, carry):
        v = to_colours(bv, i * 16, w4)
        out[pl.ds(aligned(i * 128, 128), 128), :] = pltpu.roll(v, 122, 1)
        return carry

    lax.fori_loop(0, 5, colours, 0, unroll=True)


STEPS = 6
HALF = STEPS + 1
TILES = 2 * HALF
LANES = TILES * 128
EVEN = HALF * 128


def critic_kernel(
    where, anchors, owners, strip, pick, rows_of, rows_back, mine, other, _, out,
    strip32, grads, w_pre, w_one, w_two, w_back, score, x_all, pre, act, two, cols,
):
    r, me = where[0], where[1]
    first_row = r * TH - 2 + SHARE * (me & 1)
    lane = iota((1, 128), 1)
    upper = lane >= 64
    first_x = (lane & 63) == 0
    last_x = (lane & 63) == 63

    def unpack(k, carry):
        v = strip[k].astype(F32)
        b, d = pltpu.roll(v[:, 128:256], 64, 1), pltpu.roll(v[:, 256:384], 64, 1)
        at = aligned(k * TW, 32)
        strip32[pl.ds(at, 16), :] = v[:, 0:256]
        strip32[pl.ds(at + 16, 16), :] = jnp.concatenate([jnp.where(upper, d, b), d], axis=1)
        return carry

    lax.fori_loop(0, COLS, unpack, 0, unroll=8)
    strip32[IMG_W:, :] = jnp.zeros((8, 256), F32)
    grads[...] = jnp.zeros(grads.shape, F32)
    w_back[...] = jnp.zeros(w_back.shape, BF)
    for g, source in enumerate((mine, other)):
        w_one[g] = source[1024:1120, :]
        w_pre[g] = taller(source[1024:1120, :].astype(F32)).T.astype(BF)
        score[g] = taller(source[1120:1136, :].astype(F32)).T
        for i in range(4):
            w_two[g, i] = jnp.concatenate(
                [
                    source[i * 256 + k * 128 : i * 256 + (k + 1) * 128, :].astype(F32).T
                    for k in range(2)
                ],
                axis=1,
            ).astype(BF)
        for par in range(2):
            for p in range(2):
                for t in range(2):
                    i = par + 2 * t
                    for kind, j in ((0, 1 + p), (1 + p, 3 - 3 * p)):
                        w_back[
                            g,
                            (par * 2 + p) * 64 : (par * 2 + p + 1) * 64,
                            (t * 3 + kind) * 128 : (t * 3 + kind + 1) * 128,
                        ] = source[i * 256 + j * 64 : i * 256 + (j + 1) * 64, :]
    two[:, 0:128] = jnp.zeros((384, 128), BF)
    two[:, (STEPS + 1) * 128 :] = jnp.zeros((384, 128), BF)
    cols[192:, :] = jnp.zeros((64, 384), F32)
    wide = iota((1, 256), 1)

    def score_crop(top, left, g):
        y0 = first_row - top
        v0 = lax.shift_right_arithmetic(y0 - 3, 2)
        e = 4 * v0 - y0 + 6
        crop_row = y0 - 9 + (wide & 63)
        in_crop = (crop_row >= 0) & (crop_row < CROP) & (wide < 192)
        window = strip32[pl.ds(aligned((left >> 3) * 8, 8), CROP + 8), :]
        window = pltpu.roll(window, lax.rem((CROP + 8) - (left & 7), CROP + 8), 0)[0:CROP]
        window = jnp.where(in_crop, window, 0.0).astype(BF)
        cols_of = mm(window, pick[...], 0, 0)
        none = jnp.zeros((8, 384), F32)
        halves = [
            jnp.concatenate(
                [cols_of[k * 64 + 24 * h : k * 64 + 24 * h + 40, :] for k in range(3)] + [none],
                axis=0,
            )
            for h in range(2)
        ]
        mixed = []
        for m in range(6):
            tile = slice((m // 2) * 128, (m // 2 + 1) * 128)
            low, high = halves[0][:, tile], halves[1][:, tile]
            if m % 2 == 0:
                high = pltpu.roll(high, 64, 1)
            else:
                low = pltpu.roll(low, 64, 1)
            mixed.append(jnp.where(upper, high, low))
        patches = mm(rows_of[e], jnp.concatenate(mixed, axis=1).astype(BF)).astype(BF)
        for t in range(TILES):
            for m in range(6):
                x_all[m * 16 : (m + 1) * 16, t * 128 : (t + 1) * 128] = patches[
                    t * 16 : (t + 1) * 16, m * 128 : (m + 1) * 128
                ]
        weight = w_pre[g][:, 0:96]
        for t0 in range(0, TILES, 2):
            at = slice(t0 * 128, (t0 + 2) * 128)
            value = mm(weight, x_all[:, at])
            for t in range(t0, t0 + 2):
                at = slice(t * 128, (t + 1) * 128)
                n = 2 * (t % HALF) + t // HALF + jnp.where(upper, 2 * STEPS, 0)
                u = 2 * v0 - 1 + n
                ok = ((u >= 0) & (u < CROP // 2)).astype(F32)
                a, slope = silu_parts(value[:, (t - t0) * 128 : (t - t0 + 1) * 128])
                a = a * ok
                pre[:, at] = slope * ok
                even, odd = a[:64], a[64:]
                act[0:64, at] = jnp.where(first_x, 0.0, pltpu.roll(odd, 1, 1)).astype(BF)
                act[64:128, at] = even.astype(BF)
                act[128:192, at] = odd.astype(BF)
                act[192:256, at] = jnp.where(last_x, 0.0, pltpu.roll(even, 127, 1)).astype(BF)
        column = score[g][:, 0:1]
        for t0 in range(0, STEPS, 2):
            value = None
            for i in range(4):
                start = (i % 2) * EVEN + (i // 2 + t0) * 128
                part = mm(w_two[g, i], act[:, start : start + 256])
                value = part if value is None else value + part
            for t in range(t0, t0 + 2):
                f, slope = silu_parts(value[:, (t - t0) * 128 : (t - t0 + 1) * 128])
                logit = jnp.sum(f * column, axis=0, keepdims=True)
                v = v0 + t + jnp.where(upper, STEPS, 0)
                ok = (v >= 0) & (v < CROP // 4)
                grad = jnp.where(ok, -LOSS_SCALE * sigmoid(-logit), 0.0)
                b = grad * (column * slope)
                at = slice((t + 1) * 128, (t + 2) * 128)
                two[0:128, at] = b.astype(BF)
                two[128:256, at] = jnp.where(first_x, 0.0, pltpu.roll(b, 1, 1)).astype(BF)
                two[256:384, at] = jnp.where(last_x, 0.0, pltpu.roll(b, 127, 1)).astype(BF)
        for s0 in range(0, HALF, 2):
            n = min(2, HALF - s0) * 128
            at = s0 * 128
            both = jnp.concatenate([two[:, 128 + at : 128 + at + n], two[:, at : at + n]], axis=0)
            up = mm(w_back[g], both)
            for par in range(2):
                here = slice(par * EVEN + at, par * EVEN + at + n)
                one = (up[par * 128 : (par + 1) * 128] * pre[:, here]).astype(BF)
                x_all[:, here] = mm(w_one[g], one).astype(BF)
        spread = jnp.concatenate(
            [
                jnp.concatenate(
                    [
                        x_all[m * 16 : (m + 1) * 16, t * 128 : (t + 1) * 128]
                        for t in range(TILES)
                    ],
                    axis=0,
                )
                for m in range(6)
            ],
            axis=1,
        )
        back = mm(rows_back[e], spread)
        parts = []
        for h in range(2):
            tiles = []
            for k in range(3):
                low = back[:, 2 * k * 128 : (2 * k + 1) * 128]
                high = back[:, (2 * k + 1) * 128 : (2 * k + 2) * 128]
                if h == 0:
                    high = pltpu.roll(high, 64, 1)
                else:
                    low = pltpu.roll(low, 64, 1)
                tiles.append(jnp.where(upper, high, low))
            parts.append(jnp.concatenate(tiles, axis=1))
        for k in range(3):
            low, high = (part[k * 40 : (k + 1) * 40, :] for part in parts)
            cols[k * 64 : (k + 1) * 64, :] = jnp.concatenate(
                [low[0:24], low[24:40] + high[0:16], high[16:40]], axis=0
            )
        placed = mm(pick[...], cols[...].astype(BF), 1, 1)
        y = wide & 63
        keep = in_crop & (y >= 9) & (y < 9 + SHARE)
        placed = jnp.concatenate([jnp.where(keep, placed, 0.0), jnp.zeros((8, 256), F32)], axis=0)
        start = left + GRAD_PAD
        here = pl.ds(aligned((start >> 3) * 8, 8), CROP + 8)
        grads[here, :] = grads[here, :] + pltpu.roll(placed, start & 7, 0)

    def one_crop(q, carry):
        top, left, owner = anchors[q, 0], anchors[q, 1], owners[q]
        y0 = first_row - top

        @pl.when(((owner >> 1) == (me >> 1)) & (y0 < CROP) & (y0 + SHARE > 0))
        def _():
            score_crop(top, left, (owner ^ me) & 1)

        return carry

    lax.fori_loop(0, CROPS, one_crop, 0)

    def pack(k, carry):
        block = grads[pl.ds(aligned(k * TW + 8, 8), 40), :]
        a, b = block[:, 0:128], block[:, 128:256]
        out[k] = jnp.where(
            lane < 40,
            pltpu.roll(a, 128 - 9, 1),
            jnp.where(lane < 80, pltpu.roll(a, 128 - 33, 1), pltpu.roll(b, 71, 1)),
        ).astype(BF)
        return carry

    lax.fori_loop(0, COLS, pack, 0, unroll=4)


def finish_kernel(
    where, parts, lpips, slope, feats, w_mid, w_out, out, turned, planes, px, bm, w, w1
):
    r, c = where[0], where[1]
    for dy in range(3):
        for dx in range(3):
            w[dx * 128 : (dx + 1) * 128, dy * 128 : (dy + 1) * 128] = w_mid[2 - dy, 2 - dx]

    def small(dy):
        flipped = [w_out[2 - dy, (2 - dx) * 8 : (3 - dx) * 8, :] for dx in range(3)]
        return jnp.concatenate(flipped + [jnp.zeros((8, 128), F32)], axis=0)

    patch_weights(w1, small)
    col_ok = column_mask(c * TW - 2)
    planes[...] = jnp.zeros(planes.shape, F32)
    for half in range(2):
        total = parts[half].astype(F32)
        for k in range(1, COLS // 2):
            total = total + parts[2 * k + half].astype(F32)
        turned[...] = taller(total).T
        for k in range(3):
            planes[pl.ds(half * SHARE * 8 + k, 40, stride=8), :] = turned[k * 40 : (k + 1) * 40, :]

    def gather(i, carry):
        at = pl.ds(aligned(i * 32, 32), 32)
        ok = planar_inside(r * TH - 2 + i * 4, c * TW - 2, 0, 36, 4, 4)
        px[pl.ds(aligned(i * WIDE, 16), WIDE), :] = patch_tile(
            jnp.where(ok, lpips[at, :] + planes[at, :], 0.0)
        )
        return carry

    lax.fori_loop(0, 17, gather, 0, unroll=True)
    px[17 * WIDE :, :] = jnp.zeros((WIDE, 128), BF)

    def middle(tile, count):
        v = from_colours(px, tile, count, w1)
        for j in range(count):
            for k in range(4):
                n = (tile + j) * 4 + k
                x = v[j * WIDE : (j + 1) * WIDE, k * 128 : (k + 1) * 128]
                x = keep_inside(x * slope[n + 11].astype(F32), r * TH - 1 + n, 1, col_ok)
                bm[pl.ds(aligned(n * WIDE, 16), WIDE), :] = x.astype(BF)

    def middle_group(i, carry):
        middle(i * 4, 4)
        return carry

    lax.fori_loop(0, 4, middle_group, 0, unroll=True)
    middle(16, 1)

    def last(i, carry):
        v = conv_rows(bm, i * 8, 8, w[...], transposed=True, shift=2)
        v = v.reshape(8, WIDE, 128)[:, 0:TW, :]
        x = feats[pl.ds(i * 8, 8)].astype(F32)
        out[pl.ds(i * 8, 8)] = (v * silu_parts(x)[1]).astype(BF)
        return carry

    lax.fori_loop(0, TH // 8, last, 0, unroll=4)


def call(kernel, outs, scratch, args, scalars=1, unused=0):
    specs = [pl.BlockSpec(memory_space=pltpu.SMEM)] * scalars
    specs += [pl.BlockSpec(memory_space=pltpu.VMEM)] * (len(args) - scalars - unused)
    specs += [pl.BlockSpec(memory_space=pl.ANY)] * unused
    return pl.pallas_call(
        kernel,
        in_specs=specs,
        out_specs=jax.tree.map(lambda _: pl.BlockSpec(memory_space=pltpu.VMEM), outs),
        out_shape=outs,
        scratch_shapes=[pltpu.VMEM(s, t) for s, t in scratch],
        compiler_params=pltpu.CompilerParams(vmem_limit_bytes=VMEM),
        interpret=INTERPRET,
    )(*args)


INTERPRET = False


def shape(dims, kind):
    return jax.ShapeDtypeStruct(dims, kind)


def row_tables():
    table = np.zeros((4, TILES, 16, 128), np.float32)
    for e in range(4):
        for t in range(TILES):
            u = 2 * (t % HALF) + t // HALF
            for i in range(4):
                for k in range(3):
                    table[e, t, i * 4 + k, k * 40 + 2 * u + i + e] = 1.0
    return table.reshape(4, TILES * 16, 128)


def column_table():
    table = np.zeros((CROP, 6, 64), np.float32)
    for m in range(6):
        for x in range(64):
            if 0 <= 4 * x + m - 1 < CROP:
                table[4 * x + m - 1, m, x] = 1.0
    return table.reshape(CROP, 384)


def colour_first(w):
    w = jnp.pad(w.astype(F32), ((0, 0), (0, 1), (0, 5), (0, 128 - w.shape[-1])))
    return w.reshape(3, 32, 128)


def decode(where, top, mid, bot, left, right, conv_mid, small):
    return call(
        decode_kernel,
        (
            shape((COLS, TW // 2, 384), BF),
            shape((1024, 128), F32),
            shape((88, WIDE, 128), BF),
        ),
        [((90 * WIDE, 128), BF), ((98 * WIDE, 128), BF), ((384, 384), BF), ((384, 384), BF)],
        (where, top, mid, bot, left, right, conv_mid, small),
    )


def percept(where, dec, tall, left, right, small, vgg_second, weights):
    scaled = jnp.pad(2.0 * LOSS_SCALE * weights, (0, 64)).reshape(1, 128)
    return call(
        percept_kernel,
        (shape((72 * WIDE, 128), BF), shape((76 * WIDE, 128), BF)),
        [
            ((80 * 8, 128), F32),
            ((20 * WIDE, 128), BF),
            ((76 * WIDE, 128), BF),
            ((256, 512), BF),
            ((384, 384), BF),
        ],
        (where, dec, tall, left, right, small, vgg_second, scaled),
    )


def percept_back(where, feat, slope_one, small, vgg_second):
    return call(
        percept_back_kernel,
        shape((80 * 8, 128), F32),
        [((82 * WIDE, 128), BF), ((384, 384), BF), ((384, 384), BF)],
        (where, feat, slope_one, small, vgg_second),
    )


def critic_weights(first, second, score):
    w = jnp.pad(first, ((0, 0), (0, 0), (0, 1), (0, 0)))
    w = jnp.transpose(w, (1, 0, 2, 3)).reshape(4, 16, 64)
    w = jnp.concatenate(
        [jnp.pad(w, ((0, 2), (0, 0), (0, 0))), jnp.pad(w, ((2, 0), (0, 0), (0, 0)))], -1
    ).reshape(96, 128)
    score = jnp.pad(score[None], ((0, 15), (0, 0)))
    return jnp.concatenate([second.reshape(1024, 128), w, score], 0)


def critics(where, anchors, owners, strip, mine, other, after):
    rows_of = row_tables()
    return call(
        critic_kernel,
        shape((COLS, 40, 128), BF),
        [
            ((IMG_W + 8, 256), F32),
            ((IMG_W + 24, 256), F32),
            ((2, 128, 128), BF),
            ((2, 96, 128), BF),
            ((2, 4, 128, 256), BF),
            ((2, 256, 768), BF),
            ((2, 128, 128), F32),
            ((96, LANES), BF),
            ((128, LANES), F32),
            ((256, LANES), BF),
            ((384, (STEPS + 2) * 128), BF),
            ((256, 384), F32),
        ],
        (
            where,
            anchors,
            owners,
            strip,
            jnp.asarray(column_table(), BF),
            jnp.asarray(rows_of, BF),
            jnp.asarray(np.swapaxes(rows_of, 1, 2), BF),
            mine,
            other,
            after,
        ),
        scalars=3,
        unused=1,
    )


def finish(where, parts, lpips, slope, feats, conv_mid, small):
    return call(
        finish_kernel,
        shape((TH, TW, 128), BF),
        [
            ((128, 128), F32),
            ((80 * 8, 128), F32),
            ((18 * WIDE, 128), BF),
            ((68 * WIDE, 128), BF),
            ((384, 384), BF),
            ((256, 512), BF),
        ],
        (where, parts, lpips, slope, feats, conv_mid, small),
    )


def exchange(low, high, axis):
    count = lax.axis_size(axis)
    forward = [(i, i + 1) for i in range(count - 1)]
    backward = [(target, source) for source, target in forward]
    return lax.ppermute(low, axis, forward), lax.ppermute(high, axis, backward)


def local(
    features, conv_mid, conv_out, target, vgg_first, vgg_second, perceptual_weights,
    crop_anchors, crop_owner, critic_first, critic_second, critic_score,
):
    where = jnp.stack([lax.axis_index("row"), lax.axis_index("col")]).astype(jnp.int32)
    feats = features[0]
    planar = jnp.transpose(target[0], (2, 1, 0))

    def row_part(rows, colours):
        colours = jnp.transpose(colours, (1, 0, 2)).reshape(TW, 3 * TGT_HALO)
        colours = jnp.pad(colours, ((0, 0), (0, 128 - 3 * TGT_HALO)))
        return jnp.concatenate([rows, colours[None]], 0)

    top, bot = exchange(
        row_part(feats[TH - FEAT_HALO :], planar[:, :, TH - TGT_HALO :]),
        row_part(feats[:FEAT_HALO], planar[:, :, :TGT_HALO]),
        "row",
    )

    def colours_of(part):
        part = part[FEAT_HALO, :, : 3 * TGT_HALO].reshape(TW, 3, TGT_HALO)
        return jnp.transpose(part, (1, 0, 2))

    tall = jnp.concatenate(
        [
            colours_of(top),
            planar,
            colours_of(bot),
            jnp.zeros((3, TW, 128 - TH - 2 * TGT_HALO), BF),
        ],
        2,
    )

    def edge(first, last):
        parts = (top[:FEAT_HALO], feats, bot[:FEAT_HALO], tall)
        return jnp.concatenate([a[:, first:last] for a in parts], 0)

    left, right = exchange(edge(TW - COL_HALO, TW), edge(0, COL_HALO), "col")
    out_small = colour_first(jnp.transpose(conv_out, (0, 1, 3, 2)))
    vgg_small = colour_first(vgg_first)
    pay, dec, slope = decode(where, top, feats, bot, left, right, conv_mid, out_small)
    strip = lax.all_to_all(pay, "col", split_axis=0, concat_axis=0, tiled=True)
    mine = critic_weights(critic_first[0], critic_second[0], critic_score[0])
    other = lax.ppermute(mine, "col", [(i, i ^ 1) for i in range(COLS)])
    feat, slope_one = percept(
        where, dec, tall, left, right, vgg_small, vgg_second, perceptual_weights
    )
    grads = critics(
        where,
        crop_anchors.reshape(CROPS, 2),
        crop_owner.reshape(CROPS),
        strip,
        mine,
        other,
        feat,
    )
    parts = lax.all_to_all(grads, "col", split_axis=0, concat_axis=0, tiled=True)
    lpips = percept_back(where, feat, slope_one, vgg_small, vgg_second)
    return finish(where, parts, lpips, slope, feats, conv_mid, out_small)[None]


def solution(mesh):
    placed = (
        P(None, "row", "col", None),
        P(),
        P(),
        P(None, "row", "col", None),
        P(),
        P(),
        P(),
        P(),
        P(),
        P("col", None, None, None, None),
        P("col", None, None, None, None),
        P("col", None),
    )
    return jax.shard_map(
        local, mesh=mesh, in_specs=placed, out_specs=P(None, "row", "col", None), check_vma=False
    )
```

```python
import jax
import jax.numpy as jnp
import numpy as np
from jax import lax
from jax.experimental import pallas as pl
from jax.experimental.pallas import tpu as pltpu
from jax.sharding import PartitionSpec as P

BF = jnp.bfloat16
F32 = jnp.float32

LOSS_SCALE = 32.0
EPSILON = 1e-06
CROP = 256
TH, TW = 64, 32
IMG_H, IMG_W = 512, 1024
ROWS, COLS = 8, 32
CROPS = 64
DEC_HALO = 11
FEAT_HALO = 13
COL_HALO = 8
WIDE = TW + 2 * COL_HALO
TGT_HALO = 6
GRAD_PAD = 8
SHARE = 34
VMEM = 20 * 1024 * 1024


def sigmoid(v):
    return 0.5 * jnp.tanh(0.5 * v) + 0.5


def silu_parts(v):
    sig = sigmoid(v)
    act = v * sig
    return act, sig + act * (1.0 - sig)


def mm(a, b, ca=1, cb=0):
    return lax.dot_general(a, b, (((ca,), (cb,)), ((), ())), preferred_element_type=F32)


def iota(shape, dim):
    return lax.broadcasted_iota(jnp.int32, shape, dim)


def aligned(start, unit):
    return pl.multiple_of(start, unit) if not isinstance(start, int) else start


def conv_rows(src, row0, rows, weight, transposed=False, shift=0):
    n = rows * WIDE
    lhs = jnp.concatenate(
        [src[pl.ds(aligned((row0 + dy) * WIDE, 16), n), :] for dy in range(3)], axis=1
    )
    z = mm(lhs, weight, 1, 1 if transposed else 0)
    parts = []
    for dx in range(3):
        amount = (1 - dx - shift) % n
        part = z[:, dx * 128 : (dx + 1) * 128]
        parts.append(pltpu.roll(part, amount, 0) if amount else part)
    return parts[0] + parts[1] + parts[2]


def column_mask(col_first):
    x = col_first + iota((1, WIDE, 128), 1)
    return ((x >= 0) & (x < IMG_W)).astype(F32)


def keep_inside(v, row_first, rows, col_ok):
    y = row_first + iota((rows, 1, 128), 0)
    row_ok = ((y >= 0) & (y < IMG_H)).astype(F32)
    return (v.reshape(rows, WIDE, 128) * (col_ok * row_ok)).reshape(rows * WIDE, 128)


def planar_inside(row_first, col_first, low, high, rows, limit):
    lane = iota((rows * 8, 128), 1)
    row = iota((rows * 8, 128), 0) >> 3
    x = col_first + lane
    y = row_first + row
    ok = (x >= 0) & (x < IMG_W) & (lane >= low) & (lane < high) & (y >= 0) & (y < IMG_H)
    return ok & (row < limit)


def taller(v):
    return jnp.concatenate([v, jnp.zeros((128 - v.shape[0], 128), F32)], axis=0)


def colour_weights(w, small):
    k = iota((32, 384), 0)
    n = iota((32, 384), 1)
    copies = (((n >> 7) * 8 + (n & 7)) == k).astype(F32).astype(BF)
    for dy in range(3):
        w[dy * 128 : (dy + 1) * 128, :] = mm(small(dy).astype(BF), copies, 0, 0).astype(BF)


def to_colours(src, first, w):
    group = iota((WIDE, 128), 1) >> 3
    tile = jnp.zeros((WIDE, 128), F32)
    for half in range(2):
        v = conv_rows(src, first + half * 8, 8, w[...])
        for k in range(8):
            tile = jnp.where(group == half * 8 + k, v[k * WIDE : (k + 1) * WIDE], tile)
    return taller(tile).T


def patch_tile(v):
    after, before = pltpu.roll(v, 1, 1), pltpu.roll(v, 127, 1)
    none = jnp.zeros((8, 128), F32)
    parts = []
    for k in range(4):
        at = slice(k * 8, (k + 1) * 8)
        parts += [after[at], v[at], before[at], none]
    return jnp.concatenate(parts, axis=0).T[0:WIDE].astype(BF)


def patch_weights(w, small):
    w[...] = jnp.zeros(w.shape, BF)
    for k in range(4):
        for dy in range(3):
            w[(k + dy) * 32 : (k + dy + 1) * 32, k * 128 : (k + 1) * 128] = small(dy).astype(BF)


def from_colours(px, tile, count, w):
    at = [pl.ds(aligned((tile + k) * WIDE, 16), count * WIDE) for k in range(2)]
    return mm(jnp.concatenate([px[at[0], :], px[at[1], :]], axis=1), w[...])


def decode_kernel(
    meta, top, mid, bot, left, right, w_mid, w_out, pay, dec, slope_out, s1, s2, w, w3
):
    r, c = meta[0], meta[1]
    for dy in range(3):
        for dx in range(3):
            w[dy * 128 : (dy + 1) * 128, dx * 128 : (dx + 1) * 128] = w_mid[dy, dx]
    colour_weights(w3, lambda dy: w_out[dy])

    def fill(first, rows, centre):
        n = rows * WIDE
        parts = [left[pl.ds(first, rows)], centre, right[pl.ds(first, rows)]]
        v = jnp.concatenate([p.astype(F32) for p in parts], axis=1).reshape(n, 128)
        s1[pl.ds(aligned(first * WIDE, 16), n), :] = (v * sigmoid(v)).astype(BF)

    fill(0, FEAT_HALO, top[0:FEAT_HALO])
    fill(FEAT_HALO + TH, FEAT_HALO, bot[0:FEAT_HALO])

    def fill_mid(i, carry):
        fill(FEAT_HALO + i * 8, 8, mid[pl.ds(i * 8, 8)])
        return carry

    lax.fori_loop(0, TH // 8, fill_mid, 0, unroll=2)
    col_ok = column_mask(c * TW - COL_HALO)

    def middle(i, carry):
        v = conv_rows(s1, i * 8, 8, w[...])
        act, slope = silu_parts(v)
        act = keep_inside(act, r * TH - 12 + i * 8, 8, col_ok)
        s2[pl.ds(aligned(i * 8 * WIDE, 16), 8 * WIDE), :] = act.astype(BF)
        slope = pltpu.roll(slope, 8 * WIDE - 6, 0).reshape(8, WIDE, 128).astype(BF)
        first, last = max(i * 8, 11), min(i * 8 + 8, 79)
        if first < last:
            slope_out[first - 11 : last - 11] = slope[first - i * 8 : last - i * 8]
        return carry

    for i in range(11):
        middle(i, 0)
    s2[88 * WIDE :, :] = jnp.zeros((10 * WIDE, 128), BF)
    dec[768:, :] = jnp.zeros((256, 128), F32)

    def colours(i, carry):
        v = to_colours(s2, i * 16, w3)
        ok = planar_inside(
            r * TH - DEC_HALO + i * 16, c * TW - COL_HALO, 2, WIDE - 2, 16, 86 - i * 16
        )
        dec[pl.ds(aligned(i * 128, 128), 128), :] = jnp.where(ok, v, 0.0).astype(BF).astype(F32)
        return carry

    lax.fori_loop(0, 6, colours, 0, unroll=True)
    planes = [
        dec[pl.ds(k, 128, stride=8), :].T[COL_HALO : COL_HALO + TW, :] for k in range(3)
    ]
    upper = iota((16, 128), 1) >= 64
    for half in range(2):
        low, high = [], []
        for x in range(2):
            for p in planes:
                p = p[x * 16 : (x + 1) * 16]
                start = half * SHARE
                low.append(pltpu.roll(p, 128 - start, 1) if start else p)
                high.append(pltpu.roll(p, 64 - start, 1))
        packed = [jnp.where(upper, high[k + 1], low[k]) for k in (0, 2, 4)]
        packed = jnp.concatenate(packed, axis=1).astype(BF)
        for k in range(COLS // 2):
            pay[2 * k + half] = packed


def percept_kernel(
    meta, dec, tall, left, right, v_first, v_second, weights, feat, slope_one, done,
    planes, px, one, w1, w2,
):
    r, c = meta[0], meta[1]
    col_first = c * TW - COL_HALO
    col_ok = column_mask(col_first)

    def first_small(dy):
        v = v_first[dy]
        return v + pltpu.roll(pltpu.roll(v, 3, 0), 64, 1)

    patch_weights(w1, first_small)
    for dy in range(3):
        for dx in range(3):
            v = v_second[dy, dx].astype(F32)
            v = jnp.concatenate([v, jnp.zeros((64, 64), F32)], axis=1)
            u = pltpu.roll(v, 64, 1)
            w2[dy * 128 : (dy + 1) * 128, dx * 128 : (dx + 1) * 128] = jnp.concatenate(
                [v, u], axis=0
            ).astype(BF)

    planes[...] = jnp.zeros(planes.shape, F32)
    for k in range(3):
        v = jnp.concatenate(
            [a.astype(F32) for a in (left[90 + k], tall[k], right[90 + k])], axis=0
        )
        planes[pl.ds(3 + k, 80, stride=8), :] = taller(v).T[0:80]

    done[...] = jnp.zeros((8, 128), F32)

    def gather(i, carry):
        v = dec[pl.ds(aligned(i * 32 + 40, 8), 32), :] + planes[pl.ds(aligned(i * 32, 32), 32), :]
        px[pl.ds(aligned(i * WIDE, 16), WIDE), :] = patch_tile(v)
        return carry

    lax.fori_loop(0, 19, gather, 0, unroll=True)
    px[19 * WIDE :, :] = jnp.zeros((WIDE, 128), BF)

    def first(tile, count):
        v = from_colours(px, tile, count, w1)
        for j in range(count):
            for k in range(4):
                p = (tile + j) * 4 + k
                x = v[j * WIDE : (j + 1) * WIDE, k * 128 : (k + 1) * 128]
                act, slope = silu_parts(x)
                act = keep_inside(act, r * TH - 5 + p, 1, col_ok)
                slope_one[pl.ds(aligned(p * WIDE, 16), WIDE), :] = slope.astype(BF)
                one[pl.ds(aligned(p * WIDE, 16), WIDE), :] = act.astype(BF)

    def first_group(i, carry):
        first(i * 4, 4)
        return carry

    lax.fori_loop(0, 4, first_group, 0, unroll=True)
    first(16, 3)
    ones = ((iota((128, 128), 0) >> 6) == (iota((128, 128), 1) >> 6)).astype(F32).astype(BF)

    def half_sum(v):
        high = v.astype(BF)
        low = (v - high.astype(F32)).astype(BF)
        return mm(high, ones) + mm(low, ones)

    def second(i, carry):
        v = conv_rows(one, i * 8, 8, w2[...])
        f, slope = silu_parts(v)
        scale = lax.rsqrt(half_sum(f * f) + EPSILON)
        unit = f * scale
        weighted = weights[...] * (unit - pltpu.roll(unit, 64, 1))
        g = scale * (weighted - unit * half_sum(weighted * unit)) * slope
        g = keep_inside(g, r * TH - 4 + i * 8, 8, col_ok)
        feat[pl.ds(aligned(i * 8 * WIDE, 16), 8 * WIDE), :] = g.astype(BF)
        return carry

    lax.fori_loop(0, 9, second, 0, unroll=3)


def percept_back_kernel(meta, feat, slope_one, v_first, v_second, out, bv, w3, w4):
    r, c = meta[0], meta[1]
    col_ok = column_mask(c * TW - COL_HALO)

    def last_small(dy):
        parts = [v_first[2 - dy, (2 - dx) * 8 : (3 - dx) * 8, :] for dx in range(3)]
        return jnp.concatenate(parts + [jnp.zeros((8, 128), F32)], axis=0)

    colour_weights(w4, last_small)
    for dy in range(3):
        for dx in range(3):
            v = v_second[dy, dx].astype(F32)
            v = jnp.concatenate([v, jnp.zeros((64, 64), F32)], axis=1)
            w3[(2 - dx) * 128 : (3 - dx) * 128, (2 - dy) * 128 : (3 - dy) * 128] = jnp.concatenate(
                [v, jnp.zeros((64, 128), F32)], axis=0
            ).astype(BF)

    def back(i, carry):
        v = conv_rows(feat, i * 10, 10, w3[...], transposed=True)
        x = slope_one[pl.ds(aligned((i * 10 + 2) * WIDE, 16), 10 * WIDE), :]
        v = keep_inside(v * x.astype(F32), r * TH - 3 + i * 10, 10, col_ok)
        bv[pl.ds(aligned(i * 10 * WIDE, 16), 10 * WIDE), :] = v.astype(BF)
        return carry

    lax.fori_loop(0, 7, back, 0, unroll=True)
    bv[70 * WIDE :, :] = jnp.zeros((12 * WIDE, 128), BF)

    def colours(i, carry):
        v = to_colours(bv, i * 16, w4)
        out[pl.ds(aligned(i * 128, 128), 128), :] = pltpu.roll(v, 122, 1)
        return carry

    lax.fori_loop(0, 5, colours, 0, unroll=True)


STOP = object()
STEPS = 6
HALF = STEPS + 1
TILES = 2 * HALF
LANES = TILES * 128
EVEN = HALF * 128


def critic_kernel(
    meta, strip, mine, other, _, out,
    strip32, grads, w_pre, w_one, w_two, w_back, score, distance, row_gap, row_gap_back, x_all, x_all_b, pre, pre_b, act, act_b,
    two, two_b, cols, cols_b, jobs,
):
    r, me = meta[0], meta[1]
    first_row = r * TH - 2 + SHARE * (me & 1)
    lane = iota((1, 128), 1)
    upper = lane >= 64
    first_x = (lane & 63) == 0
    last_x = (lane & 63) == 63

    def unpack(k, carry):
        v = strip[k].astype(F32)
        b, d = pltpu.roll(v[:, 128:256], 64, 1), pltpu.roll(v[:, 256:384], 64, 1)
        at = aligned(k * TW, 32)
        strip32[pl.ds(at, 16), :] = v[:, 0:256]
        strip32[pl.ds(at + 16, 16), :] = jnp.concatenate([jnp.where(upper, d, b), d], axis=1)
        return carry

    lax.fori_loop(0, COLS, unpack, 0, unroll=8)
    strip32[IMG_W:, :] = jnp.zeros((8, 256), F32)
    grads[...] = jnp.zeros(grads.shape, F32)
    w_back[...] = jnp.zeros(w_back.shape, BF)
    for g, source in enumerate((mine, other)):
        w_one[g] = source[1024:1120, :]
        w_pre[g] = (0.5 * taller(source[1024:1120, :].astype(F32))).T.astype(BF)
        score[g] = taller(source[1120:1136, :].astype(F32)).T
        for i in range(4):
            first, second = (
                pltpu.roll(
                    source[i * 256 + k * 128 : i * 256 + (k + 1) * 128, :].astype(F32).T, 64, 1
                )
                for k in range(2)
            )
            at = slice((i // 2) * 128, (i // 2 + 1) * 128)
            w_two[g, i % 2, 0:128, at] = jnp.where(upper, second, first).astype(BF)
            w_two[g, i % 2, 128:256, at] = jnp.where(upper, first, 0.0).astype(BF)
            w_two[g, i % 2, 256:384, at] = jnp.where(upper, 0.0, second).astype(BF)
        for par in range(2):
            for p in range(2):
                for t in range(2):
                    i = par + 2 * t
                    for kind, j in ((0, 1 + p), (1 + p, 3 - 3 * p)):
                        w_back[
                            g,
                            (par * 2 + p) * 64 : (par * 2 + p + 1) * 64,
                            (t * 3 + kind) * 128 : (t * 3 + kind + 1) * 128,
                        ] = 0.5 * source[i * 256 + j * 64 : i * 256 + (j + 1) * 64, :]
    for t in (two, two_b):
        t[:, 0:128] = jnp.zeros((384, 128), BF)
        t[:, (STEPS + 1) * 128 :] = jnp.zeros((384, 128), BF)
    for t in (cols, cols_b):
        t[192:, :] = jnp.zeros((64, 384), F32)
    x, n = iota((CROP + 8, 384), 0), iota((CROP + 8, 384), 1)
    wanted = 4 * (n & 63) + (n >> 6) - 1
    wanted_ok = (wanted >= 0) & (wanted < CROP)
    distance[...] = jnp.where(wanted_ok, x - wanted, -1).astype(F32)

    def gap(dims, rho, n):
        tile, i, k = rho >> 4, (rho >> 2) & 3, rho & 3
        u = 2 * jnp.where(tile >= HALF, tile - HALF, tile) + jnp.where(tile >= HALF, 1, 0)
        return jnp.where(k < 3, n - (k * 40 + 2 * u + i), -1).astype(F32)

    dims = (TILES * 16, 128)
    row_gap[...] = gap(dims, iota(dims, 0), iota(dims, 1))
    dims = (128, TILES * 16)
    row_gap_back[...] = gap(dims, iota(dims, 1), iota(dims, 0))
    wide = iota((1, 256), 1)

    def anchor(q, k):
        return meta[2 + 2 * q + k]

    def owner_of(q):
        return meta[2 + 2 * CROPS + q]

    def job(q, live, x_all, pre, act, two, cols):
        top, left, g = anchor(q, 0), anchor(q, 1), (owner_of(q) ^ me) & 1
        y0 = first_row - top
        v0 = lax.shift_right_arithmetic(y0 - 3, 2)
        e = 4 * v0 - y0 + 6
        crop_row = y0 - 9 + (wide & 63)
        in_crop = (crop_row >= 0) & (crop_row < CROP) & (wide < 192)
        here = pl.ds(aligned((left >> 3) * 8, 8), CROP + 8)
        window = jnp.where(in_crop, strip32[here, :], 0.0).astype(BF)
        pick = jnp.where(distance[...] == (left & 7).astype(F32), 1.0, 0.0).astype(BF)
        cols_of = mm(window, pick, 0, 0)
        none = jnp.zeros((8, 384), F32)
        halves = [
            jnp.concatenate(
                [cols_of[k * 64 + 24 * h : k * 64 + 24 * h + 40, :] for k in range(3)] + [none],
                axis=0,
            )
            for h in range(2)
        ]
        mixed = []
        for m in range(6):
            tile = slice((m // 2) * 128, (m // 2 + 1) * 128)
            low, high = halves[0][:, tile], halves[1][:, tile]
            if m % 2 == 0:
                high = pltpu.roll(high, 64, 1)
            else:
                low = pltpu.roll(low, 64, 1)
            mixed.append(jnp.where(upper, high, low))
        yield
        chosen = jnp.where(row_gap[...] == e.astype(F32), 1.0, 0.0).astype(BF)
        patches = mm(chosen, jnp.concatenate(mixed, axis=1).astype(BF)).astype(BF)
        for t in range(TILES):
            for m in range(6):
                x_all[m * 16 : (m + 1) * 16, t * 128 : (t + 1) * 128] = patches[
                    t * 16 : (t + 1) * 16, m * 128 : (m + 1) * 128
                ]
        yield
        weight = w_pre[g][:, 0:96]
        for t0 in range(0, TILES, 2):
            at = slice(t0 * 128, (t0 + 2) * 128)
            value = mm(weight, x_all[:, at])
            for t in range(t0, t0 + 2):
                at = slice(t * 128, (t + 1) * 128)
                n = 2 * (t % HALF) + t // HALF + jnp.where(upper, 2 * STEPS, 0)
                u = 2 * v0 - 1 + n
                ok = ((u >= 0) & (u < CROP // 2)).astype(F32)
                half = value[:, (t - t0) * 128 : (t - t0 + 1) * 128]
                rise = jnp.tanh(half) + 1.0
                kept = rise * ok
                pre[:, at] = kept * (1.0 + half * (2.0 - rise))
                act[:, at] = (half * kept).astype(BF)
            yield
        column = score[g][:, 0:1]
        for t0 in range(0, STEPS, 2):
            value = 0.0
            for par in range(2):
                at = par * EVEN + t0 * 128
                taps = jnp.concatenate(
                    [act[:, at : at + 256], act[:, at + 128 : at + 384]], axis=0
                )
                value = value + mm(w_two[g, par], taps)
            for t in range(t0, t0 + 2):
                at = slice((t - t0) * 128, (t - t0 + 1) * 128)
                f = value[0:128, at]
                f = f + jnp.where(first_x, 0.0, pltpu.roll(value[128:256, at], 1, 1))
                f = f + jnp.where(last_x, 0.0, pltpu.roll(value[256:384, at], 127, 1))
                f, slope = silu_parts(f)
                logit = jnp.sum(f * column, axis=0, keepdims=True)
                v = v0 + t + jnp.where(upper, STEPS, 0)
                ok = (v >= 0) & (v < CROP // 4)
                grad = jnp.where(ok, -LOSS_SCALE * sigmoid(-logit), 0.0)
                b = grad * (column * slope)
                at = slice((t + 1) * 128, (t + 2) * 128)
                two[0:128, at] = b.astype(BF)
                two[128:256, at] = jnp.where(first_x, 0.0, pltpu.roll(b, 1, 1)).astype(BF)
                two[256:384, at] = jnp.where(last_x, 0.0, pltpu.roll(b, 127, 1)).astype(BF)
            yield
        for s0 in range(0, HALF, 2):
            n = min(2, HALF - s0) * 128
            at = s0 * 128
            both = jnp.concatenate([two[:, 128 + at : 128 + at + n], two[:, at : at + n]], axis=0)
            up = mm(w_back[g], both)
            for par in range(2):
                here = slice(par * EVEN + at, par * EVEN + at + n)
                one = (up[par * 128 : (par + 1) * 128] * pre[:, here]).astype(BF)
                x_all[:, here] = mm(w_one[g], one).astype(BF)
            yield
        spread = jnp.concatenate(
            [
                jnp.concatenate(
                    [
                        x_all[m * 16 : (m + 1) * 16, t * 128 : (t + 1) * 128]
                        for t in range(TILES)
                    ],
                    axis=0,
                )
                for m in range(6)
            ],
            axis=1,
        )
        chosen = jnp.where(row_gap_back[...] == e.astype(F32), 1.0, 0.0).astype(BF)
        back = mm(chosen, spread)
        yield
        parts = []
        for h in range(2):
            tiles = []
            for k in range(3):
                low = back[:, 2 * k * 128 : (2 * k + 1) * 128]
                high = back[:, (2 * k + 1) * 128 : (2 * k + 2) * 128]
                if h == 0:
                    high = pltpu.roll(high, 64, 1)
                else:
                    low = pltpu.roll(low, 64, 1)
                tiles.append(jnp.where(upper, high, low))
            parts.append(jnp.concatenate(tiles, axis=1))
        for k in range(3):
            low, high = (part[k * 40 : (k + 1) * 40, :] for part in parts)
            cols[k * 64 : (k + 1) * 64, :] = jnp.concatenate(
                [low[0:24], low[24:40] + high[0:16], high[16:40]], axis=0
            )
        yield
        placed = mm(pick, cols[...].astype(BF), 1, 1)
        y = wide & 63
        keep = in_crop & (y >= 9) & (y < 9 + SHARE) & live
        yield
        here = pl.ds(aligned((left >> 3) * 8 + GRAD_PAD, 8), CROP + 8)
        grads[here, :] = grads[here, :] + jnp.where(keep, placed, 0.0)

    count = jnp.int32(0)
    for q in range(CROPS):
        y0 = first_row - anchor(q, 0)
        shared = (owner_of(q) >> 1) == (me >> 1)
        shared = shared & (y0 < CROP) & (y0 + SHARE > 0)
        jobs[count] = q
        count = count + shared.astype(jnp.int32)

    def two_crops(k, carry):
        last = jnp.minimum(2 * k + 1, count - 1)
        running = [
            job(jobs[2 * k], True, x_all, pre, act, two, cols),
            job(jobs[last], 2 * k + 1 < count, x_all_b, pre_b, act_b, two_b, cols_b),
        ]
        while running:
            running = [g for g in running if next(g, STOP) is not STOP]
        return carry

    lax.fori_loop(0, (count + 1) >> 1, two_crops, 0)

    def pack(k, carry):
        block = grads[pl.ds(aligned(k * TW, 32), 48), :][GRAD_PAD - 2 : GRAD_PAD + 38]
        a, b = block[:, 0:128], block[:, 128:256]
        out[k] = jnp.where(
            lane < 40,
            pltpu.roll(a, 128 - 9, 1),
            jnp.where(lane < 80, pltpu.roll(a, 128 - 33, 1), pltpu.roll(b, 71, 1)),
        ).astype(BF)
        return carry

    lax.fori_loop(0, COLS, pack, 0, unroll=4)


def finish_kernel(
    meta, parts, lpips, slope, feats, w_mid, w_out, out, turned, planes, px, bm, w, w1
):
    r, c = meta[0], meta[1]
    for dy in range(3):
        for dx in range(3):
            w[dx * 128 : (dx + 1) * 128, dy * 128 : (dy + 1) * 128] = w_mid[2 - dy, 2 - dx]

    def small(dy):
        flipped = [w_out[2 - dy, (2 - dx) * 8 : (3 - dx) * 8, :] for dx in range(3)]
        return jnp.concatenate(flipped + [jnp.zeros((8, 128), F32)], axis=0)

    patch_weights(w1, small)
    col_ok = column_mask(c * TW - 2)
    planes[...] = jnp.zeros(planes.shape, F32)
    for half in range(2):
        total = parts[half].astype(F32)
        for k in range(1, COLS // 2):
            total = total + parts[2 * k + half].astype(F32)
        turned[...] = taller(total).T
        for k in range(3):
            planes[pl.ds(half * SHARE * 8 + k, 40, stride=8), :] = turned[k * 40 : (k + 1) * 40, :]

    def gather(i, carry):
        at = pl.ds(aligned(i * 32, 32), 32)
        ok = planar_inside(r * TH - 2 + i * 4, c * TW - 2, 0, 36, 4, 4)
        px[pl.ds(aligned(i * WIDE, 16), WIDE), :] = patch_tile(
            jnp.where(ok, lpips[at, :] + planes[at, :], 0.0)
        )
        return carry

    lax.fori_loop(0, 17, gather, 0, unroll=True)
    px[17 * WIDE :, :] = jnp.zeros((WIDE, 128), BF)

    def middle(tile, count):
        v = from_colours(px, tile, count, w1)
        for j in range(count):
            for k in range(4):
                n = (tile + j) * 4 + k
                x = v[j * WIDE : (j + 1) * WIDE, k * 128 : (k + 1) * 128]
                x = keep_inside(x * slope[n].astype(F32), r * TH - 1 + n, 1, col_ok)
                bm[pl.ds(aligned(n * WIDE, 16), WIDE), :] = x.astype(BF)

    def middle_group(i, carry):
        middle(i * 4, 4)
        return carry

    lax.fori_loop(0, 4, middle_group, 0, unroll=True)
    middle(16, 1)

    def last(i, carry):
        v = conv_rows(bm, i * 8, 8, w[...], transposed=True, shift=2)
        v = v.reshape(8, WIDE, 128)[:, 0:TW, :]
        x = feats[pl.ds(i * 8, 8)].astype(F32)
        out[pl.ds(i * 8, 8)] = (v * silu_parts(x)[1]).astype(BF)
        return carry

    lax.fori_loop(0, TH // 8, last, 0, unroll=4)


def call(kernel, outs, scratch, args, scalars=1, unused=0, lists=()):
    specs = [pl.BlockSpec(memory_space=pltpu.SMEM)] * scalars
    specs += [pl.BlockSpec(memory_space=pltpu.VMEM)] * (len(args) - scalars - unused)
    specs += [pl.BlockSpec(memory_space=pl.ANY)] * unused
    return pl.pallas_call(
        kernel,
        in_specs=specs,
        out_specs=jax.tree.map(lambda _: pl.BlockSpec(memory_space=pltpu.VMEM), outs),
        out_shape=outs,
        scratch_shapes=[pltpu.VMEM(s, t) for s, t in scratch] + list(lists),
        compiler_params=pltpu.CompilerParams(vmem_limit_bytes=VMEM),
        interpret=INTERPRET,
    )(*args)


INTERPRET = False


def shape(dims, kind):
    return jax.ShapeDtypeStruct(dims, kind)


def colour_first(w):
    w = jnp.pad(w.astype(F32), ((0, 0), (0, 1), (0, 5), (0, 128 - w.shape[-1])))
    return w.reshape(3, 32, 128)


def decode(meta, top, mid, bot, left, right, conv_mid, small):
    return call(
        decode_kernel,
        (
            shape((COLS, TW // 2, 384), BF),
            shape((1024, 128), F32),
            pltpu.HBM((68, WIDE, 128), BF),
        ),
        [((90 * WIDE, 128), BF), ((98 * WIDE, 128), BF), ((384, 384), BF), ((384, 384), BF)],
        (meta, top, mid, bot, left, right, conv_mid, small),
    )


def percept(meta, dec, tall, left, right, small, vgg_second, weights):
    scaled = jnp.pad(2.0 * LOSS_SCALE * weights, (0, 64)).reshape(1, 128)
    return call(
        percept_kernel,
        (
            pltpu.HBM((72 * WIDE, 128), BF),
            pltpu.HBM((76 * WIDE, 128), BF),
            shape((8, 128), F32),
        ),
        [
            ((80 * 8, 128), F32),
            ((20 * WIDE, 128), BF),
            ((76 * WIDE, 128), BF),
            ((256, 512), BF),
            ((384, 384), BF),
        ],
        (meta, dec, tall, left, right, small, vgg_second, scaled),
    )


def percept_back(meta, feat, slope_one, small, vgg_second):
    return call(
        percept_back_kernel,
        shape((80 * 8, 128), F32),
        [((82 * WIDE, 128), BF), ((384, 384), BF), ((384, 384), BF)],
        (meta, feat, slope_one, small, vgg_second),
    )


def critic_weights(first, second, score):
    w = jnp.pad(first, ((0, 0), (0, 0), (0, 1), (0, 0)))
    w = jnp.transpose(w, (1, 0, 2, 3)).reshape(4, 16, 64)
    w = jnp.concatenate(
        [jnp.pad(w, ((0, 2), (0, 0), (0, 0))), jnp.pad(w, ((2, 0), (0, 0), (0, 0)))], -1
    ).reshape(96, 128)
    score = jnp.pad(score[None], ((0, 15), (0, 0)))
    return jnp.concatenate([second.reshape(1024, 128), w, score], 0)


def critics(meta, strip, mine, other, after):
    pair = [
        ((96, LANES), BF),
        ((128, LANES), F32),
        ((128, LANES), BF),
        ((384, (STEPS + 2) * 128), BF),
        ((256, 384), F32),
    ]
    return call(
        critic_kernel,
        shape((COLS, 40, 128), BF),
        [
            ((IMG_W + 8, 256), F32),
            ((IMG_W + 24, 256), F32),
            ((2, 128, 128), BF),
            ((2, 96, 128), BF),
            ((2, 2, 384, 256), BF),
            ((2, 256, 768), BF),
            ((2, 128, 128), F32),
            ((CROP + 8, 384), F32),
            ((TILES * 16, 128), F32),
            ((128, TILES * 16), F32),
        ]
        + [buffer for buffer in pair for _ in range(2)],
        (meta, strip, mine, other, after),
        unused=1,
        lists=[pltpu.SMEM((CROPS,), jnp.int32)],
    )


def finish(meta, parts, lpips, slope, feats, conv_mid, small):
    return call(
        finish_kernel,
        shape((TH, TW, 128), BF),
        [
            ((128, 128), F32),
            ((80 * 8, 128), F32),
            ((18 * WIDE, 128), BF),
            ((68 * WIDE, 128), BF),
            ((384, 384), BF),
            ((256, 512), BF),
        ],
        (meta, parts, lpips, slope, feats, conv_mid, small),
    )


def in_hbm(x):
    return pltpu.with_memory_space_constraint(x, pltpu.HBM)


def exchange(low, high, axis):
    count = lax.axis_size(axis)
    forward = [(i, i + 1) for i in range(count - 1)]
    backward = [(target, source) for source, target in forward]
    return lax.ppermute(low, axis, forward), lax.ppermute(high, axis, backward)


def local(
    features, conv_mid, conv_out, target, vgg_first, vgg_second, perceptual_weights,
    crop_anchors, crop_owner, critic_first, critic_second, critic_score,
):
    meta = jnp.concatenate(
        [
            jnp.stack([lax.axis_index("row"), lax.axis_index("col")]).astype(jnp.int32),
            crop_anchors.reshape(2 * CROPS),
            crop_owner.reshape(CROPS),
        ]
    )
    feats = features[0]
    planar = jnp.transpose(target[0], (2, 1, 0))

    def row_part(rows, colours):
        colours = jnp.transpose(colours, (1, 0, 2)).reshape(TW, 3 * TGT_HALO)
        colours = jnp.pad(colours, ((0, 0), (0, 128 - 3 * TGT_HALO)))
        return jnp.concatenate([rows, colours[None]], 0)

    top, bot = exchange(
        row_part(feats[TH - FEAT_HALO :], planar[:, :, TH - TGT_HALO :]),
        row_part(feats[:FEAT_HALO], planar[:, :, :TGT_HALO]),
        "row",
    )

    def colours_of(part):
        part = part[FEAT_HALO, :, : 3 * TGT_HALO].reshape(TW, 3, TGT_HALO)
        return jnp.transpose(part, (1, 0, 2))

    tall = jnp.concatenate(
        [
            colours_of(top),
            planar,
            colours_of(bot),
            jnp.zeros((3, TW, 128 - TH - 2 * TGT_HALO), BF),
        ],
        2,
    )

    def edge(first, last):
        parts = (top[:FEAT_HALO], feats, bot[:FEAT_HALO], tall)
        return jnp.concatenate([a[:, first:last] for a in parts], 0)

    left, right = exchange(edge(TW - COL_HALO, TW), edge(0, COL_HALO), "col")
    out_small = colour_first(jnp.transpose(conv_out, (0, 1, 3, 2)))
    vgg_small = colour_first(vgg_first)
    pay, dec, slope = decode(meta, top, feats, bot, left, right, conv_mid, out_small)
    strip = lax.all_to_all(pay, "col", split_axis=0, concat_axis=0, tiled=True)
    mine = critic_weights(critic_first[0], critic_second[0], critic_score[0])
    other = lax.ppermute(mine, "col", [(i, i ^ 1) for i in range(COLS)])
    feat, slope_one, done = percept(
        meta, dec, tall, left, right, vgg_small, vgg_second, perceptual_weights
    )
    grads = critics(meta, strip, mine, other, done)
    parts = lax.all_to_all(grads, "col", split_axis=0, concat_axis=0, tiled=True)
    lpips = percept_back(meta, in_hbm(feat), in_hbm(slope_one), vgg_small, vgg_second)
    return finish(meta, parts, lpips, slope, feats, conv_mid, out_small)[None]


def solution(mesh):
    placed = (
        P(None, "row", "col", None),
        P(),
        P(),
        P(None, "row", "col", None),
        P(),
        P(),
        P(),
        P(),
        P(),
        P("col", None, None, None, None),
        P("col", None, None, None, None),
        P("col", None),
    )
    return jax.shard_map(
        local, mesh=mesh, in_specs=placed, out_specs=P(None, "row", "col", None), check_vma=False
    )
```

```python
import jax
import jax.numpy as jnp
import numpy as np
from jax import lax
from jax.experimental import pallas as pl
from jax.experimental.pallas import tpu as pltpu
from jax.sharding import PartitionSpec as P

BF = jnp.bfloat16
F32 = jnp.float32

LOSS_SCALE = 32.0
EPSILON = 1e-06
CROP = 256
TH, TW = 64, 32
IMG_H, IMG_W = 512, 1024
ROWS, COLS = 8, 32
CROPS = 64
DEC_HALO = 11
FEAT_HALO = 13
COL_HALO = 8
WIDE = TW + 2 * COL_HALO
TGT_HALO = 6
GRAD_PAD = 8
SHARE = 34
VMEM = 20 * 1024 * 1024


def sigmoid(v):
    return 0.5 * jnp.tanh(0.5 * v) + 0.5


def silu_parts(v):
    sig = sigmoid(v)
    act = v * sig
    return act, sig + act * (1.0 - sig)


def mm(a, b, ca=1, cb=0):
    return lax.dot_general(a, b, (((ca,), (cb,)), ((), ())), preferred_element_type=F32)


def iota(shape, dim):
    return lax.broadcasted_iota(jnp.int32, shape, dim)


def aligned(start, unit):
    return pl.multiple_of(start, unit) if not isinstance(start, int) else start


def conv_rows(src, row0, rows, weight, transposed=False, shift=0):
    n = rows * WIDE
    lhs = jnp.concatenate(
        [src[pl.ds(aligned((row0 + dy) * WIDE, 16), n), :] for dy in range(3)], axis=1
    )
    z = mm(lhs, weight, 1, 1 if transposed else 0)
    parts = []
    for dx in range(3):
        amount = (1 - dx - shift) % n
        part = z[:, dx * 128 : (dx + 1) * 128]
        parts.append(pltpu.roll(part, amount, 0) if amount else part)
    return parts[0] + parts[1] + parts[2]


def column_mask(col_first):
    x = col_first + iota((1, WIDE, 128), 1)
    return ((x >= 0) & (x < IMG_W)).astype(F32)


def keep_inside(v, row_first, rows, col_ok):
    y = row_first + iota((rows, 1, 128), 0)
    row_ok = ((y >= 0) & (y < IMG_H)).astype(F32)
    return (v.reshape(rows, WIDE, 128) * (col_ok * row_ok)).reshape(rows * WIDE, 128)


def planar_inside(row_first, col_first, low, high, rows, limit):
    lane = iota((rows * 8, 128), 1)
    row = iota((rows * 8, 128), 0) >> 3
    x = col_first + lane
    y = row_first + row
    ok = (x >= 0) & (x < IMG_W) & (lane >= low) & (lane < high) & (y >= 0) & (y < IMG_H)
    return ok & (row < limit)


def wider(v):
    return jnp.concatenate([v, jnp.zeros((v.shape[0], 128 - v.shape[1]), F32)], axis=1)


def taller(v):
    return jnp.concatenate([v, jnp.zeros((128 - v.shape[0], 128), F32)], axis=0)


def colour_weights(w, small):
    k = iota((32, 384), 0)
    n = iota((32, 384), 1)
    copies = (((n >> 7) * 8 + (n & 7)) == k).astype(F32).astype(BF)
    for dy in range(3):
        w[dy * 128 : (dy + 1) * 128, :] = mm(small(dy).astype(BF), copies, 0, 0).astype(BF)


def to_colours(src, first, w):
    group = iota((WIDE, 128), 1) >> 3
    tile = jnp.zeros((WIDE, 128), F32)
    for half in range(2):
        v = conv_rows(src, first + half * 8, 8, w[...])
        for k in range(8):
            tile = jnp.where(group == half * 8 + k, v[k * WIDE : (k + 1) * WIDE], tile)
    return taller(tile).T


def patch_tile(v):
    after, before = pltpu.roll(v, 1, 1), pltpu.roll(v, 127, 1)
    none = jnp.zeros((8, 128), F32)
    parts = []
    for k in range(4):
        at = slice(k * 8, (k + 1) * 8)
        parts += [after[at], v[at], before[at], none]
    return jnp.concatenate(parts, axis=0).T[0:WIDE].astype(BF)


def patch_weights(w, small):
    w[...] = jnp.zeros(w.shape, BF)
    for k in range(4):
        for dy in range(3):
            w[(k + dy) * 32 : (k + dy + 1) * 32, k * 128 : (k + 1) * 128] = small(dy).astype(BF)


def from_colours(px, tile, count, w):
    at = [pl.ds(aligned((tile + k) * WIDE, 16), count * WIDE) for k in range(2)]
    return mm(jnp.concatenate([px[at[0], :], px[at[1], :]], axis=1), w[...])


def pack_kernel(feats, target, low, high, side_l, side_r, *corners):
    lane = iota((TW, 128), 1)
    colours = [wider(target[k].astype(F32)) for k in range(3)]
    n = TGT_HALO
    whole = feats[...].astype(F32)
    for k, (out, x0) in enumerate(((side_l, TW - COL_HALO), (side_r, 0))):
        edge = slice(x0, x0 + COL_HALO)
        out[0:TH] = whole[:, edge, :].astype(BF)
        for j in range(3):
            out[TH + j] = colours[j][edge].astype(BF)
    for k, (out, y0, t0) in enumerate(((low, TH - FEAT_HALO, TH - n), (high, 0, 0))):
        rows = whole[y0 : y0 + FEAT_HALO]
        extra = jnp.zeros((TW, 128), F32)
        for j in range(3):
            moved = pltpu.roll(colours[j], (n * j - t0) % 128, 1)
            extra = jnp.where((lane >= n * j) & (lane < n * j + n), moved, extra)
        out[0:FEAT_HALO] = rows.astype(BF)
        out[FEAT_HALO] = extra.astype(BF)
        for j, x0 in enumerate((TW - COL_HALO, 0)):
            edge = slice(x0, x0 + COL_HALO)
            corners[2 * k + j][0:FEAT_HALO] = rows[:, edge, :].astype(BF)
            corners[2 * k + j][FEAT_HALO] = extra[edge].astype(BF)


def decode_kernel(
    meta, top, mid, bot, left, right, tl, tr, bl, br, w_mid, w_out, pay, dec, slope_out,
    s1, s2, w, w3,
):
    r, c = meta[0], meta[1]
    for dy in range(3):
        for dx in range(3):
            w[dy * 128 : (dy + 1) * 128, dx * 128 : (dx + 1) * 128] = w_mid[dy, dx]
    colour_weights(w3, lambda dy: w_out[dy])

    def fill(first, rows, parts):
        n = rows * WIDE
        v = jnp.concatenate([p.astype(F32) for p in parts], axis=1).reshape(n, 128)
        s1[pl.ds(aligned(first * WIDE, 16), n), :] = (v * sigmoid(v)).astype(BF)

    near = slice(0, FEAT_HALO)
    fill(0, FEAT_HALO, (tl[near], top[near], tr[near]))
    fill(FEAT_HALO + TH, FEAT_HALO, (bl[near], bot[near], br[near]))

    def fill_mid(i, carry):
        at = pl.ds(i * 8, 8)
        fill(FEAT_HALO + i * 8, 8, (left[at], mid[at], right[at]))
        return carry

    lax.fori_loop(0, TH // 8, fill_mid, 0, unroll=2)
    col_ok = column_mask(c * TW - COL_HALO)

    def middle(i, carry):
        v = conv_rows(s1, i * 8, 8, w[...])
        act, slope = silu_parts(v)
        act = keep_inside(act, r * TH - 12 + i * 8, 8, col_ok)
        s2[pl.ds(aligned(i * 8 * WIDE, 16), 8 * WIDE), :] = act.astype(BF)
        slope = pltpu.roll(slope, 8 * WIDE - 6, 0).reshape(8, WIDE, 128).astype(BF)
        first, last = max(i * 8, 11), min(i * 8 + 8, 79)
        if first < last:
            slope_out[first - 11 : last - 11] = slope[first - i * 8 : last - i * 8]
        return carry

    for i in range(11):
        middle(i, 0)
    s2[88 * WIDE :, :] = jnp.zeros((10 * WIDE, 128), BF)
    dec[768:, :] = jnp.zeros((256, 128), F32)

    def colours(i, carry):
        v = to_colours(s2, i * 16, w3)
        ok = planar_inside(
            r * TH - DEC_HALO + i * 16, c * TW - COL_HALO, 2, WIDE - 2, 16, 86 - i * 16
        )
        dec[pl.ds(aligned(i * 128, 128), 128), :] = jnp.where(ok, v, 0.0).astype(BF).astype(F32)
        return carry

    lax.fori_loop(0, 6, colours, 0, unroll=True)
    planes = [
        dec[pl.ds(k, 128, stride=8), :].T[COL_HALO : COL_HALO + TW, :] for k in range(3)
    ]
    upper = iota((16, 128), 1) >= 64
    for half in range(2):
        low, high = [], []
        for x in range(2):
            for p in planes:
                p = p[x * 16 : (x + 1) * 16]
                start = half * SHARE
                low.append(pltpu.roll(p, 128 - start, 1) if start else p)
                high.append(pltpu.roll(p, 64 - start, 1))
        packed = [jnp.where(upper, high[k + 1], low[k]) for k in (0, 2, 4)]
        packed = jnp.concatenate(packed, axis=1).astype(BF)
        for k in range(COLS // 2):
            pay[2 * k + half] = packed


def percept_kernel(
    meta, dec, target, top, bot, left, right, tl, tr, bl, br, v_first, v_second, weights,
    feat, slope_one, done,
    planes, px, one, w1, w2,
):
    r, c = meta[0], meta[1]
    col_first = c * TW - COL_HALO
    col_ok = column_mask(col_first)

    def first_small(dy):
        v = v_first[dy]
        return v + pltpu.roll(pltpu.roll(v, 3, 0), 64, 1)

    patch_weights(w1, first_small)
    for dy in range(3):
        for dx in range(3):
            v = v_second[dy, dx].astype(F32)
            v = jnp.concatenate([v, jnp.zeros((64, 64), F32)], axis=1)
            u = pltpu.roll(v, 64, 1)
            w2[dy * 128 : (dy + 1) * 128, dx * 128 : (dx + 1) * 128] = jnp.concatenate(
                [v, u], axis=0
            ).astype(BF)

    planes[...] = jnp.zeros(planes.shape, F32)
    lane = iota((WIDE, 128), 1)

    def across(parts):
        return jnp.concatenate([p.astype(F32) for p in parts], axis=0)

    above = across((tl[FEAT_HALO], top[FEAT_HALO], tr[FEAT_HALO]))
    below = across((bl[FEAT_HALO], bot[FEAT_HALO], br[FEAT_HALO]))
    for k in range(3):
        mid = across((left[TH + k], wider(target[k].astype(F32)), right[TH + k]))
        n = TGT_HALO
        v = jnp.where(
            lane < n,
            pltpu.roll(above, (128 - n * k) % 128, 1),
            jnp.where(lane < n + TH, pltpu.roll(mid, n, 1), pltpu.roll(below, n + TH - n * k, 1)),
        )
        v = jnp.where(lane < 2 * n + TH, v, 0.0)
        planes[pl.ds(3 + k, 80, stride=8), :] = taller(v).T[0:80]

    done[...] = jnp.zeros((8, 128), F32)

    def gather(i, carry):
        v = dec[pl.ds(aligned(i * 32 + 40, 8), 32), :] + planes[pl.ds(aligned(i * 32, 32), 32), :]
        px[pl.ds(aligned(i * WIDE, 16), WIDE), :] = patch_tile(v)
        return carry

    lax.fori_loop(0, 19, gather, 0, unroll=True)
    px[19 * WIDE :, :] = jnp.zeros((WIDE, 128), BF)

    def first(tile, count):
        v = from_colours(px, tile, count, w1)
        for j in range(count):
            for k in range(4):
                p = (tile + j) * 4 + k
                x = v[j * WIDE : (j + 1) * WIDE, k * 128 : (k + 1) * 128]
                act, slope = silu_parts(x)
                act = keep_inside(act, r * TH - 5 + p, 1, col_ok)
                slope_one[pl.ds(aligned(p * WIDE, 16), WIDE), :] = slope.astype(BF)
                one[pl.ds(aligned(p * WIDE, 16), WIDE), :] = act.astype(BF)

    def first_group(i, carry):
        first(i * 4, 4)
        return carry

    lax.fori_loop(0, 4, first_group, 0, unroll=True)
    first(16, 3)
    ones = ((iota((128, 128), 0) >> 6) == (iota((128, 128), 1) >> 6)).astype(F32).astype(BF)

    def half_sum(v):
        high = v.astype(BF)
        low = (v - high.astype(F32)).astype(BF)
        return mm(high, ones) + mm(low, ones)

    def second(i, carry):
        v = conv_rows(one, i * 8, 8, w2[...])
        f, slope = silu_parts(v)
        scale = lax.rsqrt(half_sum(f * f) + EPSILON)
        unit = f * scale
        weighted = weights[...] * (unit - pltpu.roll(unit, 64, 1))
        g = scale * (weighted - unit * half_sum(weighted * unit)) * slope
        g = keep_inside(g, r * TH - 4 + i * 8, 8, col_ok)
        feat[pl.ds(aligned(i * 8 * WIDE, 16), 8 * WIDE), :] = g.astype(BF)
        return carry

    lax.fori_loop(0, 9, second, 0, unroll=3)


def percept_back_kernel(meta, feat, slope_one, v_first, v_second, out, bv, w3, w4):
    r, c = meta[0], meta[1]
    col_ok = column_mask(c * TW - COL_HALO)

    def last_small(dy):
        parts = [v_first[2 - dy, (2 - dx) * 8 : (3 - dx) * 8, :] for dx in range(3)]
        return jnp.concatenate(parts + [jnp.zeros((8, 128), F32)], axis=0)

    colour_weights(w4, last_small)
    for dy in range(3):
        for dx in range(3):
            v = v_second[dy, dx].astype(F32)
            v = jnp.concatenate([v, jnp.zeros((64, 64), F32)], axis=1)
            w3[(2 - dx) * 128 : (3 - dx) * 128, (2 - dy) * 128 : (3 - dy) * 128] = jnp.concatenate(
                [v, jnp.zeros((64, 128), F32)], axis=0
            ).astype(BF)

    def back(i, carry):
        v = conv_rows(feat, i * 10, 10, w3[...], transposed=True)
        x = slope_one[pl.ds(aligned((i * 10 + 2) * WIDE, 16), 10 * WIDE), :]
        v = keep_inside(v * x.astype(F32), r * TH - 3 + i * 10, 10, col_ok)
        bv[pl.ds(aligned(i * 10 * WIDE, 16), 10 * WIDE), :] = v.astype(BF)
        return carry

    lax.fori_loop(0, 7, back, 0, unroll=True)
    bv[70 * WIDE :, :] = jnp.zeros((12 * WIDE, 128), BF)

    def colours(i, carry):
        v = to_colours(bv, i * 16, w4)
        out[pl.ds(aligned(i * 128, 128), 128), :] = pltpu.roll(v, 122, 1)
        return carry

    lax.fori_loop(0, 5, colours, 0, unroll=True)


STOP = object()
STEPS = 6
HALF = STEPS + 1
TILES = 2 * HALF
LANES = TILES * 128
EVEN = HALF * 128


def critic_kernel(
    meta, strip, mine, other, _, out,
    strip32, grads, w_pre, w_one, w_two, w_back, score, distance, row_gap, row_gap_back, x_all, x_all_b, pre, pre_b, act, act_b,
    two, two_b, cols, cols_b, jobs,
):
    r, me = meta[0], meta[1]
    first_row = r * TH - 2 + SHARE * (me & 1)
    lane = iota((1, 128), 1)
    upper = lane >= 64
    first_x = (lane & 63) == 0
    last_x = (lane & 63) == 63

    def unpack(k, carry):
        v = strip[k].astype(F32)
        b, d = pltpu.roll(v[:, 128:256], 64, 1), pltpu.roll(v[:, 256:384], 64, 1)
        at = aligned(k * TW, 32)
        strip32[pl.ds(at, 16), :] = v[:, 0:256]
        strip32[pl.ds(at + 16, 16), :] = jnp.concatenate([jnp.where(upper, d, b), d], axis=1)
        return carry

    lax.fori_loop(0, COLS, unpack, 0, unroll=8)
    strip32[IMG_W:, :] = jnp.zeros((8, 256), F32)
    grads[...] = jnp.zeros(grads.shape, F32)
    w_back[...] = jnp.zeros(w_back.shape, BF)
    for g, source in enumerate((mine, other)):
        w_one[g] = source[1024:1120, :]
        w_pre[g] = (0.5 * taller(source[1024:1120, :].astype(F32))).T.astype(BF)
        score[g] = taller(source[1120:1136, :].astype(F32)).T
        for i in range(4):
            first, second = (
                pltpu.roll(
                    source[i * 256 + k * 128 : i * 256 + (k + 1) * 128, :].astype(F32).T, 64, 1
                )
                for k in range(2)
            )
            at = slice((i // 2) * 128, (i // 2 + 1) * 128)
            w_two[g, i % 2, 0:128, at] = jnp.where(upper, second, first).astype(BF)
            w_two[g, i % 2, 128:256, at] = jnp.where(upper, first, 0.0).astype(BF)
            w_two[g, i % 2, 256:384, at] = jnp.where(upper, 0.0, second).astype(BF)
        for par in range(2):
            for p in range(2):
                for t in range(2):
                    i = par + 2 * t
                    for kind, j in ((0, 1 + p), (1 + p, 3 - 3 * p)):
                        w_back[
                            g,
                            (par * 2 + p) * 64 : (par * 2 + p + 1) * 64,
                            (t * 3 + kind) * 128 : (t * 3 + kind + 1) * 128,
                        ] = 0.5 * source[i * 256 + j * 64 : i * 256 + (j + 1) * 64, :]
    for t in (two, two_b):
        t[:, 0:128] = jnp.zeros((384, 128), BF)
        t[:, (STEPS + 1) * 128 :] = jnp.zeros((384, 128), BF)
    for t in (cols, cols_b):
        t[192:, :] = jnp.zeros((64, 384), F32)
    x, n = iota((CROP + 8, 384), 0), iota((CROP + 8, 384), 1)
    wanted = 4 * (n & 63) + (n >> 6) - 1
    wanted_ok = (wanted >= 0) & (wanted < CROP)
    distance[...] = jnp.where(wanted_ok, x - wanted, -1).astype(F32)

    def gap(dims, rho, n):
        tile, i, k = rho >> 4, (rho >> 2) & 3, rho & 3
        u = 2 * jnp.where(tile >= HALF, tile - HALF, tile) + jnp.where(tile >= HALF, 1, 0)
        return jnp.where(k < 3, n - (k * 40 + 2 * u + i), -1).astype(F32)

    dims = (TILES * 16, 128)
    row_gap[...] = gap(dims, iota(dims, 0), iota(dims, 1))
    dims = (128, TILES * 16)
    row_gap_back[...] = gap(dims, iota(dims, 1), iota(dims, 0))
    wide = iota((1, 256), 1)

    def anchor(q, k):
        return meta[2 + 2 * q + k]

    def owner_of(q):
        return meta[2 + 2 * CROPS + q]

    def job(q, live, x_all, pre, act, two, cols):
        top, left, g = anchor(q, 0), anchor(q, 1), (owner_of(q) ^ me) & 1
        y0 = first_row - top
        v0 = lax.shift_right_arithmetic(y0 - 3, 2)
        e = 4 * v0 - y0 + 6
        crop_row = y0 - 9 + (wide & 63)
        in_crop = (crop_row >= 0) & (crop_row < CROP) & (wide < 192)
        here = pl.ds(aligned((left >> 3) * 8, 8), CROP + 8)
        window = jnp.where(in_crop, strip32[here, :], 0.0).astype(BF)
        pick = jnp.where(distance[...] == (left & 7).astype(F32), 1.0, 0.0).astype(BF)
        cols_of = mm(window, pick, 0, 0)
        none = jnp.zeros((8, 384), F32)
        halves = [
            jnp.concatenate(
                [cols_of[k * 64 + 24 * h : k * 64 + 24 * h + 40, :] for k in range(3)] + [none],
                axis=0,
            )
            for h in range(2)
        ]
        mixed = []
        for m in range(6):
            tile = slice((m // 2) * 128, (m // 2 + 1) * 128)
            low, high = halves[0][:, tile], halves[1][:, tile]
            if m % 2 == 0:
                high = pltpu.roll(high, 64, 1)
            else:
                low = pltpu.roll(low, 64, 1)
            mixed.append(jnp.where(upper, high, low))
        yield
        chosen = jnp.where(row_gap[...] == e.astype(F32), 1.0, 0.0).astype(BF)
        patches = mm(chosen, jnp.concatenate(mixed, axis=1).astype(BF)).astype(BF)
        for t in range(TILES):
            for m in range(6):
                x_all[m * 16 : (m + 1) * 16, t * 128 : (t + 1) * 128] = patches[
                    t * 16 : (t + 1) * 16, m * 128 : (m + 1) * 128
                ]
        yield
        weight = w_pre[g][:, 0:96]
        for t0 in range(0, TILES, 2):
            at = slice(t0 * 128, (t0 + 2) * 128)
            value = mm(weight, x_all[:, at])
            for t in range(t0, t0 + 2):
                at = slice(t * 128, (t + 1) * 128)
                n = 2 * (t % HALF) + t // HALF + jnp.where(upper, 2 * STEPS, 0)
                u = 2 * v0 - 1 + n
                ok = ((u >= 0) & (u < CROP // 2)).astype(F32)
                half = value[:, (t - t0) * 128 : (t - t0 + 1) * 128]
                rise = jnp.tanh(half) + 1.0
                kept = rise * ok
                pre[:, at] = kept * (1.0 + half * (2.0 - rise))
                act[:, at] = (half * kept).astype(BF)
            yield
        column = score[g][:, 0:1]
        for t0 in range(0, STEPS, 2):
            value = 0.0
            for par in range(2):
                at = par * EVEN + t0 * 128
                taps = jnp.concatenate(
                    [act[:, at : at + 256], act[:, at + 128 : at + 384]], axis=0
                )
                value = value + mm(w_two[g, par], taps)
            for t in range(t0, t0 + 2):
                at = slice((t - t0) * 128, (t - t0 + 1) * 128)
                f = value[0:128, at]
                f = f + jnp.where(first_x, 0.0, pltpu.roll(value[128:256, at], 1, 1))
                f = f + jnp.where(last_x, 0.0, pltpu.roll(value[256:384, at], 127, 1))
                f, slope = silu_parts(f)
                logit = jnp.sum(f * column, axis=0, keepdims=True)
                v = v0 + t + jnp.where(upper, STEPS, 0)
                ok = (v >= 0) & (v < CROP // 4)
                grad = jnp.where(ok, -LOSS_SCALE * sigmoid(-logit), 0.0)
                b = grad * (column * slope)
                at = slice((t + 1) * 128, (t + 2) * 128)
                two[0:128, at] = b.astype(BF)
                two[128:256, at] = jnp.where(first_x, 0.0, pltpu.roll(b, 1, 1)).astype(BF)
                two[256:384, at] = jnp.where(last_x, 0.0, pltpu.roll(b, 127, 1)).astype(BF)
            yield
        for s0 in range(0, HALF, 2):
            n = min(2, HALF - s0) * 128
            at = s0 * 128
            both = jnp.concatenate([two[:, 128 + at : 128 + at + n], two[:, at : at + n]], axis=0)
            up = mm(w_back[g], both)
            for par in range(2):
                here = slice(par * EVEN + at, par * EVEN + at + n)
                one = (up[par * 128 : (par + 1) * 128] * pre[:, here]).astype(BF)
                x_all[:, here] = mm(w_one[g], one).astype(BF)
            yield
        spread = jnp.concatenate(
            [
                jnp.concatenate(
                    [
                        x_all[m * 16 : (m + 1) * 16, t * 128 : (t + 1) * 128]
                        for t in range(TILES)
                    ],
                    axis=0,
                )
                for m in range(6)
            ],
            axis=1,
        )
        chosen = jnp.where(row_gap_back[...] == e.astype(F32), 1.0, 0.0).astype(BF)
        back = mm(chosen, spread)
        yield
        parts = []
        for h in range(2):
            tiles = []
            for k in range(3):
                low = back[:, 2 * k * 128 : (2 * k + 1) * 128]
                high = back[:, (2 * k + 1) * 128 : (2 * k + 2) * 128]
                if h == 0:
                    high = pltpu.roll(high, 64, 1)
                else:
                    low = pltpu.roll(low, 64, 1)
                tiles.append(jnp.where(upper, high, low))
            parts.append(jnp.concatenate(tiles, axis=1))
        for k in range(3):
            low, high = (part[k * 40 : (k + 1) * 40, :] for part in parts)
            cols[k * 64 : (k + 1) * 64, :] = jnp.concatenate(
                [low[0:24], low[24:40] + high[0:16], high[16:40]], axis=0
            )
        yield
        placed = mm(pick, cols[...].astype(BF), 1, 1)
        y = wide & 63
        keep = in_crop & (y >= 9) & (y < 9 + SHARE) & live
        yield
        here = pl.ds(aligned((left >> 3) * 8 + GRAD_PAD, 8), CROP + 8)
        grads[here, :] = grads[here, :] + jnp.where(keep, placed, 0.0)

    count = jnp.int32(0)
    for q in range(CROPS):
        y0 = first_row - anchor(q, 0)
        shared = (owner_of(q) >> 1) == (me >> 1)
        shared = shared & (y0 < CROP) & (y0 + SHARE > 0)
        jobs[count] = q
        count = count + shared.astype(jnp.int32)

    def two_crops(k, carry):
        last = jnp.minimum(2 * k + 1, count - 1)
        running = [
            job(jobs[2 * k], True, x_all, pre, act, two, cols),
            job(jobs[last], 2 * k + 1 < count, x_all_b, pre_b, act_b, two_b, cols_b),
        ]
        while running:
            running = [g for g in running if next(g, STOP) is not STOP]
        return carry

    lax.fori_loop(0, (count + 1) >> 1, two_crops, 0)

    def pack(k, carry):
        block = grads[pl.ds(aligned(k * TW, 32), 48), :][GRAD_PAD - 2 : GRAD_PAD + 38]
        a, b = block[:, 0:128], block[:, 128:256]
        out[k] = jnp.where(
            lane < 40,
            pltpu.roll(a, 128 - 9, 1),
            jnp.where(lane < 80, pltpu.roll(a, 128 - 33, 1), pltpu.roll(b, 71, 1)),
        ).astype(BF)
        return carry

    lax.fori_loop(0, COLS, pack, 0, unroll=4)


def finish_kernel(
    meta, parts, lpips, slope, feats, w_mid, w_out, out, turned, planes, px, bm, w, w1
):
    r, c = meta[0], meta[1]
    for dy in range(3):
        for dx in range(3):
            w[dx * 128 : (dx + 1) * 128, dy * 128 : (dy + 1) * 128] = w_mid[2 - dy, 2 - dx]

    def small(dy):
        flipped = [w_out[2 - dy, (2 - dx) * 8 : (3 - dx) * 8, :] for dx in range(3)]
        return jnp.concatenate(flipped + [jnp.zeros((8, 128), F32)], axis=0)

    patch_weights(w1, small)
    col_ok = column_mask(c * TW - 2)
    planes[...] = jnp.zeros(planes.shape, F32)
    for half in range(2):
        total = parts[half].astype(F32)
        for k in range(1, COLS // 2):
            total = total + parts[2 * k + half].astype(F32)
        turned[...] = taller(total).T
        for k in range(3):
            planes[pl.ds(half * SHARE * 8 + k, 40, stride=8), :] = turned[k * 40 : (k + 1) * 40, :]

    def gather(i, carry):
        at = pl.ds(aligned(i * 32, 32), 32)
        ok = planar_inside(r * TH - 2 + i * 4, c * TW - 2, 0, 36, 4, 4)
        px[pl.ds(aligned(i * WIDE, 16), WIDE), :] = patch_tile(
            jnp.where(ok, lpips[at, :] + planes[at, :], 0.0)
        )
        return carry

    lax.fori_loop(0, 17, gather, 0, unroll=True)
    px[17 * WIDE :, :] = jnp.zeros((WIDE, 128), BF)

    def middle(tile, count):
        v = from_colours(px, tile, count, w1)
        for j in range(count):
            for k in range(4):
                n = (tile + j) * 4 + k
                x = v[j * WIDE : (j + 1) * WIDE, k * 128 : (k + 1) * 128]
                x = keep_inside(x * slope[n].astype(F32), r * TH - 1 + n, 1, col_ok)
                bm[pl.ds(aligned(n * WIDE, 16), WIDE), :] = x.astype(BF)

    def middle_group(i, carry):
        middle(i * 4, 4)
        return carry

    lax.fori_loop(0, 4, middle_group, 0, unroll=True)
    middle(16, 1)

    def last(i, carry):
        v = conv_rows(bm, i * 8, 8, w[...], transposed=True, shift=2)
        v = v.reshape(8, WIDE, 128)[:, 0:TW, :]
        x = feats[pl.ds(i * 8, 8)].astype(F32)
        out[pl.ds(i * 8, 8)] = (v * silu_parts(x)[1]).astype(BF)
        return carry

    lax.fori_loop(0, TH // 8, last, 0, unroll=4)


def call(kernel, outs, scratch, args, scalars=1, unused=0, lists=()):
    specs = [pl.BlockSpec(memory_space=pltpu.SMEM)] * scalars
    specs += [pl.BlockSpec(memory_space=pltpu.VMEM)] * (len(args) - scalars - unused)
    specs += [pl.BlockSpec(memory_space=pl.ANY)] * unused
    return pl.pallas_call(
        kernel,
        in_specs=specs,
        out_specs=jax.tree.map(lambda _: pl.BlockSpec(memory_space=pltpu.VMEM), outs),
        out_shape=outs,
        scratch_shapes=[pltpu.VMEM(s, t) for s, t in scratch] + list(lists),
        compiler_params=pltpu.CompilerParams(vmem_limit_bytes=VMEM),
        interpret=INTERPRET,
    )(*args)


INTERPRET = False


def shape(dims, kind):
    return jax.ShapeDtypeStruct(dims, kind)


def colour_first(w):
    w = jnp.pad(w.astype(F32), ((0, 0), (0, 1), (0, 5), (0, 128 - w.shape[-1])))
    return w.reshape(3, 32, 128)


def decode(meta, feats, halo, conv_mid, small):
    top, bot, left, right, *corners = halo
    return call(
        decode_kernel,
        (
            shape((COLS, TW // 2, 384), BF),
            shape((1024, 128), F32),
            pltpu.HBM((68, WIDE, 128), BF),
        ),
        [((90 * WIDE, 128), BF), ((98 * WIDE, 128), BF), ((384, 384), BF), ((384, 384), BF)],
        (meta, top, feats, bot, left, right, *corners, conv_mid, small),
    )


def percept(meta, dec, target, halo, small, vgg_second, weights):
    scaled = jnp.pad(2.0 * LOSS_SCALE * weights, (0, 64)).reshape(1, 128)
    return call(
        percept_kernel,
        (
            pltpu.HBM((72 * WIDE, 128), BF),
            pltpu.HBM((76 * WIDE, 128), BF),
            shape((8, 128), F32),
        ),
        [
            ((80 * 8, 128), F32),
            ((20 * WIDE, 128), BF),
            ((76 * WIDE, 128), BF),
            ((256, 512), BF),
            ((384, 384), BF),
        ],
        (meta, dec, target, *halo, small, vgg_second, scaled),
    )


def percept_back(meta, feat, slope_one, small, vgg_second):
    return call(
        percept_back_kernel,
        shape((80 * 8, 128), F32),
        [((82 * WIDE, 128), BF), ((384, 384), BF), ((384, 384), BF)],
        (meta, feat, slope_one, small, vgg_second),
    )


def critic_weights(first, second, score):
    w = jnp.pad(first, ((0, 0), (0, 0), (0, 1), (0, 0)))
    w = jnp.transpose(w, (1, 0, 2, 3)).reshape(4, 16, 64)
    w = jnp.concatenate(
        [jnp.pad(w, ((0, 2), (0, 0), (0, 0))), jnp.pad(w, ((2, 0), (0, 0), (0, 0)))], -1
    ).reshape(96, 128)
    score = jnp.pad(score[None], ((0, 15), (0, 0)))
    return jnp.concatenate([second.reshape(1024, 128), w, score], 0)


def critics(meta, strip, mine, other, after):
    pair = [
        ((96, LANES), BF),
        ((128, LANES), F32),
        ((128, LANES), BF),
        ((384, (STEPS + 2) * 128), BF),
        ((256, 384), F32),
    ]
    return call(
        critic_kernel,
        shape((COLS, 40, 128), BF),
        [
            ((IMG_W + 8, 256), F32),
            ((IMG_W + 24, 256), F32),
            ((2, 128, 128), BF),
            ((2, 96, 128), BF),
            ((2, 2, 384, 256), BF),
            ((2, 256, 768), BF),
            ((2, 128, 128), F32),
            ((CROP + 8, 384), F32),
            ((TILES * 16, 128), F32),
            ((128, TILES * 16), F32),
        ]
        + [buffer for buffer in pair for _ in range(2)],
        (meta, strip, mine, other, after),
        unused=1,
        lists=[pltpu.SMEM((CROPS,), jnp.int32)],
    )


def finish(meta, parts, lpips, slope, feats, conv_mid, small):
    return call(
        finish_kernel,
        shape((TH, TW, 128), BF),
        [
            ((128, 128), F32),
            ((80 * 8, 128), F32),
            ((18 * WIDE, 128), BF),
            ((68 * WIDE, 128), BF),
            ((384, 384), BF),
            ((256, 512), BF),
        ],
        (meta, parts, lpips, slope, feats, conv_mid, small),
    )


def in_hbm(x):
    return pltpu.with_memory_space_constraint(x, pltpu.HBM)


def pack(feats, target):
    row = shape((FEAT_HALO + 1, TW, 128), BF)
    side = shape((TH + 3, COL_HALO, 128), BF)
    corner = shape((FEAT_HALO + 1, COL_HALO, 128), BF)
    return call(pack_kernel, (row, row, side, side) + (corner,) * 4, [], (feats, target), scalars=0)


def moved(x, down, right):
    rows, cols = lax.axis_size("row"), lax.axis_size("col")
    pairs = [
        (r * cols + c, (r + down) * cols + c + right)
        for r in range(rows)
        for c in range(cols)
        if 0 <= r + down < rows and 0 <= c + right < cols
    ]
    return lax.ppermute(x, ("row", "col"), pairs)


def local(
    features, conv_mid, conv_out, target, vgg_first, vgg_second, perceptual_weights,
    crop_anchors, crop_owner, critic_first, critic_second, critic_score,
):
    meta = jnp.concatenate(
        [
            jnp.stack([lax.axis_index("row"), lax.axis_index("col")]).astype(jnp.int32),
            crop_anchors.reshape(2 * CROPS),
            crop_owner.reshape(CROPS),
        ]
    )
    feats = features[0]
    planar = jnp.transpose(target[0], (2, 1, 0))

    low, high, side_l, side_r, low_l, low_r, high_l, high_r = pack(feats, planar)
    halo = (
        moved(low, 1, 0),
        moved(high, -1, 0),
        moved(side_l, 0, 1),
        moved(side_r, 0, -1),
        moved(low_l, 1, 1),
        moved(low_r, 1, -1),
        moved(high_l, -1, 1),
        moved(high_r, -1, -1),
    )
    out_small = colour_first(jnp.transpose(conv_out, (0, 1, 3, 2)))
    vgg_small = colour_first(vgg_first)
    pay, dec, slope = decode(meta, feats, halo, conv_mid, out_small)
    strip = lax.all_to_all(pay, "col", split_axis=0, concat_axis=0, tiled=True)
    mine = critic_weights(critic_first[0], critic_second[0], critic_score[0])
    other = lax.ppermute(mine, "col", [(i, i ^ 1) for i in range(COLS)])
    feat, slope_one, done = percept(
        meta, dec, planar, halo, vgg_small, vgg_second, perceptual_weights
    )
    grads = critics(meta, strip, mine, other, done)
    parts = lax.all_to_all(grads, "col", split_axis=0, concat_axis=0, tiled=True)
    lpips = percept_back(meta, in_hbm(feat), in_hbm(slope_one), vgg_small, vgg_second)
    return finish(meta, parts, lpips, slope, feats, conv_mid, out_small)[None]


def solution(mesh):
    placed = (
        P(None, "row", "col", None),
        P(),
        P(),
        P(None, "row", "col", None),
        P(),
        P(),
        P(),
        P(),
        P(),
        P("col", None, None, None, None),
        P("col", None, None, None, None),
        P("col", None),
    )
    return jax.shard_map(
        local, mesh=mesh, in_specs=placed, out_specs=P(None, "row", "col", None), check_vma=False
    )
```

```python
import jax
import jax.numpy as jnp
import numpy as np
from jax import lax
from jax.experimental import pallas as pl
from jax.experimental.pallas import tpu as pltpu
from jax.sharding import PartitionSpec as P

BF = jnp.bfloat16
F32 = jnp.float32

LOSS_SCALE = 32.0
EPSILON = 1e-06
CROP = 256
TH, TW = 64, 32
IMG_H, IMG_W = 512, 1024
ROWS, COLS = 8, 32
CROPS = 64
DEC_HALO = 11
FEAT_HALO = 13
COL_HALO = 8
WIDE = TW + 2 * COL_HALO
TGT_HALO = 6
GRAD_PAD = 8
SHARE = 34
VMEM = 20 * 1024 * 1024


def sigmoid(v):
    return 0.5 * jnp.tanh(0.5 * v) + 0.5


def silu_parts(v):
    sig = sigmoid(v)
    act = v * sig
    return act, sig + act * (1.0 - sig)


def mm(a, b, ca=1, cb=0):
    return lax.dot_general(a, b, (((ca,), (cb,)), ((), ())), preferred_element_type=F32)


def iota(shape, dim):
    return lax.broadcasted_iota(jnp.int32, shape, dim)


def aligned(start, unit):
    return pl.multiple_of(start, unit) if not isinstance(start, int) else start


def conv_rows(src, row0, rows, weight, transposed=False, shift=0):
    n = rows * WIDE
    lhs = jnp.concatenate(
        [src[pl.ds(aligned((row0 + dy) * WIDE, 16), n), :] for dy in range(3)], axis=1
    )
    z = mm(lhs, weight, 1, 1 if transposed else 0)
    parts = []
    for dx in range(3):
        amount = (1 - dx - shift) % n
        part = z[:, dx * 128 : (dx + 1) * 128]
        parts.append(pltpu.roll(part, amount, 0) if amount else part)
    return parts[0] + parts[1] + parts[2]


def column_mask(col_first):
    x = col_first + iota((1, WIDE, 128), 1)
    return ((x >= 0) & (x < IMG_W)).astype(F32)


def keep_inside(v, row_first, rows, col_ok):
    y = row_first + iota((rows, 1, 128), 0)
    row_ok = ((y >= 0) & (y < IMG_H)).astype(F32)
    return (v.reshape(rows, WIDE, 128) * (col_ok * row_ok)).reshape(rows * WIDE, 128)


def planar_inside(row_first, col_first, low, high, rows, limit):
    lane = iota((rows * 8, 128), 1)
    row = iota((rows * 8, 128), 0) >> 3
    x = col_first + lane
    y = row_first + row
    ok = (x >= 0) & (x < IMG_W) & (lane >= low) & (lane < high) & (y >= 0) & (y < IMG_H)
    return ok & (row < limit)


def taller(v):
    return jnp.concatenate([v, jnp.zeros((128 - v.shape[0], 128), F32)], axis=0)


def colour_weights(w, small):
    k = iota((32, 384), 0)
    n = iota((32, 384), 1)
    copies = (((n >> 7) * 8 + (n & 7)) == k).astype(F32).astype(BF)
    for dy in range(3):
        w[dy * 128 : (dy + 1) * 128, :] = mm(small(dy).astype(BF), copies, 0, 0).astype(BF)


def to_colours(src, first, w):
    group = iota((WIDE, 128), 1) >> 3
    tile = jnp.zeros((WIDE, 128), F32)
    for half in range(2):
        v = conv_rows(src, first + half * 8, 8, w[...])
        for k in range(8):
            tile = jnp.where(group == half * 8 + k, v[k * WIDE : (k + 1) * WIDE], tile)
    return taller(tile).T


def patch_tile(v):
    after, before = pltpu.roll(v, 1, 1), pltpu.roll(v, 127, 1)
    none = jnp.zeros((8, 128), F32)
    parts = []
    for k in range(4):
        at = slice(k * 8, (k + 1) * 8)
        parts += [after[at], v[at], before[at], none]
    return jnp.concatenate(parts, axis=0).T[0:WIDE].astype(BF)


def patch_weights(w, small):
    w[...] = jnp.zeros(w.shape, BF)
    for k in range(4):
        for dy in range(3):
            w[(k + dy) * 32 : (k + dy + 1) * 32, k * 128 : (k + 1) * 128] = small(dy).astype(BF)


def from_colours(px, tile, count, w):
    at = [pl.ds(aligned((tile + k) * WIDE, 16), count * WIDE) for k in range(2)]
    return mm(jnp.concatenate([px[at[0], :], px[at[1], :]], axis=1), w[...])


def decode_kernel(
    meta, top, mid, bot, left, right, w_mid, w_out, pay, dec, slope_out, s1, s2, w, w3
):
    r, c = meta[0], meta[1]
    for dy in range(3):
        for dx in range(3):
            w[dy * 128 : (dy + 1) * 128, dx * 128 : (dx + 1) * 128] = w_mid[dy, dx]
    colour_weights(w3, lambda dy: w_out[dy])

    def fill(first, rows, centre):
        n = rows * WIDE
        parts = [left[pl.ds(first, rows)], centre, right[pl.ds(first, rows)]]
        v = jnp.concatenate([p.astype(F32) for p in parts], axis=1).reshape(n, 128)
        s1[pl.ds(aligned(first * WIDE, 16), n), :] = (v * sigmoid(v)).astype(BF)

    fill(0, FEAT_HALO, top[0:FEAT_HALO])
    fill(FEAT_HALO + TH, FEAT_HALO, bot[0:FEAT_HALO])

    def fill_mid(i, carry):
        fill(FEAT_HALO + i * 8, 8, mid[pl.ds(i * 8, 8)])
        return carry

    lax.fori_loop(0, TH // 8, fill_mid, 0, unroll=2)
    col_ok = column_mask(c * TW - COL_HALO)

    def middle(i, carry):
        v = conv_rows(s1, i * 8, 8, w[...])
        act, slope = silu_parts(v)
        act = keep_inside(act, r * TH - 12 + i * 8, 8, col_ok)
        s2[pl.ds(aligned(i * 8 * WIDE, 16), 8 * WIDE), :] = act.astype(BF)
        slope = pltpu.roll(slope, 8 * WIDE - 6, 0).reshape(8, WIDE, 128).astype(BF)
        first, last = max(i * 8, 11), min(i * 8 + 8, 79)
        if first < last:
            slope_out[first - 11 : last - 11] = slope[first - i * 8 : last - i * 8]
        return carry

    for i in range(11):
        middle(i, 0)
    s2[88 * WIDE :, :] = jnp.zeros((10 * WIDE, 128), BF)
    dec[768:, :] = jnp.zeros((256, 128), F32)

    def colours(i, carry):
        v = to_colours(s2, i * 16, w3)
        ok = planar_inside(
            r * TH - DEC_HALO + i * 16, c * TW - COL_HALO, 2, WIDE - 2, 16, 86 - i * 16
        )
        dec[pl.ds(aligned(i * 128, 128), 128), :] = jnp.where(ok, v, 0.0).astype(BF).astype(F32)
        return carry

    lax.fori_loop(0, 6, colours, 0, unroll=True)
    planes = [
        dec[pl.ds(k, 128, stride=8), :].T[COL_HALO : COL_HALO + TW, :] for k in range(3)
    ]
    upper = iota((16, 128), 1) >= 64
    for half in range(2):
        low, high = [], []
        for x in range(2):
            for p in planes:
                p = p[x * 16 : (x + 1) * 16]
                start = half * SHARE
                low.append(pltpu.roll(p, 128 - start, 1) if start else p)
                high.append(pltpu.roll(p, 64 - start, 1))
        packed = [jnp.where(upper, high[k + 1], low[k]) for k in (0, 2, 4)]
        packed = jnp.concatenate(packed, axis=1).astype(BF)
        for k in range(COLS // 2):
            pay[2 * k + half] = packed


def percept_kernel(
    meta, dec, tall, left, right, v_first, v_second, weights, feat, slope_one, done,
    planes, px, one, w1, w2,
):
    r, c = meta[0], meta[1]
    col_first = c * TW - COL_HALO
    col_ok = column_mask(col_first)

    def first_small(dy):
        v = v_first[dy]
        return v + pltpu.roll(pltpu.roll(v, 3, 0), 64, 1)

    patch_weights(w1, first_small)
    for dy in range(3):
        for dx in range(3):
            v = v_second[dy, dx].astype(F32)
            v = jnp.concatenate([v, jnp.zeros((64, 64), F32)], axis=1)
            u = pltpu.roll(v, 64, 1)
            w2[dy * 128 : (dy + 1) * 128, dx * 128 : (dx + 1) * 128] = jnp.concatenate(
                [v, u], axis=0
            ).astype(BF)

    planes[...] = jnp.zeros(planes.shape, F32)
    for k in range(3):
        v = jnp.concatenate(
            [a.astype(F32) for a in (left[90 + k], tall[k], right[90 + k])], axis=0
        )
        planes[pl.ds(3 + k, 80, stride=8), :] = taller(v).T[0:80]

    done[...] = jnp.zeros((8, 128), F32)

    def gather(i, carry):
        v = dec[pl.ds(aligned(i * 32 + 40, 8), 32), :] + planes[pl.ds(aligned(i * 32, 32), 32), :]
        px[pl.ds(aligned(i * WIDE, 16), WIDE), :] = patch_tile(v)
        return carry

    lax.fori_loop(0, 19, gather, 0, unroll=True)
    px[19 * WIDE :, :] = jnp.zeros((WIDE, 128), BF)

    def first(tile, count):
        v = from_colours(px, tile, count, w1)
        for j in range(count):
            for k in range(4):
                p = (tile + j) * 4 + k
                x = v[j * WIDE : (j + 1) * WIDE, k * 128 : (k + 1) * 128]
                act, slope = silu_parts(x)
                act = keep_inside(act, r * TH - 5 + p, 1, col_ok)
                slope_one[pl.ds(aligned(p * WIDE, 16), WIDE), :] = slope.astype(BF)
                one[pl.ds(aligned(p * WIDE, 16), WIDE), :] = act.astype(BF)

    def first_group(i, carry):
        first(i * 4, 4)
        return carry

    lax.fori_loop(0, 4, first_group, 0, unroll=True)
    first(16, 3)
    ones = ((iota((128, 128), 0) >> 6) == (iota((128, 128), 1) >> 6)).astype(F32).astype(BF)

    def half_sum(v):
        return mm(v.astype(BF), ones)

    def second(i, carry):
        v = conv_rows(one, i * 8, 8, w2[...])
        f, slope = silu_parts(v)
        scale = lax.rsqrt(half_sum(f * f) + EPSILON)
        unit = f * scale
        weighted = weights[...] * (unit - pltpu.roll(unit, 64, 1))
        g = scale * (weighted - unit * half_sum(weighted * unit)) * slope
        g = keep_inside(g, r * TH - 4 + i * 8, 8, col_ok)
        feat[pl.ds(aligned(i * 8 * WIDE, 16), 8 * WIDE), :] = g.astype(BF)
        return carry

    lax.fori_loop(0, 9, second, 0, unroll=3)


def percept_back_kernel(meta, feat, slope_one, v_first, v_second, out, bv, w3, w4):
    r, c = meta[0], meta[1]
    col_ok = column_mask(c * TW - COL_HALO)

    def last_small(dy):
        parts = [v_first[2 - dy, (2 - dx) * 8 : (3 - dx) * 8, :] for dx in range(3)]
        return jnp.concatenate(parts + [jnp.zeros((8, 128), F32)], axis=0)

    colour_weights(w4, last_small)
    for dy in range(3):
        for dx in range(3):
            v = v_second[dy, dx].astype(F32)
            v = jnp.concatenate([v, jnp.zeros((64, 64), F32)], axis=1)
            w3[(2 - dx) * 128 : (3 - dx) * 128, (2 - dy) * 128 : (3 - dy) * 128] = jnp.concatenate(
                [v, jnp.zeros((64, 128), F32)], axis=0
            ).astype(BF)

    def back(i, carry):
        v = conv_rows(feat, i * 10, 10, w3[...], transposed=True)
        x = slope_one[pl.ds(aligned((i * 10 + 2) * WIDE, 16), 10 * WIDE), :]
        v = keep_inside(v * x.astype(F32), r * TH - 3 + i * 10, 10, col_ok)
        bv[pl.ds(aligned(i * 10 * WIDE, 16), 10 * WIDE), :] = v.astype(BF)
        return carry

    lax.fori_loop(0, 7, back, 0, unroll=True)
    bv[70 * WIDE :, :] = jnp.zeros((12 * WIDE, 128), BF)

    def colours(i, carry):
        v = to_colours(bv, i * 16, w4)
        out[pl.ds(aligned(i * 128, 128), 128), :] = pltpu.roll(v, 122, 1)
        return carry

    lax.fori_loop(0, 5, colours, 0, unroll=True)


STOP = object()
FAR = 16
STEPS = 6
HALF = STEPS + 1
TILES = 2 * HALF
LANES = TILES * 128
EVEN = HALF * 128


def critic_kernel(
    meta, strip, mine, other, far, far_other, _, out,
    strip32, grads, w_pre, w_one, w_two, w_back, score, distance, row_gap, row_gap_back, x_all, x_all_b, pre, pre_b, act, act_b,
    two, two_b, cols, cols_b, jobs,
):
    r, me = meta[0], meta[1]
    first_row = r * TH - 2 + SHARE * (me & 1)
    lane = iota((1, 128), 1)
    upper = lane >= 64
    first_x = (lane & 63) == 0
    last_x = (lane & 63) == 63

    def unpack(k, carry):
        v = strip[k].astype(F32)
        b, d = pltpu.roll(v[:, 128:256], 64, 1), pltpu.roll(v[:, 256:384], 64, 1)
        at = aligned(k * TW, 32)
        strip32[pl.ds(at, 16), :] = v[:, 0:256]
        strip32[pl.ds(at + 16, 16), :] = jnp.concatenate([jnp.where(upper, d, b), d], axis=1)
        return carry

    lax.fori_loop(0, COLS, unpack, 0, unroll=8)
    strip32[IMG_W:, :] = jnp.zeros((8, 256), F32)
    grads[...] = jnp.zeros(grads.shape, F32)
    w_back[...] = jnp.zeros(w_back.shape, BF)
    for g, source in enumerate((mine, other, far, far_other)):
        w_one[g] = source[1024:1120, :]
        w_pre[g] = (0.5 * taller(source[1024:1120, :].astype(F32))).T.astype(BF)
        score[g] = taller(source[1120:1136, :].astype(F32)).T
        for i in range(4):
            first, second = (
                source[i * 256 + k * 128 : i * 256 + (k + 1) * 128, :].astype(F32).T
                for k in range(2)
            )
            at = slice((i // 2) * 128, (i // 2 + 1) * 128)
            w_two[g, i % 2, 0:128, at] = jnp.where(upper, first, second).astype(BF)
            w_two[g, i % 2, 128:256, at] = jnp.where(upper, 0.0, first).astype(BF)
            w_two[g, i % 2, 256:384, at] = jnp.where(upper, second, 0.0).astype(BF)
        for par in range(2):
            for p in range(2):
                for t in range(2):
                    i = par + 2 * t
                    for kind, j in ((0, 1 + p), (1 + p, 3 - 3 * p)):
                        w_back[
                            g,
                            (par * 2 + 1 - p) * 64 : (par * 2 + 2 - p) * 64,
                            (t * 3 + kind) * 128 : (t * 3 + kind + 1) * 128,
                        ] = 0.5 * source[i * 256 + j * 64 : i * 256 + (j + 1) * 64, :]
    for t in (two, two_b):
        t[:, 0:128] = jnp.zeros((384, 128), BF)
        t[:, (STEPS + 1) * 128 :] = jnp.zeros((384, 128), BF)
    for t in (cols, cols_b):
        t[192:, :] = jnp.zeros((64, 384), F32)
    x, n = iota((CROP + 8, 384), 0), iota((CROP + 8, 384), 1)
    wanted = 4 * (n & 63) + (n >> 6) - 1
    wanted_ok = (wanted >= 0) & (wanted < CROP)
    distance[...] = jnp.where(wanted_ok, x - wanted, -1).astype(F32)

    def gap(dims, rho, n):
        tile, i, k = rho >> 4, (rho >> 2) & 3, rho & 3
        u = 2 * jnp.where(tile >= HALF, tile - HALF, tile) + jnp.where(tile >= HALF, 1, 0)
        return jnp.where(k < 3, n - (k * 40 + 2 * u + i), -1).astype(F32)

    dims = (TILES * 16, 128)
    row_gap[...] = gap(dims, iota(dims, 0), iota(dims, 1))
    dims = (128, TILES * 16)
    row_gap_back[...] = gap(dims, iota(dims, 1), iota(dims, 0))
    wide = iota((1, 256), 1)

    def anchor(q, k):
        return meta[2 + 2 * q + k]

    def owner_of(q):
        return meta[2 + 2 * CROPS + q]

    def job(q, live, x_all, pre, act, two, cols):
        top, left, apart = anchor(q, 0), anchor(q, 1), owner_of(q) ^ me
        g = (apart & 1) + 2 * ((apart // FAR) & 1)
        y0 = first_row - top
        v0 = lax.shift_right_arithmetic(y0 - 3, 2)
        e = 4 * v0 - y0 + 6
        crop_row = y0 - 9 + (wide & 63)
        in_crop = (crop_row >= 0) & (crop_row < CROP) & (wide < 192)
        here = pl.ds(aligned((left >> 3) * 8, 8), CROP + 8)
        window = jnp.where(in_crop, strip32[here, :], 0.0).astype(BF)
        pick = jnp.where(distance[...] == (left & 7).astype(F32), 1.0, 0.0).astype(BF)
        cols_of = mm(window, pick, 0, 0)
        none = jnp.zeros((8, 384), F32)
        halves = [
            jnp.concatenate(
                [cols_of[k * 64 + 24 * h : k * 64 + 24 * h + 40, :] for k in range(3)] + [none],
                axis=0,
            )
            for h in range(2)
        ]
        mixed = []
        for m in range(6):
            tile = slice((m // 2) * 128, (m // 2 + 1) * 128)
            low, high = halves[0][:, tile], halves[1][:, tile]
            if m % 2 == 0:
                high = pltpu.roll(high, 64, 1)
            else:
                low = pltpu.roll(low, 64, 1)
            mixed.append(jnp.where(upper, high, low))
        yield
        chosen = jnp.where(row_gap[...] == e.astype(F32), 1.0, 0.0).astype(BF)
        patches = mm(chosen, jnp.concatenate(mixed, axis=1).astype(BF)).astype(BF)
        for t in range(TILES):
            for m in range(6):
                x_all[m * 16 : (m + 1) * 16, t * 128 : (t + 1) * 128] = patches[
                    t * 16 : (t + 1) * 16, m * 128 : (m + 1) * 128
                ]
        yield
        weight = w_pre[g][:, 0:96]
        for t0 in range(0, TILES, 2):
            at = slice(t0 * 128, (t0 + 2) * 128)
            value = mm(weight, x_all[:, at])
            for t in range(t0, t0 + 2):
                at = slice(t * 128, (t + 1) * 128)
                n = 2 * (t % HALF) + t // HALF + jnp.where(upper, 2 * STEPS, 0)
                u = 2 * v0 - 1 + n
                ok = ((u >= 0) & (u < CROP // 2)).astype(F32)
                half = value[:, (t - t0) * 128 : (t - t0 + 1) * 128]
                rise = jnp.tanh(half) + 1.0
                kept = rise * ok
                pre[:, at] = kept * (1.0 + half * (2.0 - rise))
                act[:, at] = (half * kept).astype(BF)
            yield
        column = score[g][:, 0:1]
        for t0 in range(0, STEPS, 2):
            value = 0.0
            for par in range(2):
                at = par * EVEN + t0 * 128
                taps = jnp.concatenate(
                    [act[:, at : at + 256], act[:, at + 128 : at + 384]], axis=0
                )
                value = value + mm(w_two[g, par], taps)
            for t in range(t0, t0 + 2):
                at = slice((t - t0) * 128, (t - t0 + 1) * 128)
                f = value[0:128, at]
                f = f + jnp.where(first_x, 0.0, pltpu.roll(value[128:256, at], 1, 1))
                f = f + jnp.where(last_x, 0.0, pltpu.roll(value[256:384, at], 127, 1))
                f, slope = silu_parts(f)
                logit = jnp.sum(f * column, axis=0, keepdims=True)
                v = v0 + t + jnp.where(upper, STEPS, 0)
                ok = (v >= 0) & (v < CROP // 4)
                grad = jnp.where(ok, -LOSS_SCALE * sigmoid(-logit), 0.0)
                b = grad * (column * slope)
                at = slice((t + 1) * 128, (t + 2) * 128)
                two[0:128, at] = b.astype(BF)
                two[128:256, at] = jnp.where(first_x, 0.0, pltpu.roll(b, 1, 1)).astype(BF)
                two[256:384, at] = jnp.where(last_x, 0.0, pltpu.roll(b, 127, 1)).astype(BF)
            yield
        for s0 in range(0, HALF, 2):
            n = min(2, HALF - s0) * 128
            at = s0 * 128
            both = jnp.concatenate([two[:, 128 + at : 128 + at + n], two[:, at : at + n]], axis=0)
            up = mm(w_back[g], both)
            for par in range(2):
                here = slice(par * EVEN + at, par * EVEN + at + n)
                one = (up[par * 128 : (par + 1) * 128] * pre[:, here]).astype(BF)
                x_all[:, here] = mm(w_one[g], one).astype(BF)
            yield
        spread = jnp.concatenate(
            [
                jnp.concatenate(
                    [
                        x_all[m * 16 : (m + 1) * 16, t * 128 : (t + 1) * 128]
                        for t in range(TILES)
                    ],
                    axis=0,
                )
                for m in range(6)
            ],
            axis=1,
        )
        chosen = jnp.where(row_gap_back[...] == e.astype(F32), 1.0, 0.0).astype(BF)
        back = mm(chosen, spread)
        yield
        parts = []
        for h in range(2):
            tiles = []
            for k in range(3):
                low = back[:, 2 * k * 128 : (2 * k + 1) * 128]
                high = back[:, (2 * k + 1) * 128 : (2 * k + 2) * 128]
                if h == 0:
                    high = pltpu.roll(high, 64, 1)
                else:
                    low = pltpu.roll(low, 64, 1)
                tiles.append(jnp.where(upper, high, low))
            parts.append(jnp.concatenate(tiles, axis=1))
        for k in range(3):
            low, high = (part[k * 40 : (k + 1) * 40, :] for part in parts)
            cols[k * 64 : (k + 1) * 64, :] = jnp.concatenate(
                [low[0:24], low[24:40] + high[0:16], high[16:40]], axis=0
            )
        yield
        placed = mm(pick, cols[...].astype(BF), 1, 1)
        y = wide & 63
        keep = in_crop & (y >= 9) & (y < 9 + SHARE) & live
        yield
        here = pl.ds(aligned((left >> 3) * 8 + GRAD_PAD, 8), CROP + 8)
        grads[here, :] = grads[here, :] + jnp.where(keep, placed, 0.0)

    count, seen, turn = jnp.int32(0), jnp.int32(0), (me // FAR) & 1
    for q in range(CROPS):
        y0 = first_row - anchor(q, 0)
        shared = ((owner_of(q) ^ me) & (COLS - 2 - FAR)) == 0
        shared = (shared & (y0 < CROP) & (y0 + SHARE > 0)).astype(jnp.int32)
        jobs[count] = q
        count = count + shared * ((seen & 1) == turn).astype(jnp.int32)
        seen = seen + shared

    def two_crops(k, carry):
        last = jnp.minimum(2 * k + 1, count - 1)
        running = [
            job(jobs[2 * k], True, x_all, pre, act, two, cols),
            job(jobs[last], 2 * k + 1 < count, x_all_b, pre_b, act_b, two_b, cols_b),
        ]
        while running:
            running = [g for g in running if next(g, STOP) is not STOP]
        return carry

    lax.fori_loop(0, (count + 1) >> 1, two_crops, 0)

    def pack(k, carry):
        block = grads[pl.ds(aligned(k * TW, 32), 48), :][GRAD_PAD - 2 : GRAD_PAD + 38]
        a, b = block[:, 0:128], block[:, 128:256]
        out[k] = jnp.where(
            lane < 40,
            pltpu.roll(a, 128 - 9, 1),
            jnp.where(lane < 80, pltpu.roll(a, 128 - 33, 1), pltpu.roll(b, 71, 1)),
        ).astype(BF)
        return carry

    lax.fori_loop(0, COLS, pack, 0, unroll=4)


def finish_kernel(
    meta, parts, lpips, slope, feats, w_mid, w_out, out, turned, planes, px, bm, w, w1
):
    r, c = meta[0], meta[1]
    for dy in range(3):
        for dx in range(3):
            w[dx * 128 : (dx + 1) * 128, dy * 128 : (dy + 1) * 128] = w_mid[2 - dy, 2 - dx]

    def small(dy):
        flipped = [w_out[2 - dy, (2 - dx) * 8 : (3 - dx) * 8, :] for dx in range(3)]
        return jnp.concatenate(flipped + [jnp.zeros((8, 128), F32)], axis=0)

    patch_weights(w1, small)
    col_ok = column_mask(c * TW - 2)
    planes[...] = jnp.zeros(planes.shape, F32)
    for half in range(2):
        total = parts[half].astype(F32)
        for k in range(1, COLS // 2):
            total = total + parts[2 * k + half].astype(F32)
        turned[...] = taller(total).T
        for k in range(3):
            planes[pl.ds(half * SHARE * 8 + k, 40, stride=8), :] = turned[k * 40 : (k + 1) * 40, :]

    def gather(i, carry):
        at = pl.ds(aligned(i * 32, 32), 32)
        ok = planar_inside(r * TH - 2 + i * 4, c * TW - 2, 0, 36, 4, 4)
        px[pl.ds(aligned(i * WIDE, 16), WIDE), :] = patch_tile(
            jnp.where(ok, lpips[at, :] + planes[at, :], 0.0)
        )
        return carry

    lax.fori_loop(0, 17, gather, 0, unroll=True)
    px[17 * WIDE :, :] = jnp.zeros((WIDE, 128), BF)

    def middle(tile, count):
        v = from_colours(px, tile, count, w1)
        for j in range(count):
            for k in range(4):
                n = (tile + j) * 4 + k
                x = v[j * WIDE : (j + 1) * WIDE, k * 128 : (k + 1) * 128]
                x = keep_inside(x * slope[n].astype(F32), r * TH - 1 + n, 1, col_ok)
                bm[pl.ds(aligned(n * WIDE, 16), WIDE), :] = x.astype(BF)

    def middle_group(i, carry):
        middle(i * 4, 4)
        return carry

    lax.fori_loop(0, 4, middle_group, 0, unroll=True)
    middle(16, 1)

    def last(i, carry):
        v = conv_rows(bm, i * 8, 8, w[...], transposed=True, shift=2)
        v = v.reshape(8, WIDE, 128)[:, 0:TW, :]
        x = feats[pl.ds(i * 8, 8)].astype(F32)
        out[pl.ds(i * 8, 8)] = (v * silu_parts(x)[1]).astype(BF)
        return carry

    lax.fori_loop(0, TH // 8, last, 0, unroll=4)


def call(kernel, outs, scratch, args, scalars=1, unused=0, lists=()):
    specs = [pl.BlockSpec(memory_space=pltpu.SMEM)] * scalars
    specs += [pl.BlockSpec(memory_space=pltpu.VMEM)] * (len(args) - scalars - unused)
    specs += [pl.BlockSpec(memory_space=pl.ANY)] * unused
    return pl.pallas_call(
        kernel,
        in_specs=specs,
        out_specs=jax.tree.map(lambda _: pl.BlockSpec(memory_space=pltpu.VMEM), outs),
        out_shape=outs,
        scratch_shapes=[pltpu.VMEM(s, t) for s, t in scratch] + list(lists),
        compiler_params=pltpu.CompilerParams(vmem_limit_bytes=VMEM),
        interpret=INTERPRET,
    )(*args)


INTERPRET = False


def shape(dims, kind):
    return jax.ShapeDtypeStruct(dims, kind)


def colour_first(w):
    w = jnp.pad(w.astype(F32), ((0, 0), (0, 1), (0, 5), (0, 128 - w.shape[-1])))
    return w.reshape(3, 32, 128)


def decode(meta, top, mid, bot, left, right, conv_mid, small):
    return call(
        decode_kernel,
        (
            shape((COLS, TW // 2, 384), BF),
            shape((1024, 128), F32),
            pltpu.HBM((68, WIDE, 128), BF),
        ),
        [((90 * WIDE, 128), BF), ((98 * WIDE, 128), BF), ((384, 384), BF), ((384, 384), BF)],
        (meta, top, mid, bot, left, right, conv_mid, small),
    )


def percept(meta, dec, tall, left, right, small, vgg_second, weights):
    scaled = jnp.pad(2.0 * LOSS_SCALE * weights, (0, 64)).reshape(1, 128)
    return call(
        percept_kernel,
        (
            pltpu.HBM((72 * WIDE, 128), BF),
            pltpu.HBM((76 * WIDE, 128), BF),
            shape((8, 128), F32),
        ),
        [
            ((80 * 8, 128), F32),
            ((20 * WIDE, 128), BF),
            ((76 * WIDE, 128), BF),
            ((256, 512), BF),
            ((384, 384), BF),
        ],
        (meta, dec, tall, left, right, small, vgg_second, scaled),
    )


def percept_back(meta, feat, slope_one, small, vgg_second):
    return call(
        percept_back_kernel,
        shape((80 * 8, 128), F32),
        [((82 * WIDE, 128), BF), ((384, 384), BF), ((384, 384), BF)],
        (meta, feat, slope_one, small, vgg_second),
    )


def critic_weights(first, second, score):
    w = jnp.pad(first, ((0, 0), (0, 0), (0, 1), (0, 0)))
    w = jnp.transpose(w, (1, 0, 2, 3)).reshape(4, 16, 64)
    w = jnp.concatenate(
        [jnp.pad(w, ((2, 0), (0, 0), (0, 0))), jnp.pad(w, ((0, 2), (0, 0), (0, 0)))], -1
    ).reshape(96, 128)
    score = jnp.pad(score[None], ((0, 15), (0, 0)))
    return jnp.concatenate([second.reshape(1024, 128), w, score], 0)


def critics(meta, strip, weights, after):
    pair = [
        ((96, LANES), BF),
        ((128, LANES), F32),
        ((128, LANES), BF),
        ((384, (STEPS + 2) * 128), BF),
        ((256, 384), F32),
    ]
    return call(
        critic_kernel,
        shape((COLS, 40, 128), BF),
        [
            ((IMG_W + 8, 256), F32),
            ((IMG_W + 24, 256), F32),
            ((4, 128, 128), BF),
            ((4, 96, 128), BF),
            ((4, 2, 384, 256), BF),
            ((4, 256, 768), BF),
            ((4, 128, 128), F32),
            ((CROP + 8, 384), F32),
            ((TILES * 16, 128), F32),
            ((128, TILES * 16), F32),
        ]
        + [buffer for buffer in pair for _ in range(2)],
        (meta, strip, *weights, after),
        unused=1,
        lists=[pltpu.SMEM((CROPS,), jnp.int32)],
    )


def finish(meta, parts, lpips, slope, feats, conv_mid, small):
    return call(
        finish_kernel,
        shape((TH, TW, 128), BF),
        [
            ((128, 128), F32),
            ((80 * 8, 128), F32),
            ((18 * WIDE, 128), BF),
            ((68 * WIDE, 128), BF),
            ((384, 384), BF),
            ((256, 512), BF),
        ],
        (meta, parts, lpips, slope, feats, conv_mid, small),
    )


def in_hbm(x):
    return pltpu.with_memory_space_constraint(x, pltpu.HBM)


def exchange(low, high, axis):
    count = lax.axis_size(axis)
    forward = [(i, i + 1) for i in range(count - 1)]
    backward = [(target, source) for source, target in forward]
    return lax.ppermute(low, axis, forward), lax.ppermute(high, axis, backward)


def local(
    features, conv_mid, conv_out, target, vgg_first, vgg_second, perceptual_weights,
    crop_anchors, crop_owner, critic_first, critic_second, critic_score,
):
    meta = jnp.concatenate(
        [
            jnp.stack([lax.axis_index("row"), lax.axis_index("col")]).astype(jnp.int32),
            crop_anchors.reshape(2 * CROPS),
            crop_owner.reshape(CROPS),
        ]
    )
    feats = features[0]
    planar = jnp.transpose(target[0], (2, 1, 0))

    def row_part(rows, colours):
        colours = jnp.transpose(colours, (1, 0, 2)).reshape(TW, 3 * TGT_HALO)
        colours = jnp.pad(colours, ((0, 0), (0, 128 - 3 * TGT_HALO)))
        return jnp.concatenate([rows, colours[None]], 0)

    top, bot = exchange(
        row_part(feats[TH - FEAT_HALO :], planar[:, :, TH - TGT_HALO :]),
        row_part(feats[:FEAT_HALO], planar[:, :, :TGT_HALO]),
        "row",
    )

    def colours_of(part):
        part = part[FEAT_HALO, :, : 3 * TGT_HALO].reshape(TW, 3, TGT_HALO)
        return jnp.transpose(part, (1, 0, 2))

    tall = jnp.concatenate(
        [
            colours_of(top),
            planar,
            colours_of(bot),
            jnp.zeros((3, TW, 128 - TH - 2 * TGT_HALO), BF),
        ],
        2,
    )

    def edge(first, last):
        parts = (top[:FEAT_HALO], feats, bot[:FEAT_HALO], tall)
        return jnp.concatenate([a[:, first:last] for a in parts], 0)

    left, right = exchange(edge(TW - COL_HALO, TW), edge(0, COL_HALO), "col")
    out_small = colour_first(jnp.transpose(conv_out, (0, 1, 3, 2)))
    vgg_small = colour_first(vgg_first)
    pay, dec, slope = decode(meta, top, feats, bot, left, right, conv_mid, out_small)
    strip = lax.all_to_all(pay, "col", split_axis=0, concat_axis=0, tiled=True)
    mine = critic_weights(critic_first[0], critic_second[0], critic_score[0])
    other = lax.ppermute(mine, "col", [(i, i ^ 1) for i in range(COLS)])
    far = lax.ppermute(mine, "col", [(i, i ^ FAR) for i in range(COLS)])
    far_other = lax.ppermute(far, "col", [(i, i ^ 1) for i in range(COLS)])
    feat, slope_one, done = percept(
        meta, dec, tall, left, right, vgg_small, vgg_second, perceptual_weights
    )
    grads = critics(meta, strip, (mine, other, far, far_other), done)
    parts = lax.all_to_all(grads, "col", split_axis=0, concat_axis=0, tiled=True)
    lpips = percept_back(meta, in_hbm(feat), in_hbm(slope_one), vgg_small, vgg_second)
    return finish(meta, parts, lpips, slope, feats, conv_mid, out_small)[None]


def solution(mesh):
    placed = (
        P(None, "row", "col", None),
        P(),
        P(),
        P(None, "row", "col", None),
        P(),
        P(),
        P(),
        P(),
        P(),
        P("col", None, None, None, None),
        P("col", None, None, None, None),
        P("col", None),
    )
    return jax.shard_map(
        local, mesh=mesh, in_specs=placed, out_specs=P(None, "row", "col", None), check_vma=False
    )
```

```python
import jax
import jax.numpy as jnp
import numpy as np
from jax import lax
from jax.experimental import pallas as pl
from jax.experimental.pallas import tpu as pltpu
from jax.sharding import PartitionSpec as P

BF = jnp.bfloat16
F32 = jnp.float32

LOSS_SCALE = 32.0
EPSILON = 1e-06
CROP = 256
TH, TW = 64, 32
IMG_H, IMG_W = 512, 1024
ROWS, COLS = 8, 32
CROPS = 64
DEC_HALO = 11
FEAT_HALO = 13
COL_HALO = 8
WIDE = TW + 2 * COL_HALO
TGT_HALO = 6
GRAD_PAD = 8
SHARE = 34
VMEM = 20 * 1024 * 1024


def sigmoid(v):
    return 0.5 * jnp.tanh(0.5 * v) + 0.5


def silu_parts(v):
    sig = sigmoid(v)
    act = v * sig
    return act, sig + act * (1.0 - sig)


def mm(a, b, ca=1, cb=0):
    return lax.dot_general(a, b, (((ca,), (cb,)), ((), ())), preferred_element_type=F32)


def iota(shape, dim):
    return lax.broadcasted_iota(jnp.int32, shape, dim)


def aligned(start, unit):
    return pl.multiple_of(start, unit) if not isinstance(start, int) else start


def conv_rows(src, row0, rows, weight, transposed=False, shift=0):
    n = rows * WIDE
    lhs = jnp.concatenate(
        [src[pl.ds(aligned((row0 + dy) * WIDE, 16), n), :] for dy in range(3)], axis=1
    )
    z = mm(lhs, weight, 1, 1 if transposed else 0)
    parts = []
    for dx in range(3):
        amount = (1 - dx - shift) % n
        part = z[:, dx * 128 : (dx + 1) * 128]
        parts.append(pltpu.roll(part, amount, 0) if amount else part)
    return parts[0] + parts[1] + parts[2]


def column_mask(col_first):
    x = col_first + iota((1, WIDE, 128), 1)
    return ((x >= 0) & (x < IMG_W)).astype(F32)


def keep_inside(v, row_first, rows, col_ok):
    y = row_first + iota((rows, 1, 128), 0)
    row_ok = ((y >= 0) & (y < IMG_H)).astype(F32)
    return (v.reshape(rows, WIDE, 128) * (col_ok * row_ok)).reshape(rows * WIDE, 128)


def planar_inside(row_first, col_first, low, high, rows, limit):
    lane = iota((rows * 8, 128), 1)
    row = iota((rows * 8, 128), 0) >> 3
    x = col_first + lane
    y = row_first + row
    ok = (x >= 0) & (x < IMG_W) & (lane >= low) & (lane < high) & (y >= 0) & (y < IMG_H)
    return ok & (row < limit)


def taller(v):
    return jnp.concatenate([v, jnp.zeros((128 - v.shape[0], 128), F32)], axis=0)


def colour_weights(w, small):
    k = iota((32, 384), 0)
    n = iota((32, 384), 1)
    copies = (((n >> 7) * 8 + (n & 7)) == k).astype(F32).astype(BF)
    for dy in range(3):
        w[dy * 128 : (dy + 1) * 128, :] = mm(small(dy).astype(BF), copies, 0, 0).astype(BF)


def to_colours(src, first, w):
    group = iota((WIDE, 128), 1) >> 3
    tile = jnp.zeros((WIDE, 128), F32)
    for half in range(2):
        v = conv_rows(src, first + half * 8, 8, w[...])
        for k in range(8):
            tile = jnp.where(group == half * 8 + k, v[k * WIDE : (k + 1) * WIDE], tile)
    return taller(tile).T


def patch_tile(v):
    after, before = pltpu.roll(v, 1, 1), pltpu.roll(v, 127, 1)
    none = jnp.zeros((8, 128), F32)
    parts = []
    for k in range(4):
        at = slice(k * 8, (k + 1) * 8)
        parts += [after[at], v[at], before[at], none]
    return jnp.concatenate(parts, axis=0).T[0:WIDE].astype(BF)


def patch_weights(w, small):
    w[...] = jnp.zeros(w.shape, BF)
    for k in range(4):
        for dy in range(3):
            w[(k + dy) * 32 : (k + dy + 1) * 32, k * 128 : (k + 1) * 128] = small(dy).astype(BF)


def from_colours(px, tile, count, w):
    at = [pl.ds(aligned((tile + k) * WIDE, 16), count * WIDE) for k in range(2)]
    return mm(jnp.concatenate([px[at[0], :], px[at[1], :]], axis=1), w[...])


def decode_kernel(
    meta, top, mid, bot, left, right, w_mid, w_out, pay, dec, slope_out, s1, s2, w, w3
):
    r, c = meta[0], meta[1]
    for dy in range(3):
        for dx in range(3):
            w[dy * 128 : (dy + 1) * 128, dx * 128 : (dx + 1) * 128] = w_mid[dy, dx]
    colour_weights(w3, lambda dy: w_out[dy])

    def fill(first, rows, centre):
        n = rows * WIDE
        parts = [left[pl.ds(first, rows)], centre, right[pl.ds(first, rows)]]
        v = jnp.concatenate([p.astype(F32) for p in parts], axis=1).reshape(n, 128)
        s1[pl.ds(aligned(first * WIDE, 16), n), :] = (v * sigmoid(v)).astype(BF)

    fill(0, FEAT_HALO, top[0:FEAT_HALO])
    fill(FEAT_HALO + TH, FEAT_HALO, bot[0:FEAT_HALO])

    def fill_mid(i, carry):
        fill(FEAT_HALO + i * 8, 8, mid[pl.ds(i * 8, 8)])
        return carry

    lax.fori_loop(0, TH // 8, fill_mid, 0, unroll=2)
    col_ok = column_mask(c * TW - COL_HALO)

    def middle(i, carry):
        v = conv_rows(s1, i * 8, 8, w[...])
        act, slope = silu_parts(v)
        act = keep_inside(act, r * TH - 12 + i * 8, 8, col_ok)
        s2[pl.ds(aligned(i * 8 * WIDE, 16), 8 * WIDE), :] = act.astype(BF)
        slope = pltpu.roll(slope, 8 * WIDE - 6, 0).reshape(8, WIDE, 128).astype(BF)
        first, last = max(i * 8, 11), min(i * 8 + 8, 79)
        if first < last:
            slope_out[first - 11 : last - 11] = slope[first - i * 8 : last - i * 8]
        return carry

    for i in range(11):
        middle(i, 0)
    s2[88 * WIDE :, :] = jnp.zeros((10 * WIDE, 128), BF)
    dec[768:, :] = jnp.zeros((256, 128), F32)

    def colours(i, carry):
        v = to_colours(s2, i * 16, w3)
        ok = planar_inside(
            r * TH - DEC_HALO + i * 16, c * TW - COL_HALO, 2, WIDE - 2, 16, 86 - i * 16
        )
        dec[pl.ds(aligned(i * 128, 128), 128), :] = jnp.where(ok, v, 0.0).astype(BF).astype(F32)
        return carry

    lax.fori_loop(0, 6, colours, 0, unroll=True)
    planes = [
        dec[pl.ds(k, 128, stride=8), :].T[COL_HALO : COL_HALO + TW, :] for k in range(3)
    ]
    upper = iota((16, 128), 1) >= 64
    for half in range(2):
        low, high = [], []
        for x in range(2):
            for p in planes:
                p = p[x * 16 : (x + 1) * 16]
                start = half * SHARE
                low.append(pltpu.roll(p, 128 - start, 1) if start else p)
                high.append(pltpu.roll(p, 64 - start, 1))
        packed = [jnp.where(upper, high[k + 1], low[k]) for k in (0, 2, 4)]
        packed = jnp.concatenate(packed, axis=1).astype(BF)
        for k in range(COLS // 2):
            pay[2 * k + half] = packed


def percept_kernel(
    meta, dec, tall, left, right, v_first, v_second, weights, feat, slope_one, done,
    planes, px, one, w1, w2,
):
    r, c = meta[0], meta[1]
    col_first = c * TW - COL_HALO
    col_ok = column_mask(col_first)

    def first_small(dy):
        v = v_first[dy]
        return v + pltpu.roll(pltpu.roll(v, 3, 0), 64, 1)

    patch_weights(w1, first_small)
    for dy in range(3):
        for dx in range(3):
            v = v_second[dy, dx].astype(F32)
            v = jnp.concatenate([v, jnp.zeros((64, 64), F32)], axis=1)
            u = pltpu.roll(v, 64, 1)
            w2[dy * 128 : (dy + 1) * 128, dx * 128 : (dx + 1) * 128] = jnp.concatenate(
                [v, u], axis=0
            ).astype(BF)

    planes[...] = jnp.zeros(planes.shape, F32)
    for k in range(3):
        v = jnp.concatenate(
            [a.astype(F32) for a in (left[90 + k], tall[k], right[90 + k])], axis=0
        )
        planes[pl.ds(3 + k, 80, stride=8), :] = taller(v).T[0:80]

    done[...] = jnp.zeros((8, 128), F32)

    def gather(i, carry):
        v = dec[pl.ds(aligned(i * 32 + 40, 8), 32), :] + planes[pl.ds(aligned(i * 32, 32), 32), :]
        px[pl.ds(aligned(i * WIDE, 16), WIDE), :] = patch_tile(v)
        return carry

    lax.fori_loop(0, 19, gather, 0, unroll=True)
    px[19 * WIDE :, :] = jnp.zeros((WIDE, 128), BF)

    def first(tile, count):
        v = from_colours(px, tile, count, w1)
        for j in range(count):
            for k in range(4):
                p = (tile + j) * 4 + k
                x = v[j * WIDE : (j + 1) * WIDE, k * 128 : (k + 1) * 128]
                act, slope = silu_parts(x)
                act = keep_inside(act, r * TH - 5 + p, 1, col_ok)
                slope_one[pl.ds(aligned(p * WIDE, 16), WIDE), :] = slope.astype(BF)
                one[pl.ds(aligned(p * WIDE, 16), WIDE), :] = act.astype(BF)

    def first_group(i, carry):
        first(i * 4, 4)
        return carry

    lax.fori_loop(0, 4, first_group, 0, unroll=True)
    first(16, 3)
    ones = ((iota((128, 128), 0) >> 6) == (iota((128, 128), 1) >> 6)).astype(F32).astype(BF)

    def half_sum(v):
        return mm(v.astype(BF), ones)

    def second(i, carry):
        v = conv_rows(one, i * 8, 8, w2[...])
        f, slope = silu_parts(v)
        scale = lax.rsqrt(half_sum(f * f) + EPSILON)
        unit = f * scale
        weighted = weights[...] * (unit - pltpu.roll(unit, 64, 1))
        g = scale * (weighted - unit * half_sum(weighted * unit)) * slope
        g = keep_inside(g, r * TH - 4 + i * 8, 8, col_ok)
        feat[pl.ds(aligned(i * 8 * WIDE, 16), 8 * WIDE), :] = g.astype(BF)
        return carry

    lax.fori_loop(0, 9, second, 0, unroll=3)


def percept_back_kernel(meta, feat, slope_one, v_first, v_second, out, bv, w3, w4):
    r, c = meta[0], meta[1]
    col_ok = column_mask(c * TW - COL_HALO)

    def last_small(dy):
        parts = [v_first[2 - dy, (2 - dx) * 8 : (3 - dx) * 8, :] for dx in range(3)]
        return jnp.concatenate(parts + [jnp.zeros((8, 128), F32)], axis=0)

    colour_weights(w4, last_small)
    for dy in range(3):
        for dx in range(3):
            v = v_second[dy, dx].astype(F32)
            v = jnp.concatenate([v, jnp.zeros((64, 64), F32)], axis=1)
            w3[(2 - dx) * 128 : (3 - dx) * 128, (2 - dy) * 128 : (3 - dy) * 128] = jnp.concatenate(
                [v, jnp.zeros((64, 128), F32)], axis=0
            ).astype(BF)

    def back(i, carry):
        v = conv_rows(feat, i * 10, 10, w3[...], transposed=True)
        x = slope_one[pl.ds(aligned((i * 10 + 2) * WIDE, 16), 10 * WIDE), :]
        v = keep_inside(v * x.astype(F32), r * TH - 3 + i * 10, 10, col_ok)
        bv[pl.ds(aligned(i * 10 * WIDE, 16), 10 * WIDE), :] = v.astype(BF)
        return carry

    lax.fori_loop(0, 7, back, 0, unroll=True)
    bv[70 * WIDE :, :] = jnp.zeros((12 * WIDE, 128), BF)

    def colours(i, carry):
        v = to_colours(bv, i * 16, w4)
        out[pl.ds(aligned(i * 128, 128), 128), :] = pltpu.roll(v, 122, 1)
        return carry

    lax.fori_loop(0, 5, colours, 0, unroll=True)


STOP = object()
FAR = 16
STEPS = 6
HALF = STEPS + 1
TILES = 2 * HALF
LANES = TILES * 128
EVEN = HALF * 128


def critic_kernel(
    meta, strip, mine, other, far, far_other, _, out,
    strip32, grads, w_pre, w_one, w_two, w_back, score, distance, row_gap, row_gap_back, x_all, x_all_b, pre, pre_b, act, act_b,
    two, two_b, cols, cols_b, jobs,
):
    r, me = meta[0], meta[1]
    first_row = r * TH - 2 + SHARE * (me & 1)
    lane = iota((1, 128), 1)
    upper = lane >= 64
    first_x = (lane & 63) == 0
    last_x = (lane & 63) == 63

    def unpack(k, carry):
        v = strip[k].astype(F32)
        b, d = pltpu.roll(v[:, 128:256], 64, 1), pltpu.roll(v[:, 256:384], 64, 1)
        at = aligned(k * TW, 32)
        strip32[pl.ds(at, 16), :] = v[:, 0:256]
        strip32[pl.ds(at + 16, 16), :] = jnp.concatenate([jnp.where(upper, d, b), d], axis=1)
        return carry

    lax.fori_loop(0, COLS, unpack, 0, unroll=8)
    strip32[IMG_W:, :] = jnp.zeros((8, 256), F32)
    grads[...] = jnp.zeros(grads.shape, F32)
    w_back[...] = jnp.zeros(w_back.shape, BF)
    for g, source in enumerate((mine, other, far, far_other)):
        w_one[g] = source[1024:1120, :]
        w_pre[g] = (0.5 * taller(source[1024:1120, :].astype(F32))).T.astype(BF)
        score[g] = taller(source[1120:1136, :].astype(F32)).T
        for i in range(4):
            first, second = (
                source[i * 256 + k * 128 : i * 256 + (k + 1) * 128, :].astype(F32).T
                for k in range(2)
            )
            at = slice((i // 2) * 128, (i // 2 + 1) * 128)
            w_two[g, i % 2, 0:128, at] = jnp.where(upper, first, second).astype(BF)
            w_two[g, i % 2, 128:256, at] = jnp.where(upper, 0.0, first).astype(BF)
            w_two[g, i % 2, 256:384, at] = jnp.where(upper, second, 0.0).astype(BF)
        for par in range(2):
            for p in range(2):
                for t in range(2):
                    i = par + 2 * t
                    for kind, j in ((0, 1 + p), (1 + p, 3 - 3 * p)):
                        w_back[
                            g,
                            (par * 2 + 1 - p) * 64 : (par * 2 + 2 - p) * 64,
                            (t * 3 + kind) * 128 : (t * 3 + kind + 1) * 128,
                        ] = 0.5 * source[i * 256 + j * 64 : i * 256 + (j + 1) * 64, :]
    for t in (two, two_b):
        t[:, 0:128] = jnp.zeros((384, 128), BF)
        t[:, (STEPS + 1) * 128 :] = jnp.zeros((384, 128), BF)
    for t in (cols, cols_b):
        t[192:, :] = jnp.zeros((64, 384), F32)
    x, n = iota((CROP + 8, 384), 0), iota((CROP + 8, 384), 1)
    wanted = 4 * (n & 63) + (n >> 6) - 1
    wanted_ok = (wanted >= 0) & (wanted < CROP)
    distance[...] = jnp.where(wanted_ok, x - wanted, -1).astype(F32)

    def gap(dims, rho, n):
        tile, i, k = rho >> 4, (rho >> 2) & 3, rho & 3
        u = 2 * jnp.where(tile >= HALF, tile - HALF, tile) + jnp.where(tile >= HALF, 1, 0)
        return jnp.where(k < 3, n - (k * 40 + 2 * u + i), -1).astype(F32)

    dims = (TILES * 16, 128)
    row_gap[...] = gap(dims, iota(dims, 0), iota(dims, 1))
    dims = (128, TILES * 16)
    row_gap_back[...] = gap(dims, iota(dims, 1), iota(dims, 0))
    wide = iota((1, 256), 1)

    def anchor(q, k):
        return meta[2 + 2 * q + k]

    def owner_of(q):
        return meta[2 + 2 * CROPS + q]

    def job(q, x_all, pre, act, two, cols):
        top, left, apart = anchor(q, 0), anchor(q, 1), owner_of(q) ^ me
        g = (apart & 1) + 2 * ((apart // FAR) & 1)
        y0 = first_row - top
        v0 = lax.shift_right_arithmetic(y0 - 3, 2)
        e = 4 * v0 - y0 + 6
        crop_row = y0 - 9 + (wide & 63)
        in_crop = (crop_row >= 0) & (crop_row < CROP) & (wide < 192)
        here = pl.ds(aligned((left >> 3) * 8, 8), CROP + 8)
        window = jnp.where(in_crop, strip32[here, :], 0.0).astype(BF)
        pick = jnp.where(distance[...] == (left & 7).astype(F32), 1.0, 0.0).astype(BF)
        cols_of = mm(window, pick, 0, 0)
        none = jnp.zeros((8, 384), F32)
        halves = [
            jnp.concatenate(
                [cols_of[k * 64 + 24 * h : k * 64 + 24 * h + 40, :] for k in range(3)] + [none],
                axis=0,
            )
            for h in range(2)
        ]
        mixed = []
        for m in range(6):
            tile = slice((m // 2) * 128, (m // 2 + 1) * 128)
            low, high = halves[0][:, tile], halves[1][:, tile]
            if m % 2 == 0:
                high = pltpu.roll(high, 64, 1)
            else:
                low = pltpu.roll(low, 64, 1)
            mixed.append(jnp.where(upper, high, low))
        yield
        chosen = jnp.where(row_gap[...] == e.astype(F32), 1.0, 0.0).astype(BF)
        patches = mm(chosen, jnp.concatenate(mixed, axis=1).astype(BF)).astype(BF)
        for t in range(TILES):
            for m in range(6):
                x_all[m * 16 : (m + 1) * 16, t * 128 : (t + 1) * 128] = patches[
                    t * 16 : (t + 1) * 16, m * 128 : (m + 1) * 128
                ]
        yield
        weight = w_pre[g][:, 0:96]
        for t0 in range(0, TILES, 2):
            at = slice(t0 * 128, (t0 + 2) * 128)
            value = mm(weight, x_all[:, at])
            for t in range(t0, t0 + 2):
                at = slice(t * 128, (t + 1) * 128)
                n = 2 * (t % HALF) + t // HALF + jnp.where(upper, 2 * STEPS, 0)
                u = 2 * v0 - 1 + n
                ok = ((u >= 0) & (u < CROP // 2)).astype(F32)
                half = value[:, (t - t0) * 128 : (t - t0 + 1) * 128]
                rise = jnp.tanh(half) + 1.0
                kept = rise * ok
                pre[:, at] = kept * (1.0 + half * (2.0 - rise))
                act[:, at] = (half * kept).astype(BF)
            yield
        column = score[g][:, 0:1]
        for t0 in range(0, STEPS, 2):
            value = 0.0
            for par in range(2):
                at = par * EVEN + t0 * 128
                taps = jnp.concatenate(
                    [act[:, at : at + 256], act[:, at + 128 : at + 384]], axis=0
                )
                value = value + mm(w_two[g, par], taps)
            for t in range(t0, t0 + 2):
                at = slice((t - t0) * 128, (t - t0 + 1) * 128)
                f = value[0:128, at]
                f = f + jnp.where(first_x, 0.0, pltpu.roll(value[128:256, at], 1, 1))
                f = f + jnp.where(last_x, 0.0, pltpu.roll(value[256:384, at], 127, 1))
                f, slope = silu_parts(f)
                logit = jnp.sum(f * column, axis=0, keepdims=True)
                v = v0 + t + jnp.where(upper, STEPS, 0)
                ok = (v >= 0) & (v < CROP // 4)
                grad = jnp.where(ok, -LOSS_SCALE * sigmoid(-logit), 0.0)
                b = grad * (column * slope)
                at = slice((t + 1) * 128, (t + 2) * 128)
                two[0:128, at] = b.astype(BF)
                two[128:256, at] = jnp.where(first_x, 0.0, pltpu.roll(b, 1, 1)).astype(BF)
                two[256:384, at] = jnp.where(last_x, 0.0, pltpu.roll(b, 127, 1)).astype(BF)
            yield
        for s0 in range(0, HALF, 2):
            n = min(2, HALF - s0) * 128
            at = s0 * 128
            both = jnp.concatenate([two[:, 128 + at : 128 + at + n], two[:, at : at + n]], axis=0)
            up = mm(w_back[g], both)
            for par in range(2):
                here = slice(par * EVEN + at, par * EVEN + at + n)
                one = (up[par * 128 : (par + 1) * 128] * pre[:, here]).astype(BF)
                x_all[:, here] = mm(w_one[g], one).astype(BF)
            yield
        spread = jnp.concatenate(
            [
                jnp.concatenate(
                    [
                        x_all[m * 16 : (m + 1) * 16, t * 128 : (t + 1) * 128]
                        for t in range(TILES)
                    ],
                    axis=0,
                )
                for m in range(6)
            ],
            axis=1,
        )
        chosen = jnp.where(row_gap_back[...] == e.astype(F32), 1.0, 0.0).astype(BF)
        back = mm(chosen, spread)
        yield
        parts = []
        for h in range(2):
            tiles = []
            for k in range(3):
                low = back[:, 2 * k * 128 : (2 * k + 1) * 128]
                high = back[:, (2 * k + 1) * 128 : (2 * k + 2) * 128]
                if h == 0:
                    high = pltpu.roll(high, 64, 1)
                else:
                    low = pltpu.roll(low, 64, 1)
                tiles.append(jnp.where(upper, high, low))
            parts.append(jnp.concatenate(tiles, axis=1))
        for k in range(3):
            low, high = (part[k * 40 : (k + 1) * 40, :] for part in parts)
            cols[k * 64 : (k + 1) * 64, :] = jnp.concatenate(
                [low[0:24], low[24:40] + high[0:16], high[16:40]], axis=0
            )
        yield
        placed = mm(pick, cols[...].astype(BF), 1, 1)
        y = wide & 63
        keep = in_crop & (y >= 9) & (y < 9 + SHARE)
        yield
        here = pl.ds(aligned((left >> 3) * 8 + GRAD_PAD, 8), CROP + 8)
        grads[here, :] = grads[here, :] + jnp.where(keep, placed, 0.0)

    count, seen, turn = jnp.int32(0), jnp.int32(0), (me // FAR) & 1
    for q in range(CROPS):
        y0 = first_row - anchor(q, 0)
        shared = ((owner_of(q) ^ me) & (COLS - 2 - FAR)) == 0
        shared = (shared & (y0 < CROP) & (y0 + SHARE > 0)).astype(jnp.int32)
        jobs[count] = q
        count = count + shared * ((seen & 1) == turn).astype(jnp.int32)
        seen = seen + shared

    first_set, second_set = (x_all, pre, act, two, cols), (x_all_b, pre_b, act_b, two_b, cols_b)

    def two_crops(k, carry):
        running = [job(jobs[2 * k], *first_set), job(jobs[2 * k + 1], *second_set)]
        while running:
            running = [g for g in running if next(g, STOP) is not STOP]
        return carry

    lax.fori_loop(0, count >> 1, two_crops, 0)

    @pl.when((count & 1) == 1)
    def _():
        for _ in job(jobs[count - 1], *first_set):
            pass

    def pack(k, carry):
        block = grads[pl.ds(aligned(k * TW, 32), 48), :][GRAD_PAD - 2 : GRAD_PAD + 38]
        a, b = block[:, 0:128], block[:, 128:256]
        out[k] = jnp.where(
            lane < 40,
            pltpu.roll(a, 128 - 9, 1),
            jnp.where(lane < 80, pltpu.roll(a, 128 - 33, 1), pltpu.roll(b, 71, 1)),
        ).astype(BF)
        return carry

    lax.fori_loop(0, COLS, pack, 0, unroll=4)


def finish_kernel(
    meta, parts, lpips, slope, feats, w_mid, w_out, out, turned, planes, px, bm, w, w1
):
    r, c = meta[0], meta[1]
    for dy in range(3):
        for dx in range(3):
            w[dx * 128 : (dx + 1) * 128, dy * 128 : (dy + 1) * 128] = w_mid[2 - dy, 2 - dx]

    def small(dy):
        flipped = [w_out[2 - dy, (2 - dx) * 8 : (3 - dx) * 8, :] for dx in range(3)]
        return jnp.concatenate(flipped + [jnp.zeros((8, 128), F32)], axis=0)

    patch_weights(w1, small)
    col_ok = column_mask(c * TW - 2)
    planes[...] = jnp.zeros(planes.shape, F32)
    for half in range(2):
        total = parts[half].astype(F32)
        for k in range(1, COLS // 2):
            total = total + parts[2 * k + half].astype(F32)
        turned[...] = taller(total).T
        for k in range(3):
            planes[pl.ds(half * SHARE * 8 + k, 40, stride=8), :] = turned[k * 40 : (k + 1) * 40, :]

    def gather(i, carry):
        at = pl.ds(aligned(i * 32, 32), 32)
        ok = planar_inside(r * TH - 2 + i * 4, c * TW - 2, 0, 36, 4, 4)
        px[pl.ds(aligned(i * WIDE, 16), WIDE), :] = patch_tile(
            jnp.where(ok, lpips[at, :] + planes[at, :], 0.0)
        )
        return carry

    lax.fori_loop(0, 17, gather, 0, unroll=True)
    px[17 * WIDE :, :] = jnp.zeros((WIDE, 128), BF)

    def middle(tile, count):
        v = from_colours(px, tile, count, w1)
        for j in range(count):
            for k in range(4):
                n = (tile + j) * 4 + k
                x = v[j * WIDE : (j + 1) * WIDE, k * 128 : (k + 1) * 128]
                x = keep_inside(x * slope[n].astype(F32), r * TH - 1 + n, 1, col_ok)
                bm[pl.ds(aligned(n * WIDE, 16), WIDE), :] = x.astype(BF)

    def middle_group(i, carry):
        middle(i * 4, 4)
        return carry

    lax.fori_loop(0, 4, middle_group, 0, unroll=True)
    middle(16, 1)

    def last(i, carry):
        v = conv_rows(bm, i * 8, 8, w[...], transposed=True, shift=2)
        v = v.reshape(8, WIDE, 128)[:, 0:TW, :]
        x = feats[pl.ds(i * 8, 8)].astype(F32)
        out[pl.ds(i * 8, 8)] = (v * silu_parts(x)[1]).astype(BF)
        return carry

    lax.fori_loop(0, TH // 8, last, 0, unroll=4)


def call(kernel, outs, scratch, args, scalars=1, unused=0, lists=()):
    specs = [pl.BlockSpec(memory_space=pltpu.SMEM)] * scalars
    specs += [pl.BlockSpec(memory_space=pltpu.VMEM)] * (len(args) - scalars - unused)
    specs += [pl.BlockSpec(memory_space=pl.ANY)] * unused
    return pl.pallas_call(
        kernel,
        in_specs=specs,
        out_specs=jax.tree.map(lambda _: pl.BlockSpec(memory_space=pltpu.VMEM), outs),
        out_shape=outs,
        scratch_shapes=[pltpu.VMEM(s, t) for s, t in scratch] + list(lists),
        compiler_params=pltpu.CompilerParams(vmem_limit_bytes=VMEM),
        interpret=INTERPRET,
    )(*args)


INTERPRET = False


def shape(dims, kind):
    return jax.ShapeDtypeStruct(dims, kind)


def colour_first(w):
    w = jnp.pad(w.astype(F32), ((0, 0), (0, 1), (0, 5), (0, 128 - w.shape[-1])))
    return w.reshape(3, 32, 128)


def decode(meta, top, mid, bot, left, right, conv_mid, small):
    return call(
        decode_kernel,
        (
            shape((COLS, TW // 2, 384), BF),
            shape((1024, 128), F32),
            pltpu.HBM((68, WIDE, 128), BF),
        ),
        [((90 * WIDE, 128), BF), ((98 * WIDE, 128), BF), ((384, 384), BF), ((384, 384), BF)],
        (meta, top, mid, bot, left, right, conv_mid, small),
    )


def percept(meta, dec, tall, left, right, small, vgg_second, weights):
    scaled = jnp.pad(2.0 * LOSS_SCALE * weights, (0, 64)).reshape(1, 128)
    return call(
        percept_kernel,
        (
            pltpu.HBM((72 * WIDE, 128), BF),
            pltpu.HBM((76 * WIDE, 128), BF),
            shape((8, 128), F32),
        ),
        [
            ((80 * 8, 128), F32),
            ((20 * WIDE, 128), BF),
            ((76 * WIDE, 128), BF),
            ((256, 512), BF),
            ((384, 384), BF),
        ],
        (meta, dec, tall, left, right, small, vgg_second, scaled),
    )


def percept_back(meta, feat, slope_one, small, vgg_second):
    return call(
        percept_back_kernel,
        shape((80 * 8, 128), F32),
        [((82 * WIDE, 128), BF), ((384, 384), BF), ((384, 384), BF)],
        (meta, feat, slope_one, small, vgg_second),
    )


def critic_weights(first, second, score):
    w = jnp.pad(first, ((0, 0), (0, 0), (0, 1), (0, 0)))
    w = jnp.transpose(w, (1, 0, 2, 3)).reshape(4, 16, 64)
    w = jnp.concatenate(
        [jnp.pad(w, ((2, 0), (0, 0), (0, 0))), jnp.pad(w, ((0, 2), (0, 0), (0, 0)))], -1
    ).reshape(96, 128)
    score = jnp.pad(score[None], ((0, 15), (0, 0)))
    return jnp.concatenate([second.reshape(1024, 128), w, score], 0)


def critics(meta, strip, weights, after):
    pair = [
        ((96, LANES), BF),
        ((128, LANES), F32),
        ((128, LANES), BF),
        ((384, (STEPS + 2) * 128), BF),
        ((256, 384), F32),
    ]
    return call(
        critic_kernel,
        shape((COLS, 40, 128), BF),
        [
            ((IMG_W + 8, 256), F32),
            ((IMG_W + 24, 256), F32),
            ((4, 128, 128), BF),
            ((4, 96, 128), BF),
            ((4, 2, 384, 256), BF),
            ((4, 256, 768), BF),
            ((4, 128, 128), F32),
            ((CROP + 8, 384), F32),
            ((TILES * 16, 128), F32),
            ((128, TILES * 16), F32),
        ]
        + [buffer for buffer in pair for _ in range(2)],
        (meta, strip, *weights, after),
        unused=1,
        lists=[pltpu.SMEM((CROPS,), jnp.int32)],
    )


def finish(meta, parts, lpips, slope, feats, conv_mid, small):
    return call(
        finish_kernel,
        shape((TH, TW, 128), BF),
        [
            ((128, 128), F32),
            ((80 * 8, 128), F32),
            ((18 * WIDE, 128), BF),
            ((68 * WIDE, 128), BF),
            ((384, 384), BF),
            ((256, 512), BF),
        ],
        (meta, parts, lpips, slope, feats, conv_mid, small),
    )


def in_hbm(x):
    return pltpu.with_memory_space_constraint(x, pltpu.HBM)


def exchange(low, high, axis):
    count = lax.axis_size(axis)
    forward = [(i, i + 1) for i in range(count - 1)]
    backward = [(target, source) for source, target in forward]
    return lax.ppermute(low, axis, forward), lax.ppermute(high, axis, backward)


def local(
    features, conv_mid, conv_out, target, vgg_first, vgg_second, perceptual_weights,
    crop_anchors, crop_owner, critic_first, critic_second, critic_score,
):
    meta = jnp.concatenate(
        [
            jnp.stack([lax.axis_index("row"), lax.axis_index("col")]).astype(jnp.int32),
            crop_anchors.reshape(2 * CROPS),
            crop_owner.reshape(CROPS),
        ]
    )
    feats = features[0]
    planar = jnp.transpose(target[0], (2, 1, 0))

    def row_part(rows, colours):
        colours = jnp.transpose(colours, (1, 0, 2)).reshape(TW, 3 * TGT_HALO)
        colours = jnp.pad(colours, ((0, 0), (0, 128 - 3 * TGT_HALO)))
        return jnp.concatenate([rows, colours[None]], 0)

    top, bot = exchange(
        row_part(feats[TH - FEAT_HALO :], planar[:, :, TH - TGT_HALO :]),
        row_part(feats[:FEAT_HALO], planar[:, :, :TGT_HALO]),
        "row",
    )

    def colours_of(part):
        part = part[FEAT_HALO, :, : 3 * TGT_HALO].reshape(TW, 3, TGT_HALO)
        return jnp.transpose(part, (1, 0, 2))

    tall = jnp.concatenate(
        [
            colours_of(top),
            planar,
            colours_of(bot),
            jnp.zeros((3, TW, 128 - TH - 2 * TGT_HALO), BF),
        ],
        2,
    )

    def edge(first, last):
        parts = (top[:FEAT_HALO], feats, bot[:FEAT_HALO], tall)
        return jnp.concatenate([a[:, first:last] for a in parts], 0)

    left, right = exchange(edge(TW - COL_HALO, TW), edge(0, COL_HALO), "col")
    out_small = colour_first(jnp.transpose(conv_out, (0, 1, 3, 2)))
    vgg_small = colour_first(vgg_first)
    mine = critic_weights(critic_first[0], critic_second[0], critic_score[0])
    left, right, sent = lax.optimization_barrier((left, right, mine))
    far = lax.ppermute(sent, "col", [(i, i ^ FAR) for i in range(COLS)])
    pay, dec, slope = decode(meta, top, feats, bot, left, right, conv_mid, out_small)
    pay, far = lax.optimization_barrier((pay, far))
    strip = lax.all_to_all(pay, "col", split_axis=0, concat_axis=0, tiled=True)
    other = lax.ppermute(mine, "col", [(i, i ^ 1) for i in range(COLS)])
    far_other = lax.ppermute(far, "col", [(i, i ^ 1) for i in range(COLS)])
    feat, slope_one, done = percept(
        meta, dec, tall, left, right, vgg_small, vgg_second, perceptual_weights
    )
    grads = critics(meta, strip, (mine, other, far, far_other), done)
    parts = lax.all_to_all(grads, "col", split_axis=0, concat_axis=0, tiled=True)
    lpips = percept_back(meta, in_hbm(feat), in_hbm(slope_one), vgg_small, vgg_second)
    return finish(meta, parts, lpips, slope, feats, conv_mid, out_small)[None]


def solution(mesh):
    placed = (
        P(None, "row", "col", None),
        P(),
        P(),
        P(None, "row", "col", None),
        P(),
        P(),
        P(),
        P(),
        P(),
        P("col", None, None, None, None),
        P("col", None, None, None, None),
        P("col", None),
    )
    return jax.shard_map(
        local, mesh=mesh, in_specs=placed, out_specs=P(None, "row", "col", None), check_vma=False
    )
```

```python
import jax
import jax.numpy as jnp
import numpy as np
from jax import lax
from jax.experimental import pallas as pl
from jax.experimental.pallas import tpu as pltpu
from jax.sharding import PartitionSpec as P

BF = jnp.bfloat16
F32 = jnp.float32

LOSS_SCALE = 32.0
EPSILON = 1e-06
CROP = 256
TH, TW = 64, 32
IMG_H, IMG_W = 512, 1024
ROWS, COLS = 8, 32
CROPS = 64
DEC_HALO = 11
FEAT_HALO = 13
COL_HALO = 8
WIDE = TW + 2 * COL_HALO
TGT_HALO = 6
GRAD_PAD = 8
SHARE = 34
VMEM = 20 * 1024 * 1024


def sigmoid(v):
    return 0.5 * jnp.tanh(0.5 * v) + 0.5


def silu_parts(v):
    sig = sigmoid(v)
    act = v * sig
    return act, sig + act * (1.0 - sig)


def mm(a, b, ca=1, cb=0):
    return lax.dot_general(a, b, (((ca,), (cb,)), ((), ())), preferred_element_type=F32)


def iota(shape, dim):
    return lax.broadcasted_iota(jnp.int32, shape, dim)


def aligned(start, unit):
    return pl.multiple_of(start, unit) if not isinstance(start, int) else start


def conv_rows(src, row0, rows, weight, transposed=False, shift=0):
    n = rows * WIDE
    lhs = jnp.concatenate(
        [src[pl.ds(aligned((row0 + dy) * WIDE, 16), n), :] for dy in range(3)], axis=1
    )
    z = mm(lhs, weight, 1, 1 if transposed else 0)
    parts = []
    for dx in range(3):
        amount = (1 - dx - shift) % n
        part = z[:, dx * 128 : (dx + 1) * 128]
        parts.append(pltpu.roll(part, amount, 0) if amount else part)
    return parts[0] + parts[1] + parts[2]


def column_mask(col_first):
    x = col_first + iota((1, WIDE, 128), 1)
    return ((x >= 0) & (x < IMG_W)).astype(F32)


def keep_inside(v, row_first, rows, col_ok):
    y = row_first + iota((rows, 1, 128), 0)
    row_ok = ((y >= 0) & (y < IMG_H)).astype(F32)
    return (v.reshape(rows, WIDE, 128) * (col_ok * row_ok)).reshape(rows * WIDE, 128)


def planar_inside(row_first, col_first, low, high, rows, limit):
    lane = iota((rows * 8, 128), 1)
    row = iota((rows * 8, 128), 0) >> 3
    x = col_first + lane
    y = row_first + row
    ok = (x >= 0) & (x < IMG_W) & (lane >= low) & (lane < high) & (y >= 0) & (y < IMG_H)
    return ok & (row < limit)


def wider(v):
    return jnp.concatenate([v, jnp.zeros((v.shape[0], 128 - v.shape[1]), F32)], axis=1)


def taller(v):
    return jnp.concatenate([v, jnp.zeros((128 - v.shape[0], 128), F32)], axis=0)


def colour_weights(w, small):
    k = iota((32, 384), 0)
    n = iota((32, 384), 1)
    copies = (((n >> 7) * 8 + (n & 7)) == k).astype(F32).astype(BF)
    for dy in range(3):
        w[dy * 128 : (dy + 1) * 128, :] = mm(small(dy).astype(BF), copies, 0, 0).astype(BF)


def to_colours(src, first, w):
    group = iota((WIDE, 128), 1) >> 3
    tile = jnp.zeros((WIDE, 128), F32)
    for half in range(2):
        v = conv_rows(src, first + half * 8, 8, w[...])
        for k in range(8):
            tile = jnp.where(group == half * 8 + k, v[k * WIDE : (k + 1) * WIDE], tile)
    return taller(tile).T


def patch_tile(v):
    after, before = pltpu.roll(v, 1, 1), pltpu.roll(v, 127, 1)
    none = jnp.zeros((8, 128), F32)
    parts = []
    for k in range(4):
        at = slice(k * 8, (k + 1) * 8)
        parts += [after[at], v[at], before[at], none]
    return jnp.concatenate(parts, axis=0).T[0:WIDE].astype(BF)


def patch_weights(w, small):
    w[...] = jnp.zeros(w.shape, BF)
    for k in range(4):
        for dy in range(3):
            w[(k + dy) * 32 : (k + dy + 1) * 32, k * 128 : (k + 1) * 128] = small(dy).astype(BF)


def from_colours(px, tile, count, w):
    at = [pl.ds(aligned((tile + k) * WIDE, 16), count * WIDE) for k in range(2)]
    return mm(jnp.concatenate([px[at[0], :], px[at[1], :]], axis=1), w[...])


def pack_rows_kernel(feats, target, low, high, own):
    lane = iota((TW, 128), 1)
    n = TGT_HALO
    colours = [wider(target[k].astype(F32)) for k in range(3)]
    for k in range(3):
        own[k] = colours[k].astype(BF)
    for out, y0, t0 in ((low, TH - FEAT_HALO, TH - n), (high, 0, 0)):
        extra = jnp.zeros((TW, 128), F32)
        for k in range(3):
            amount = (n * k - t0) % 128
            moved = pltpu.roll(colours[k], amount, 1) if amount else colours[k]
            extra = jnp.where((lane >= n * k) & (lane < n * k + n), moved, extra)
        out[0:FEAT_HALO] = feats[y0 : y0 + FEAT_HALO]
        out[FEAT_HALO] = extra.astype(BF)


def pack_sides_kernel(feats, own, top, bot, side_l, side_r, tall):
    lane = iota((TW, 128), 1)
    n = TGT_HALO
    above, below = top[FEAT_HALO].astype(F32), bot[FEAT_HALO].astype(F32)
    colours = []
    for k in range(3):
        first = pltpu.roll(above, 128 - n * k, 1) if k else above
        last = pltpu.roll(below, n + TH - n * k, 1)
        v = jnp.where(lane < n, first, pltpu.roll(own[k].astype(F32), n, 1))
        v = jnp.where(lane < n + TH, v, jnp.where(lane < 2 * n + TH, last, 0.0))
        tall[k] = v.astype(BF)
        colours.append(v)
    parts = (
        (0, top[0:FEAT_HALO]),
        (FEAT_HALO, feats[...]),
        (FEAT_HALO + TH, bot[0:FEAT_HALO]),
        (2 * FEAT_HALO + TH, jnp.stack(colours)),
    )
    for y, v in parts:
        v = v.astype(F32)
        for out, x0 in ((side_l, TW - COL_HALO), (side_r, 0)):
            out[y : y + v.shape[0]] = v[:, x0 : x0 + COL_HALO, :].astype(BF)


def decode_kernel(
    meta, top, mid, bot, left, right, w_mid, w_out, pay, dec, slope_out, s1, s2, w, w3
):
    r, c = meta[0], meta[1]
    for dy in range(3):
        for dx in range(3):
            w[dy * 128 : (dy + 1) * 128, dx * 128 : (dx + 1) * 128] = w_mid[dy, dx]
    colour_weights(w3, lambda dy: w_out[dy])

    def fill(first, rows, centre):
        n = rows * WIDE
        parts = [left[pl.ds(first, rows)], centre, right[pl.ds(first, rows)]]
        v = jnp.concatenate([p.astype(F32) for p in parts], axis=1).reshape(n, 128)
        s1[pl.ds(aligned(first * WIDE, 16), n), :] = (v * sigmoid(v)).astype(BF)

    fill(0, FEAT_HALO, top[0:FEAT_HALO])
    fill(FEAT_HALO + TH, FEAT_HALO, bot[0:FEAT_HALO])

    def fill_mid(i, carry):
        fill(FEAT_HALO + i * 8, 8, mid[pl.ds(i * 8, 8)])
        return carry

    lax.fori_loop(0, TH // 8, fill_mid, 0, unroll=2)
    col_ok = column_mask(c * TW - COL_HALO)

    def middle(i, carry):
        v = conv_rows(s1, i * 8, 8, w[...])
        act, slope = silu_parts(v)
        act = keep_inside(act, r * TH - 12 + i * 8, 8, col_ok)
        s2[pl.ds(aligned(i * 8 * WIDE, 16), 8 * WIDE), :] = act.astype(BF)
        slope = pltpu.roll(slope, 8 * WIDE - 6, 0).reshape(8, WIDE, 128).astype(BF)
        first, last = max(i * 8, 11), min(i * 8 + 8, 79)
        if first < last:
            slope_out[first - 11 : last - 11] = slope[first - i * 8 : last - i * 8]
        return carry

    for i in range(11):
        middle(i, 0)
    s2[88 * WIDE :, :] = jnp.zeros((10 * WIDE, 128), BF)
    dec[768:, :] = jnp.zeros((256, 128), F32)

    def colours(i, carry):
        v = to_colours(s2, i * 16, w3)
        ok = planar_inside(
            r * TH - DEC_HALO + i * 16, c * TW - COL_HALO, 2, WIDE - 2, 16, 86 - i * 16
        )
        dec[pl.ds(aligned(i * 128, 128), 128), :] = jnp.where(ok, v, 0.0).astype(BF).astype(F32)
        return carry

    lax.fori_loop(0, 6, colours, 0, unroll=True)
    planes = [
        dec[pl.ds(k, 128, stride=8), :].T[COL_HALO : COL_HALO + TW, :] for k in range(3)
    ]
    upper = iota((16, 128), 1) >= 64
    for half in range(2):
        low, high = [], []
        for x in range(2):
            for p in planes:
                p = p[x * 16 : (x + 1) * 16]
                start = half * SHARE
                low.append(pltpu.roll(p, 128 - start, 1) if start else p)
                high.append(pltpu.roll(p, 64 - start, 1))
        packed = [jnp.where(upper, high[k + 1], low[k]) for k in (0, 2, 4)]
        packed = jnp.concatenate(packed, axis=1).astype(BF)
        for k in range(COLS // 2):
            pay[2 * k + half] = packed


def percept_kernel(
    meta, dec, tall, left, right, v_first, v_second, weights, feat, slope_one, done,
    planes, px, one, w1, w2,
):
    r, c = meta[0], meta[1]
    col_first = c * TW - COL_HALO
    col_ok = column_mask(col_first)

    def first_small(dy):
        v = v_first[dy]
        return v + pltpu.roll(pltpu.roll(v, 3, 0), 64, 1)

    patch_weights(w1, first_small)
    for dy in range(3):
        for dx in range(3):
            v = v_second[dy, dx].astype(F32)
            v = jnp.concatenate([v, jnp.zeros((64, 64), F32)], axis=1)
            u = pltpu.roll(v, 64, 1)
            w2[dy * 128 : (dy + 1) * 128, dx * 128 : (dx + 1) * 128] = jnp.concatenate(
                [v, u], axis=0
            ).astype(BF)

    planes[...] = jnp.zeros(planes.shape, F32)
    for k in range(3):
        v = jnp.concatenate(
            [a.astype(F32) for a in (left[90 + k], tall[k], right[90 + k])], axis=0
        )
        planes[pl.ds(3 + k, 80, stride=8), :] = taller(v).T[0:80]

    done[...] = jnp.zeros((8, 128), F32)

    def gather(i, carry):
        v = dec[pl.ds(aligned(i * 32 + 40, 8), 32), :] + planes[pl.ds(aligned(i * 32, 32), 32), :]
        px[pl.ds(aligned(i * WIDE, 16), WIDE), :] = patch_tile(v)
        return carry

    lax.fori_loop(0, 19, gather, 0, unroll=True)
    px[19 * WIDE :, :] = jnp.zeros((WIDE, 128), BF)

    def first(tile, count):
        v = from_colours(px, tile, count, w1)
        for j in range(count):
            for k in range(4):
                p = (tile + j) * 4 + k
                x = v[j * WIDE : (j + 1) * WIDE, k * 128 : (k + 1) * 128]
                act, slope = silu_parts(x)
                act = keep_inside(act, r * TH - 5 + p, 1, col_ok)
                slope_one[pl.ds(aligned(p * WIDE, 16), WIDE), :] = slope.astype(BF)
                one[pl.ds(aligned(p * WIDE, 16), WIDE), :] = act.astype(BF)

    def first_group(i, carry):
        first(i * 4, 4)
        return carry

    lax.fori_loop(0, 4, first_group, 0, unroll=True)
    first(16, 3)
    ones = ((iota((128, 128), 0) >> 6) == (iota((128, 128), 1) >> 6)).astype(F32).astype(BF)

    def half_sum(v):
        return mm(v.astype(BF), ones)

    def second(i, carry):
        v = conv_rows(one, i * 8, 8, w2[...])
        f, slope = silu_parts(v)
        scale = lax.rsqrt(half_sum(f * f) + EPSILON)
        unit = f * scale
        weighted = weights[...] * (unit - pltpu.roll(unit, 64, 1))
        g = scale * (weighted - unit * half_sum(weighted * unit)) * slope
        g = keep_inside(g, r * TH - 4 + i * 8, 8, col_ok)
        feat[pl.ds(aligned(i * 8 * WIDE, 16), 8 * WIDE), :] = g.astype(BF)
        return carry

    lax.fori_loop(0, 9, second, 0, unroll=3)


def percept_back_kernel(meta, feat, slope_one, v_first, v_second, out, bv, w3, w4):
    r, c = meta[0], meta[1]
    col_ok = column_mask(c * TW - COL_HALO)

    def last_small(dy):
        parts = [v_first[2 - dy, (2 - dx) * 8 : (3 - dx) * 8, :] for dx in range(3)]
        return jnp.concatenate(parts + [jnp.zeros((8, 128), F32)], axis=0)

    colour_weights(w4, last_small)
    for dy in range(3):
        for dx in range(3):
            v = v_second[dy, dx].astype(F32)
            v = jnp.concatenate([v, jnp.zeros((64, 64), F32)], axis=1)
            w3[(2 - dx) * 128 : (3 - dx) * 128, (2 - dy) * 128 : (3 - dy) * 128] = jnp.concatenate(
                [v, jnp.zeros((64, 128), F32)], axis=0
            ).astype(BF)

    def back(i, carry):
        v = conv_rows(feat, i * 10, 10, w3[...], transposed=True)
        x = slope_one[pl.ds(aligned((i * 10 + 2) * WIDE, 16), 10 * WIDE), :]
        v = keep_inside(v * x.astype(F32), r * TH - 3 + i * 10, 10, col_ok)
        bv[pl.ds(aligned(i * 10 * WIDE, 16), 10 * WIDE), :] = v.astype(BF)
        return carry

    lax.fori_loop(0, 7, back, 0, unroll=True)
    bv[70 * WIDE :, :] = jnp.zeros((12 * WIDE, 128), BF)

    def colours(i, carry):
        v = to_colours(bv, i * 16, w4)
        out[pl.ds(aligned(i * 128, 128), 128), :] = pltpu.roll(v, 122, 1)
        return carry

    lax.fori_loop(0, 5, colours, 0, unroll=True)


STOP = object()
FAR = 16
STEPS = 6
HALF = STEPS + 1
TILES = 2 * HALF
LANES = TILES * 128
EVEN = HALF * 128


def critic_kernel(
    meta, strip, mine, other, far, far_other, _, out,
    strip32, grads, w_pre, w_one, w_two, w_back, score, distance, row_gap, row_gap_back, x_all, x_all_b, pre, pre_b, act, act_b,
    two, two_b, cols, cols_b, jobs,
):
    r, me = meta[0], meta[1]
    first_row = r * TH - 2 + SHARE * (me & 1)
    lane = iota((1, 128), 1)
    upper = lane >= 64
    first_x = (lane & 63) == 0
    last_x = (lane & 63) == 63

    def unpack(k, carry):
        v = strip[k].astype(F32)
        b, d = pltpu.roll(v[:, 128:256], 64, 1), pltpu.roll(v[:, 256:384], 64, 1)
        at = aligned(k * TW, 32)
        strip32[pl.ds(at, 16), :] = v[:, 0:256]
        strip32[pl.ds(at + 16, 16), :] = jnp.concatenate([jnp.where(upper, d, b), d], axis=1)
        return carry

    lax.fori_loop(0, COLS, unpack, 0, unroll=8)
    strip32[IMG_W:, :] = jnp.zeros((8, 256), F32)
    grads[...] = jnp.zeros(grads.shape, F32)
    w_back[...] = jnp.zeros(w_back.shape, BF)
    for g, source in enumerate((mine, other, far, far_other)):
        w_one[g] = source[1024:1120, :]
        w_pre[g] = (0.5 * taller(source[1024:1120, :].astype(F32))).T.astype(BF)
        score[g] = taller(source[1120:1136, :].astype(F32)).T
        for i in range(4):
            first, second = (
                source[i * 256 + k * 128 : i * 256 + (k + 1) * 128, :].astype(F32).T
                for k in range(2)
            )
            at = slice((i // 2) * 128, (i // 2 + 1) * 128)
            w_two[g, i % 2, 0:128, at] = jnp.where(upper, first, second).astype(BF)
            w_two[g, i % 2, 128:256, at] = jnp.where(upper, 0.0, first).astype(BF)
            w_two[g, i % 2, 256:384, at] = jnp.where(upper, second, 0.0).astype(BF)
        for par in range(2):
            for p in range(2):
                for t in range(2):
                    i = par + 2 * t
                    for kind, j in ((0, 1 + p), (1 + p, 3 - 3 * p)):
                        w_back[
                            g,
                            (par * 2 + 1 - p) * 64 : (par * 2 + 2 - p) * 64,
                            (t * 3 + kind) * 128 : (t * 3 + kind + 1) * 128,
                        ] = 0.5 * source[i * 256 + j * 64 : i * 256 + (j + 1) * 64, :]
    for t in (two, two_b):
        t[:, 0:128] = jnp.zeros((384, 128), BF)
        t[:, (STEPS + 1) * 128 :] = jnp.zeros((384, 128), BF)
    for t in (cols, cols_b):
        t[192:, :] = jnp.zeros((64, 384), F32)
    x, n = iota((CROP + 8, 384), 0), iota((CROP + 8, 384), 1)
    wanted = 4 * (n & 63) + (n >> 6) - 1
    wanted_ok = (wanted >= 0) & (wanted < CROP)
    distance[...] = jnp.where(wanted_ok, x - wanted, -1).astype(F32)

    def gap(dims, rho, n):
        tile, i, k = rho >> 4, (rho >> 2) & 3, rho & 3
        u = 2 * jnp.where(tile >= HALF, tile - HALF, tile) + jnp.where(tile >= HALF, 1, 0)
        return jnp.where(k < 3, n - (k * 40 + 2 * u + i), -1).astype(F32)

    dims = (TILES * 16, 128)
    row_gap[...] = gap(dims, iota(dims, 0), iota(dims, 1))
    dims = (128, TILES * 16)
    row_gap_back[...] = gap(dims, iota(dims, 1), iota(dims, 0))
    wide = iota((1, 256), 1)

    def anchor(q, k):
        return meta[2 + 2 * q + k]

    def owner_of(q):
        return meta[2 + 2 * CROPS + q]

    def job(q, x_all, pre, act, two, cols):
        top, left, apart = anchor(q, 0), anchor(q, 1), owner_of(q) ^ me
        g = (apart & 1) + 2 * ((apart // FAR) & 1)
        y0 = first_row - top
        v0 = lax.shift_right_arithmetic(y0 - 3, 2)
        e = 4 * v0 - y0 + 6
        crop_row = y0 - 9 + (wide & 63)
        in_crop = (crop_row >= 0) & (crop_row < CROP) & (wide < 192)
        here = pl.ds(aligned((left >> 3) * 8, 8), CROP + 8)
        window = jnp.where(in_crop, strip32[here, :], 0.0).astype(BF)
        pick = jnp.where(distance[...] == (left & 7).astype(F32), 1.0, 0.0).astype(BF)
        cols_of = mm(window, pick, 0, 0)
        none = jnp.zeros((8, 384), F32)
        halves = [
            jnp.concatenate(
                [cols_of[k * 64 + 24 * h : k * 64 + 24 * h + 40, :] for k in range(3)] + [none],
                axis=0,
            )
            for h in range(2)
        ]
        mixed = []
        for m in range(6):
            tile = slice((m // 2) * 128, (m // 2 + 1) * 128)
            low, high = halves[0][:, tile], halves[1][:, tile]
            if m % 2 == 0:
                high = pltpu.roll(high, 64, 1)
            else:
                low = pltpu.roll(low, 64, 1)
            mixed.append(jnp.where(upper, high, low))
        yield
        chosen = jnp.where(row_gap[...] == e.astype(F32), 1.0, 0.0).astype(BF)
        patches = mm(chosen, jnp.concatenate(mixed, axis=1).astype(BF)).astype(BF)
        for t in range(TILES):
            for m in range(6):
                x_all[m * 16 : (m + 1) * 16, t * 128 : (t + 1) * 128] = patches[
                    t * 16 : (t + 1) * 16, m * 128 : (m + 1) * 128
                ]
        yield
        weight = w_pre[g][:, 0:96]
        for t0 in range(0, TILES, 2):
            at = slice(t0 * 128, (t0 + 2) * 128)
            value = mm(weight, x_all[:, at])
            for t in range(t0, t0 + 2):
                at = slice(t * 128, (t + 1) * 128)
                n = 2 * (t % HALF) + t // HALF + jnp.where(upper, 2 * STEPS, 0)
                u = 2 * v0 - 1 + n
                ok = ((u >= 0) & (u < CROP // 2)).astype(F32)
                half = value[:, (t - t0) * 128 : (t - t0 + 1) * 128]
                rise = jnp.tanh(half) + 1.0
                kept = rise * ok
                pre[:, at] = kept * (1.0 + half * (2.0 - rise))
                act[:, at] = (half * kept).astype(BF)
            yield
        column = score[g][:, 0:1]
        for t0 in range(0, STEPS, 2):
            value = 0.0
            for par in range(2):
                at = par * EVEN + t0 * 128
                taps = jnp.concatenate(
                    [act[:, at : at + 256], act[:, at + 128 : at + 384]], axis=0
                )
                value = value + mm(w_two[g, par], taps)
            for t in range(t0, t0 + 2):
                at = slice((t - t0) * 128, (t - t0 + 1) * 128)
                f = value[0:128, at]
                f = f + jnp.where(first_x, 0.0, pltpu.roll(value[128:256, at], 1, 1))
                f = f + jnp.where(last_x, 0.0, pltpu.roll(value[256:384, at], 127, 1))
                f, slope = silu_parts(f)
                logit = jnp.sum(f * column, axis=0, keepdims=True)
                v = v0 + t + jnp.where(upper, STEPS, 0)
                ok = (v >= 0) & (v < CROP // 4)
                grad = jnp.where(ok, -LOSS_SCALE * sigmoid(-logit), 0.0)
                b = grad * (column * slope)
                at = slice((t + 1) * 128, (t + 2) * 128)
                two[0:128, at] = b.astype(BF)
                two[128:256, at] = jnp.where(first_x, 0.0, pltpu.roll(b, 1, 1)).astype(BF)
                two[256:384, at] = jnp.where(last_x, 0.0, pltpu.roll(b, 127, 1)).astype(BF)
            yield
        for s0 in range(0, HALF, 2):
            n = min(2, HALF - s0) * 128
            at = s0 * 128
            both = jnp.concatenate([two[:, 128 + at : 128 + at + n], two[:, at : at + n]], axis=0)
            up = mm(w_back[g], both)
            for par in range(2):
                here = slice(par * EVEN + at, par * EVEN + at + n)
                one = (up[par * 128 : (par + 1) * 128] * pre[:, here]).astype(BF)
                x_all[:, here] = mm(w_one[g], one).astype(BF)
            yield
        spread = jnp.concatenate(
            [
                jnp.concatenate(
                    [
                        x_all[m * 16 : (m + 1) * 16, t * 128 : (t + 1) * 128]
                        for t in range(TILES)
                    ],
                    axis=0,
                )
                for m in range(6)
            ],
            axis=1,
        )
        chosen = jnp.where(row_gap_back[...] == e.astype(F32), 1.0, 0.0).astype(BF)
        back = mm(chosen, spread)
        yield
        parts = []
        for h in range(2):
            tiles = []
            for k in range(3):
                low = back[:, 2 * k * 128 : (2 * k + 1) * 128]
                high = back[:, (2 * k + 1) * 128 : (2 * k + 2) * 128]
                if h == 0:
                    high = pltpu.roll(high, 64, 1)
                else:
                    low = pltpu.roll(low, 64, 1)
                tiles.append(jnp.where(upper, high, low))
            parts.append(jnp.concatenate(tiles, axis=1))
        for k in range(3):
            low, high = (part[k * 40 : (k + 1) * 40, :] for part in parts)
            cols[k * 64 : (k + 1) * 64, :] = jnp.concatenate(
                [low[0:24], low[24:40] + high[0:16], high[16:40]], axis=0
            )
        yield
        placed = mm(pick, cols[...].astype(BF), 1, 1)
        y = wide & 63
        keep = in_crop & (y >= 9) & (y < 9 + SHARE)
        yield
        here = pl.ds(aligned((left >> 3) * 8 + GRAD_PAD, 8), CROP + 8)
        grads[here, :] = grads[here, :] + jnp.where(keep, placed, 0.0)

    count, seen, turn = jnp.int32(0), jnp.int32(0), (me // FAR) & 1
    for q in range(CROPS):
        y0 = first_row - anchor(q, 0)
        shared = ((owner_of(q) ^ me) & (COLS - 2 - FAR)) == 0
        shared = (shared & (y0 < CROP) & (y0 + SHARE > 0)).astype(jnp.int32)
        jobs[count] = q
        count = count + shared * ((seen & 1) == turn).astype(jnp.int32)
        seen = seen + shared

    first_set, second_set = (x_all, pre, act, two, cols), (x_all_b, pre_b, act_b, two_b, cols_b)

    def two_crops(k, carry):
        running = [job(jobs[2 * k], *first_set), job(jobs[2 * k + 1], *second_set)]
        while running:
            running = [g for g in running if next(g, STOP) is not STOP]
        return carry

    lax.fori_loop(0, count >> 1, two_crops, 0)

    @pl.when((count & 1) == 1)
    def _():
        for _ in job(jobs[count - 1], *first_set):
            pass

    def pack(k, carry):
        block = grads[pl.ds(aligned(k * TW, 32), 48), :][GRAD_PAD - 2 : GRAD_PAD + 38]
        a, b = block[:, 0:128], block[:, 128:256]
        out[k] = jnp.where(
            lane < 40,
            pltpu.roll(a, 128 - 9, 1),
            jnp.where(lane < 80, pltpu.roll(a, 128 - 33, 1), pltpu.roll(b, 71, 1)),
        ).astype(BF)
        return carry

    lax.fori_loop(0, COLS, pack, 0, unroll=4)


def finish_kernel(
    meta, parts, lpips, slope, feats, w_mid, w_out, out, turned, planes, px, bm, w, w1
):
    r, c = meta[0], meta[1]
    for dy in range(3):
        for dx in range(3):
            w[dx * 128 : (dx + 1) * 128, dy * 128 : (dy + 1) * 128] = w_mid[2 - dy, 2 - dx]

    def small(dy):
        flipped = [w_out[2 - dy, (2 - dx) * 8 : (3 - dx) * 8, :] for dx in range(3)]
        return jnp.concatenate(flipped + [jnp.zeros((8, 128), F32)], axis=0)

    patch_weights(w1, small)
    col_ok = column_mask(c * TW - 2)
    planes[...] = jnp.zeros(planes.shape, F32)
    for half in range(2):
        total = parts[half].astype(F32)
        for k in range(1, COLS // 2):
            total = total + parts[2 * k + half].astype(F32)
        turned[...] = taller(total).T
        for k in range(3):
            planes[pl.ds(half * SHARE * 8 + k, 40, stride=8), :] = turned[k * 40 : (k + 1) * 40, :]

    def gather(i, carry):
        at = pl.ds(aligned(i * 32, 32), 32)
        ok = planar_inside(r * TH - 2 + i * 4, c * TW - 2, 0, 36, 4, 4)
        px[pl.ds(aligned(i * WIDE, 16), WIDE), :] = patch_tile(
            jnp.where(ok, lpips[at, :] + planes[at, :], 0.0)
        )
        return carry

    lax.fori_loop(0, 17, gather, 0, unroll=True)
    px[17 * WIDE :, :] = jnp.zeros((WIDE, 128), BF)

    def middle(tile, count):
        v = from_colours(px, tile, count, w1)
        for j in range(count):
            for k in range(4):
                n = (tile + j) * 4 + k
                x = v[j * WIDE : (j + 1) * WIDE, k * 128 : (k + 1) * 128]
                x = keep_inside(x * slope[n].astype(F32), r * TH - 1 + n, 1, col_ok)
                bm[pl.ds(aligned(n * WIDE, 16), WIDE), :] = x.astype(BF)

    def middle_group(i, carry):
        middle(i * 4, 4)
        return carry

    lax.fori_loop(0, 4, middle_group, 0, unroll=True)
    middle(16, 1)

    def last(i, carry):
        v = conv_rows(bm, i * 8, 8, w[...], transposed=True, shift=2)
        v = v.reshape(8, WIDE, 128)[:, 0:TW, :]
        x = feats[pl.ds(i * 8, 8)].astype(F32)
        out[pl.ds(i * 8, 8)] = (v * silu_parts(x)[1]).astype(BF)
        return carry

    lax.fori_loop(0, TH // 8, last, 0, unroll=4)


def call(kernel, outs, scratch, args, scalars=1, unused=0, lists=()):
    specs = [pl.BlockSpec(memory_space=pltpu.SMEM)] * scalars
    specs += [pl.BlockSpec(memory_space=pltpu.VMEM)] * (len(args) - scalars - unused)
    specs += [pl.BlockSpec(memory_space=pl.ANY)] * unused
    return pl.pallas_call(
        kernel,
        in_specs=specs,
        out_specs=jax.tree.map(lambda _: pl.BlockSpec(memory_space=pltpu.VMEM), outs),
        out_shape=outs,
        scratch_shapes=[pltpu.VMEM(s, t) for s, t in scratch] + list(lists),
        compiler_params=pltpu.CompilerParams(vmem_limit_bytes=VMEM),
        interpret=INTERPRET,
    )(*args)


INTERPRET = False


def shape(dims, kind):
    return jax.ShapeDtypeStruct(dims, kind)


def colour_first(w):
    w = jnp.pad(w.astype(F32), ((0, 0), (0, 1), (0, 5), (0, 128 - w.shape[-1])))
    return w.reshape(3, 32, 128)


def decode(meta, top, mid, bot, left, right, conv_mid, small):
    return call(
        decode_kernel,
        (
            shape((COLS, TW // 2, 384), BF),
            shape((1024, 128), F32),
            pltpu.HBM((68, WIDE, 128), BF),
        ),
        [((90 * WIDE, 128), BF), ((98 * WIDE, 128), BF), ((384, 384), BF), ((384, 384), BF)],
        (meta, top, mid, bot, left, right, conv_mid, small),
    )


def percept(meta, dec, tall, left, right, small, vgg_second, weights):
    scaled = jnp.pad(2.0 * LOSS_SCALE * weights, (0, 64)).reshape(1, 128)
    return call(
        percept_kernel,
        (
            pltpu.HBM((72 * WIDE, 128), BF),
            pltpu.HBM((76 * WIDE, 128), BF),
            shape((8, 128), F32),
        ),
        [
            ((80 * 8, 128), F32),
            ((20 * WIDE, 128), BF),
            ((76 * WIDE, 128), BF),
            ((256, 512), BF),
            ((384, 384), BF),
        ],
        (meta, dec, tall, left, right, small, vgg_second, scaled),
    )


def percept_back(meta, feat, slope_one, small, vgg_second):
    return call(
        percept_back_kernel,
        shape((80 * 8, 128), F32),
        [((82 * WIDE, 128), BF), ((384, 384), BF), ((384, 384), BF)],
        (meta, feat, slope_one, small, vgg_second),
    )


def critic_weights(first, second, score):
    w = jnp.pad(first, ((0, 0), (0, 0), (0, 1), (0, 0)))
    w = jnp.transpose(w, (1, 0, 2, 3)).reshape(4, 16, 64)
    w = jnp.concatenate(
        [jnp.pad(w, ((2, 0), (0, 0), (0, 0))), jnp.pad(w, ((0, 2), (0, 0), (0, 0)))], -1
    ).reshape(96, 128)
    score = jnp.pad(score[None], ((0, 15), (0, 0)))
    return jnp.concatenate([second.reshape(1024, 128), w, score], 0)


def critics(meta, strip, weights, after):
    pair = [
        ((96, LANES), BF),
        ((128, LANES), F32),
        ((128, LANES), BF),
        ((384, (STEPS + 2) * 128), BF),
        ((256, 384), F32),
    ]
    return call(
        critic_kernel,
        shape((COLS, 40, 128), BF),
        [
            ((IMG_W + 8, 256), F32),
            ((IMG_W + 24, 256), F32),
            ((4, 128, 128), BF),
            ((4, 96, 128), BF),
            ((4, 2, 384, 256), BF),
            ((4, 256, 768), BF),
            ((4, 128, 128), F32),
            ((CROP + 8, 384), F32),
            ((TILES * 16, 128), F32),
            ((128, TILES * 16), F32),
        ]
        + [buffer for buffer in pair for _ in range(2)],
        (meta, strip, *weights, after),
        unused=1,
        lists=[pltpu.SMEM((CROPS,), jnp.int32)],
    )


def finish(meta, parts, lpips, slope, feats, conv_mid, small):
    return call(
        finish_kernel,
        shape((TH, TW, 128), BF),
        [
            ((128, 128), F32),
            ((80 * 8, 128), F32),
            ((18 * WIDE, 128), BF),
            ((68 * WIDE, 128), BF),
            ((384, 384), BF),
            ((256, 512), BF),
        ],
        (meta, parts, lpips, slope, feats, conv_mid, small),
    )


def in_hbm(x):
    return pltpu.with_memory_space_constraint(x, pltpu.HBM)


def exchange(low, high, axis):
    count = lax.axis_size(axis)
    forward = [(i, i + 1) for i in range(count - 1)]
    backward = [(target, source) for source, target in forward]
    return lax.ppermute(low, axis, forward), lax.ppermute(high, axis, backward)


def local(
    features, conv_mid, conv_out, target, vgg_first, vgg_second, perceptual_weights,
    crop_anchors, crop_owner, critic_first, critic_second, critic_score,
):
    meta = jnp.concatenate(
        [
            jnp.stack([lax.axis_index("row"), lax.axis_index("col")]).astype(jnp.int32),
            crop_anchors.reshape(2 * CROPS),
            crop_owner.reshape(CROPS),
        ]
    )
    feats = features[0]
    planar = jnp.transpose(target[0], (2, 1, 0))

    low, high, own = call(
        pack_rows_kernel,
        (shape((FEAT_HALO + 1, TW, 128), BF),) * 2 + (shape((3, TW, 128), BF),),
        [],
        (in_hbm(feats), in_hbm(planar)),
        scalars=0,
    )
    top, bot = exchange(low, high, "row")
    side_l, side_r, tall = call(
        pack_sides_kernel,
        (shape((2 * FEAT_HALO + TH + 3, COL_HALO, 128), BF),) * 2 + (shape((3, TW, 128), BF),),
        [],
        (feats, own, top, bot),
        scalars=0,
    )
    left, right = exchange(side_l, side_r, "col")
    out_small = colour_first(jnp.transpose(conv_out, (0, 1, 3, 2)))
    vgg_small = colour_first(vgg_first)
    mine = critic_weights(critic_first[0], critic_second[0], critic_score[0])
    left, right, sent, meta, out_small = lax.optimization_barrier(
        (left, right, mine, meta, out_small)
    )
    far = lax.ppermute(sent, "col", [(i, i ^ FAR) for i in range(COLS)])
    pay, dec, slope = decode(meta, top, feats, bot, left, right, conv_mid, out_small)
    pay, far = lax.optimization_barrier((pay, far))
    strip = lax.all_to_all(pay, "col", split_axis=0, concat_axis=0, tiled=True)
    other = lax.ppermute(mine, "col", [(i, i ^ 1) for i in range(COLS)])
    far_other = lax.ppermute(far, "col", [(i, i ^ 1) for i in range(COLS)])
    feat, slope_one, done = percept(
        meta, dec, tall, left, right, vgg_small, vgg_second, perceptual_weights
    )
    grads = critics(meta, strip, (mine, other, far, in_hbm(far_other)), done)
    parts = lax.all_to_all(grads, "col", split_axis=0, concat_axis=0, tiled=True)
    lpips = percept_back(meta, in_hbm(feat), in_hbm(slope_one), vgg_small, vgg_second)
    return finish(meta, parts, lpips, slope, feats, conv_mid, out_small)[None]


def solution(mesh):
    placed = (
        P(None, "row", "col", None),
        P(),
        P(),
        P(None, "row", "col", None),
        P(),
        P(),
        P(),
        P(),
        P(),
        P("col", None, None, None, None),
        P("col", None, None, None, None),
        P("col", None),
    )
    return jax.shard_map(
        local, mesh=mesh, in_specs=placed, out_specs=P(None, "row", "col", None), check_vma=False
    )
```

```python
import jax
import jax.numpy as jnp
import numpy as np
from jax import lax
from jax.experimental import pallas as pl
from jax.experimental.pallas import tpu as pltpu
from jax.sharding import PartitionSpec as P

BF = jnp.bfloat16
F32 = jnp.float32

LOSS_SCALE = 32.0
EPSILON = 1e-06
CROP = 256
TH, TW = 64, 32
IMG_H, IMG_W = 512, 1024
ROWS, COLS = 8, 32
CROPS = 64
DEC_HALO = 11
FEAT_HALO = 13
COL_HALO = 8
WIDE = TW + 2 * COL_HALO
TGT_HALO = 6
GRAD_PAD = 8
SHARE = 34
SPAN = 52
VMEM = 20 * 1024 * 1024


def sigmoid(v):
    return 0.5 * jnp.tanh(0.5 * v) + 0.5


def silu_parts(v):
    sig = sigmoid(v)
    act = v * sig
    return act, sig + act * (1.0 - sig)


def mm(a, b, ca=1, cb=0):
    return lax.dot_general(a, b, (((ca,), (cb,)), ((), ())), preferred_element_type=F32)


def iota(shape, dim):
    return lax.broadcasted_iota(jnp.int32, shape, dim)


def aligned(start, unit):
    return pl.multiple_of(start, unit) if not isinstance(start, int) else start


def conv_rows(src, row0, rows, weight, transposed=False, shift=0):
    n = rows * WIDE
    lhs = jnp.concatenate(
        [src[pl.ds(aligned((row0 + dy) * WIDE, 16), n), :] for dy in range(3)], axis=1
    )
    z = mm(lhs, weight, 1, 1 if transposed else 0)
    parts = []
    for dx in range(3):
        amount = (1 - dx - shift) % n
        part = z[:, dx * 128 : (dx + 1) * 128]
        parts.append(pltpu.roll(part, amount, 0) if amount else part)
    return parts[0] + parts[1] + parts[2]


def column_mask(col_first):
    x = col_first + iota((1, WIDE, 128), 1)
    return ((x >= 0) & (x < IMG_W)).astype(F32)


def keep_inside(v, row_first, rows, col_ok):
    y = row_first + iota((rows, 1, 128), 0)
    row_ok = ((y >= 0) & (y < IMG_H)).astype(F32)
    return (v.reshape(rows, WIDE, 128) * (col_ok * row_ok)).reshape(rows * WIDE, 128)


def planar_inside(row_first, col_first, low, high, rows, limit):
    lane = iota((rows * 8, 128), 1)
    row = iota((rows * 8, 128), 0) >> 3
    x = col_first + lane
    y = row_first + row
    ok = (x >= 0) & (x < IMG_W) & (lane >= low) & (lane < high) & (y >= 0) & (y < IMG_H)
    return ok & (row < limit)


def wider(v):
    return jnp.concatenate([v, jnp.zeros((v.shape[0], 128 - v.shape[1]), F32)], axis=1)


def taller(v):
    return jnp.concatenate([v, jnp.zeros((128 - v.shape[0], 128), F32)], axis=0)


def colour_weights(w, small):
    k = iota((32, 384), 0)
    n = iota((32, 384), 1)
    copies = (((n >> 7) * 8 + (n & 7)) == k).astype(F32).astype(BF)
    for dy in range(3):
        w[dy * 128 : (dy + 1) * 128, :] = mm(small(dy).astype(BF), copies, 0, 0).astype(BF)


def to_colours(src, first, w):
    group = iota((WIDE, 128), 1) >> 3
    tile = jnp.zeros((WIDE, 128), F32)
    for half in range(2):
        v = conv_rows(src, first + half * 8, 8, w[...])
        for k in range(8):
            tile = jnp.where(group == half * 8 + k, v[k * WIDE : (k + 1) * WIDE], tile)
    return taller(tile).T


def patch_tile(v):
    after, before = pltpu.roll(v, 1, 1), pltpu.roll(v, 127, 1)
    none = jnp.zeros((8, 128), F32)
    parts = []
    for k in range(4):
        at = slice(k * 8, (k + 1) * 8)
        parts += [after[at], v[at], before[at], none]
    return jnp.concatenate(parts, axis=0).T[0:WIDE].astype(BF)


def patch_weights(w, small):
    w[...] = jnp.zeros(w.shape, BF)
    for k in range(4):
        for dy in range(3):
            w[(k + dy) * 32 : (k + dy + 1) * 32, k * 128 : (k + 1) * 128] = small(dy).astype(BF)


def from_colours(px, tile, count, w):
    at = [pl.ds(aligned((tile + k) * WIDE, 16), count * WIDE) for k in range(2)]
    return mm(jnp.concatenate([px[at[0], :], px[at[1], :]], axis=1), w[...])


def pack_rows_kernel(feats, target, low, high, own):
    lane = iota((TW, 128), 1)
    n = TGT_HALO
    colours = [wider(target[k].astype(F32)) for k in range(3)]
    for k in range(3):
        own[k] = colours[k].astype(BF)
    for out, y0, t0 in ((low, TH - FEAT_HALO, TH - n), (high, 0, 0)):
        extra = jnp.zeros((TW, 128), F32)
        for k in range(3):
            amount = (n * k - t0) % 128
            moved = pltpu.roll(colours[k], amount, 1) if amount else colours[k]
            extra = jnp.where((lane >= n * k) & (lane < n * k + n), moved, extra)
        out[0:FEAT_HALO] = feats[y0 : y0 + FEAT_HALO]
        out[FEAT_HALO] = extra.astype(BF)


def pack_sides_kernel(feats, own, top, bot, side_l, side_r, tall):
    lane = iota((TW, 128), 1)
    n = TGT_HALO
    above, below = top[FEAT_HALO].astype(F32), bot[FEAT_HALO].astype(F32)
    colours = []
    for k in range(3):
        first = pltpu.roll(above, 128 - n * k, 1) if k else above
        last = pltpu.roll(below, n + TH - n * k, 1)
        v = jnp.where(lane < n, first, pltpu.roll(own[k].astype(F32), n, 1))
        v = jnp.where(lane < n + TH, v, jnp.where(lane < 2 * n + TH, last, 0.0))
        tall[k] = v.astype(BF)
        colours.append(v)
    parts = (
        (0, top[0:FEAT_HALO]),
        (FEAT_HALO, feats[...]),
        (FEAT_HALO + TH, bot[0:FEAT_HALO]),
        (2 * FEAT_HALO + TH, jnp.stack(colours)),
    )
    for y, v in parts:
        v = v.astype(F32)
        for out, x0 in ((side_l, TW - COL_HALO), (side_r, 0)):
            out[y : y + v.shape[0]] = v[:, x0 : x0 + COL_HALO, :].astype(BF)


def decode_kernel(
    meta, top, mid, bot, left, right, w_mid, w_out, pay, dec, slope_out, s1, s2, w, w3
):
    r, c = meta[0], meta[1]
    for dy in range(3):
        for dx in range(3):
            w[dy * 128 : (dy + 1) * 128, dx * 128 : (dx + 1) * 128] = w_mid[dy, dx]
    colour_weights(w3, lambda dy: w_out[dy])

    def fill(first, rows, centre):
        n = rows * WIDE
        parts = [left[pl.ds(first, rows)], centre, right[pl.ds(first, rows)]]
        v = jnp.concatenate([p.astype(F32) for p in parts], axis=1).reshape(n, 128)
        s1[pl.ds(aligned(first * WIDE, 16), n), :] = (v * sigmoid(v)).astype(BF)

    fill(0, FEAT_HALO, top[0:FEAT_HALO])
    fill(FEAT_HALO + TH, FEAT_HALO, bot[0:FEAT_HALO])

    def fill_mid(i, carry):
        fill(FEAT_HALO + i * 8, 8, mid[pl.ds(i * 8, 8)])
        return carry

    lax.fori_loop(0, TH // 8, fill_mid, 0, unroll=2)
    col_ok = column_mask(c * TW - COL_HALO)

    def middle(i, carry):
        v = conv_rows(s1, i * 8, 8, w[...])
        act, slope = silu_parts(v)
        act = keep_inside(act, r * TH - 12 + i * 8, 8, col_ok)
        s2[pl.ds(aligned(i * 8 * WIDE, 16), 8 * WIDE), :] = act.astype(BF)
        slope = pltpu.roll(slope, 8 * WIDE - 6, 0).reshape(8, WIDE, 128).astype(BF)
        first, last = max(i * 8, 11), min(i * 8 + 8, 79)
        if first < last:
            slope_out[first - 11 : last - 11] = slope[first - i * 8 : last - i * 8]
        return carry

    for i in range(11):
        middle(i, 0)
    s2[88 * WIDE :, :] = jnp.zeros((10 * WIDE, 128), BF)
    dec[768:, :] = jnp.zeros((256, 128), F32)

    def colours(i, carry):
        v = to_colours(s2, i * 16, w3)
        ok = planar_inside(
            r * TH - DEC_HALO + i * 16, c * TW - COL_HALO, 2, WIDE - 2, 16, 86 - i * 16
        )
        dec[pl.ds(aligned(i * 128, 128), 128), :] = jnp.where(ok, v, 0.0).astype(BF).astype(F32)
        return carry

    lax.fori_loop(0, 6, colours, 0, unroll=True)
    planes = [
        dec[pl.ds(k, 128, stride=8), :].T[COL_HALO : COL_HALO + TW, :] for k in range(3)
    ]
    lane = iota((8, 128), 1)
    for half in range(2):
        tiles = [jnp.zeros((8, 128), F32) for _ in range(5)]
        for g in range(4):
            for k in range(3):
                piece = planes[k][g * 8 : (g + 1) * 8]
                if half:
                    piece = pltpu.roll(piece, 128 - SHARE, 1)
                piece = jnp.where(lane < SPAN, piece, 0.0)
                at, off = divmod((g * 3 + k) * SPAN, 128)
                if off:
                    piece = pltpu.roll(piece, off, 1)
                tiles[at] = tiles[at] + jnp.where(lane >= off, piece, 0.0)
                if off + SPAN > 128:
                    tiles[at + 1] = tiles[at + 1] + jnp.where(lane < off, piece, 0.0)
        packed = jnp.concatenate(tiles, axis=1).astype(BF)
        for k in range(COLS // 2):
            pay[2 * k + half] = packed


def percept_kernel(
    meta, dec, tall, left, right, v_first, v_second, weights, feat, slope_one, done,
    planes, px, one, w1, w2,
):
    r, c = meta[0], meta[1]
    col_first = c * TW - COL_HALO
    col_ok = column_mask(col_first)

    def first_small(dy):
        v = v_first[dy]
        return v + pltpu.roll(pltpu.roll(v, 3, 0), 64, 1)

    patch_weights(w1, first_small)
    for dy in range(3):
        for dx in range(3):
            v = v_second[dy, dx].astype(F32)
            v = jnp.concatenate([v, jnp.zeros((64, 64), F32)], axis=1)
            u = pltpu.roll(v, 64, 1)
            w2[dy * 128 : (dy + 1) * 128, dx * 128 : (dx + 1) * 128] = jnp.concatenate(
                [v, u], axis=0
            ).astype(BF)

    planes[...] = jnp.zeros(planes.shape, F32)
    for k in range(3):
        v = jnp.concatenate(
            [a.astype(F32) for a in (left[90 + k], tall[k], right[90 + k])], axis=0
        )
        planes[pl.ds(3 + k, 80, stride=8), :] = taller(v).T[0:80]

    done[...] = jnp.zeros((8, 128), F32)

    def gather(i, carry):
        v = dec[pl.ds(aligned(i * 32 + 40, 8), 32), :] + planes[pl.ds(aligned(i * 32, 32), 32), :]
        px[pl.ds(aligned(i * WIDE, 16), WIDE), :] = patch_tile(v)
        return carry

    lax.fori_loop(0, 19, gather, 0, unroll=True)
    px[19 * WIDE :, :] = jnp.zeros((WIDE, 128), BF)

    def first(tile, count):
        v = from_colours(px, tile, count, w1)
        for j in range(count):
            for k in range(4):
                p = (tile + j) * 4 + k
                x = v[j * WIDE : (j + 1) * WIDE, k * 128 : (k + 1) * 128]
                act, slope = silu_parts(x)
                act = keep_inside(act, r * TH - 5 + p, 1, col_ok)
                slope_one[pl.ds(aligned(p * WIDE, 16), WIDE), :] = slope.astype(BF)
                one[pl.ds(aligned(p * WIDE, 16), WIDE), :] = act.astype(BF)

    def first_group(i, carry):
        first(i * 4, 4)
        return carry

    lax.fori_loop(0, 4, first_group, 0, unroll=True)
    first(16, 3)
    ones = ((iota((128, 128), 0) >> 6) == (iota((128, 128), 1) >> 6)).astype(F32).astype(BF)

    def half_sum(v):
        return mm(v.astype(BF), ones)

    def second(i, carry):
        v = conv_rows(one, i * 8, 8, w2[...])
        f, slope = silu_parts(v)
        scale = lax.rsqrt(half_sum(f * f) + EPSILON)
        unit = f * scale
        weighted = weights[...] * (unit - pltpu.roll(unit, 64, 1))
        g = scale * (weighted - unit * half_sum(weighted * unit)) * slope
        g = keep_inside(g, r * TH - 4 + i * 8, 8, col_ok)
        feat[pl.ds(aligned(i * 8 * WIDE, 16), 8 * WIDE), :] = g.astype(BF)
        return carry

    lax.fori_loop(0, 9, second, 0, unroll=3)


def percept_back_kernel(
    meta, feat, slope_one, v_first, v_second, feats, w_mid, w_out, out, feats_slope, w, w1,
    bv, w3, w4,
):
    r, c = meta[0], meta[1]
    col_ok = column_mask(c * TW - COL_HALO)

    def last_small(dy):
        parts = [v_first[2 - dy, (2 - dx) * 8 : (3 - dx) * 8, :] for dx in range(3)]
        return jnp.concatenate(parts + [jnp.zeros((8, 128), F32)], axis=0)

    colour_weights(w4, last_small)
    for dy in range(3):
        for dx in range(3):
            w[dx * 128 : (dx + 1) * 128, dy * 128 : (dy + 1) * 128] = w_mid[2 - dy, 2 - dx]

    def small(dy):
        flipped = [w_out[2 - dy, (2 - dx) * 8 : (3 - dx) * 8, :] for dx in range(3)]
        return jnp.concatenate(flipped + [jnp.zeros((8, 128), F32)], axis=0)

    patch_weights(w1, small)
    def feature_slope(i, carry):
        at = pl.ds(i * 8, 8)
        feats_slope[at] = silu_parts(feats[at].astype(F32))[1].astype(BF)
        return carry

    lax.fori_loop(0, TH // 8, feature_slope, 0, unroll=2)
    for dy in range(3):
        for dx in range(3):
            v = v_second[dy, dx].astype(F32)
            v = jnp.concatenate([v, jnp.zeros((64, 64), F32)], axis=1)
            w3[(2 - dx) * 128 : (3 - dx) * 128, (2 - dy) * 128 : (3 - dy) * 128] = jnp.concatenate(
                [v, jnp.zeros((64, 128), F32)], axis=0
            ).astype(BF)

    def back(i, carry):
        v = conv_rows(feat, i * 10, 10, w3[...], transposed=True)
        x = slope_one[pl.ds(aligned((i * 10 + 2) * WIDE, 16), 10 * WIDE), :]
        v = keep_inside(v * x.astype(F32), r * TH - 3 + i * 10, 10, col_ok)
        bv[pl.ds(aligned(i * 10 * WIDE, 16), 10 * WIDE), :] = v.astype(BF)
        return carry

    lax.fori_loop(0, 7, back, 0, unroll=True)
    bv[70 * WIDE :, :] = jnp.zeros((12 * WIDE, 128), BF)

    def colours(i, carry):
        v = to_colours(bv, i * 16, w4)
        out[pl.ds(aligned(i * 128, 128), 128), :] = pltpu.roll(v, 122, 1)
        return carry

    lax.fori_loop(0, 5, colours, 0, unroll=True)


STOP = object()
FAR = 16
STEPS = 6
HALF = STEPS + 1
TILES = 2 * HALF
LANES = TILES * 128
EVEN = HALF * 128


def critic_kernel(
    meta, strip, mine, other, far, far_other, _, out,
    strip32, grads, w_pre, w_one, w_two, w_back, score, distance, row_gap, row_gap_back, *rest,
):
    x_all, pre, act, two, cols = (rest[k * 4 : (k + 1) * 4] for k in range(5))
    jobs = rest[20]
    r, me = meta[0], meta[1]
    first_row = r * TH - 2 + SHARE * (me & 1)
    lane = iota((1, 128), 1)
    upper = lane >= 64
    first_x = (lane & 63) == 0
    last_x = (lane & 63) == 63

    def unpack(k, carry):
        v = strip[k].astype(F32)

        def piece(g, j, place):
            at, off = divmod((g * 3 + j) * SPAN, 128)
            amount = (place - off) % 128
            parts = [v[:, at * 128 : (at + 1) * 128]]
            if off + SPAN > 128:
                parts.append(v[:, (at + 1) * 128 : (at + 2) * 128])
            parts = [pltpu.roll(p, amount, 1) if amount else p for p in parts]
            if len(parts) == 1:
                return parts[0]
            return jnp.where(lane < place + 128 - off, parts[0], parts[1])

        for g in range(4):
            both = jnp.where(upper, piece(g, 1, 64), piece(g, 0, 0))
            row = jnp.concatenate([both, piece(g, 2, 0)], axis=1)
            strip32[pl.ds(aligned(k * TW + g * 8, 8), 8), :] = row
        return carry

    lax.fori_loop(0, COLS, unpack, 0, unroll=8)
    strip32[IMG_W:, :] = jnp.zeros((8, 256), F32)
    grads[...] = jnp.zeros(grads.shape, F32)
    w_back[...] = jnp.zeros(w_back.shape, BF)
    for g, source in enumerate((mine, other, far, far_other)):
        w_one[g] = source[1024:1120, :]
        w_pre[g] = (0.5 * taller(source[1024:1120, :].astype(F32))).T.astype(BF)
        score[g] = taller(source[1120:1136, :].astype(F32)).T
        for i in range(4):
            first, second = (
                source[i * 256 + k * 128 : i * 256 + (k + 1) * 128, :].astype(F32).T
                for k in range(2)
            )
            at = slice((i // 2) * 128, (i // 2 + 1) * 128)
            w_two[g, i % 2, 0:128, at] = jnp.where(upper, first, second).astype(BF)
            w_two[g, i % 2, 128:256, at] = jnp.where(upper, 0.0, first).astype(BF)
            w_two[g, i % 2, 256:384, at] = jnp.where(upper, second, 0.0).astype(BF)
        for par in range(2):
            for p in range(2):
                for t in range(2):
                    i = par + 2 * t
                    for kind, j in ((0, 1 + p), (1 + p, 3 - 3 * p)):
                        w_back[
                            g,
                            (par * 2 + 1 - p) * 64 : (par * 2 + 2 - p) * 64,
                            (t * 3 + kind) * 128 : (t * 3 + kind + 1) * 128,
                        ] = 0.5 * source[i * 256 + j * 64 : i * 256 + (j + 1) * 64, :]
    for t in two:
        t[:, 0:128] = jnp.zeros((384, 128), BF)
        t[:, (STEPS + 1) * 128 :] = jnp.zeros((384, 128), BF)
    for t in cols:
        t[192:, :] = jnp.zeros((64, 384), F32)
    x, n = iota((CROP + 8, 384), 0), iota((CROP + 8, 384), 1)
    wanted = 4 * (n & 63) + (n >> 6) - 1
    wanted_ok = (wanted >= 0) & (wanted < CROP)
    distance[...] = jnp.where(wanted_ok, x - wanted, -1).astype(F32)

    def gap(dims, rho, n):
        tile, i, k = rho >> 4, (rho >> 2) & 3, rho & 3
        u = 2 * jnp.where(tile >= HALF, tile - HALF, tile) + jnp.where(tile >= HALF, 1, 0)
        return jnp.where(k < 3, n - (k * 40 + 2 * u + i), -1).astype(F32)

    dims = (TILES * 16, 128)
    row_gap[...] = gap(dims, iota(dims, 0), iota(dims, 1))
    dims = (128, TILES * 16)
    row_gap_back[...] = gap(dims, iota(dims, 1), iota(dims, 0))
    wide = iota((1, 256), 1)

    def anchor(q, k):
        return meta[2 + 2 * q + k]

    def owner_of(q):
        return meta[2 + 2 * CROPS + q]

    def job(q, x_all, pre, act, two, cols):
        top, left, apart = anchor(q, 0), anchor(q, 1), owner_of(q) ^ me
        g = (apart & 1) + 2 * ((apart // FAR) & 1)
        y0 = first_row - top
        v0 = lax.shift_right_arithmetic(y0 - 3, 2)
        e = 4 * v0 - y0 + 6
        crop_row = y0 - 9 + (wide & 63)
        in_crop = (crop_row >= 0) & (crop_row < CROP) & (wide < 192)
        here = pl.ds(aligned((left >> 3) * 8, 8), CROP + 8)
        window = jnp.where(in_crop, strip32[here, :], 0.0).astype(BF)
        pick = jnp.where(distance[...] == (left & 7).astype(F32), 1.0, 0.0).astype(BF)
        cols_of = mm(window, pick, 0, 0)
        none = jnp.zeros((8, 384), F32)
        halves = [
            jnp.concatenate(
                [cols_of[k * 64 + 24 * h : k * 64 + 24 * h + 40, :] for k in range(3)] + [none],
                axis=0,
            )
            for h in range(2)
        ]
        mixed = []
        for m in range(6):
            tile = slice((m // 2) * 128, (m // 2 + 1) * 128)
            low, high = halves[0][:, tile], halves[1][:, tile]
            if m % 2 == 0:
                high = pltpu.roll(high, 64, 1)
            else:
                low = pltpu.roll(low, 64, 1)
            mixed.append(jnp.where(upper, high, low))
        yield
        chosen = jnp.where(row_gap[...] == e.astype(F32), 1.0, 0.0).astype(BF)
        patches = mm(chosen, jnp.concatenate(mixed, axis=1).astype(BF)).astype(BF)
        for t in range(TILES):
            for m in range(6):
                x_all[m * 16 : (m + 1) * 16, t * 128 : (t + 1) * 128] = patches[
                    t * 16 : (t + 1) * 16, m * 128 : (m + 1) * 128
                ]
        yield
        weight = w_pre[g][:, 0:96]
        for t0 in range(0, TILES, 2):
            at = slice(t0 * 128, (t0 + 2) * 128)
            value = mm(weight, x_all[:, at])
            for t in range(t0, t0 + 2):
                at = slice(t * 128, (t + 1) * 128)
                n = 2 * (t % HALF) + t // HALF + jnp.where(upper, 2 * STEPS, 0)
                u = 2 * v0 - 1 + n
                ok = ((u >= 0) & (u < CROP // 2)).astype(F32)
                half = value[:, (t - t0) * 128 : (t - t0 + 1) * 128]
                rise = jnp.tanh(half) + 1.0
                kept = rise * ok
                pre[:, at] = kept * (1.0 + half * (2.0 - rise))
                act[:, at] = (half * kept).astype(BF)
            yield
        column = score[g][:, 0:1]
        for t0 in range(0, STEPS, 2):
            value = 0.0
            for par in range(2):
                at = par * EVEN + t0 * 128
                taps = jnp.concatenate(
                    [act[:, at : at + 256], act[:, at + 128 : at + 384]], axis=0
                )
                value = value + mm(w_two[g, par], taps)
            for t in range(t0, t0 + 2):
                at = slice((t - t0) * 128, (t - t0 + 1) * 128)
                f = value[0:128, at]
                f = f + jnp.where(first_x, 0.0, pltpu.roll(value[128:256, at], 1, 1))
                f = f + jnp.where(last_x, 0.0, pltpu.roll(value[256:384, at], 127, 1))
                f, slope = silu_parts(f)
                logit = jnp.sum(f * column, axis=0, keepdims=True)
                v = v0 + t + jnp.where(upper, STEPS, 0)
                ok = (v >= 0) & (v < CROP // 4)
                grad = jnp.where(ok, -LOSS_SCALE * sigmoid(-logit), 0.0)
                b = grad * (column * slope)
                at = slice((t + 1) * 128, (t + 2) * 128)
                two[0:128, at] = b.astype(BF)
                two[128:256, at] = jnp.where(first_x, 0.0, pltpu.roll(b, 1, 1)).astype(BF)
                two[256:384, at] = jnp.where(last_x, 0.0, pltpu.roll(b, 127, 1)).astype(BF)
            yield
        for s0 in range(0, HALF, 2):
            n = min(2, HALF - s0) * 128
            at = s0 * 128
            both = jnp.concatenate([two[:, 128 + at : 128 + at + n], two[:, at : at + n]], axis=0)
            up = mm(w_back[g], both)
            for par in range(2):
                here = slice(par * EVEN + at, par * EVEN + at + n)
                one = (up[par * 128 : (par + 1) * 128] * pre[:, here]).astype(BF)
                x_all[:, here] = mm(w_one[g], one).astype(BF)
            yield
        spread = jnp.concatenate(
            [
                jnp.concatenate(
                    [
                        x_all[m * 16 : (m + 1) * 16, t * 128 : (t + 1) * 128]
                        for t in range(TILES)
                    ],
                    axis=0,
                )
                for m in range(6)
            ],
            axis=1,
        )
        chosen = jnp.where(row_gap_back[...] == e.astype(F32), 1.0, 0.0).astype(BF)
        back = mm(chosen, spread)
        yield
        parts = []
        for h in range(2):
            tiles = []
            for k in range(3):
                low = back[:, 2 * k * 128 : (2 * k + 1) * 128]
                high = back[:, (2 * k + 1) * 128 : (2 * k + 2) * 128]
                if h == 0:
                    high = pltpu.roll(high, 64, 1)
                else:
                    low = pltpu.roll(low, 64, 1)
                tiles.append(jnp.where(upper, high, low))
            parts.append(jnp.concatenate(tiles, axis=1))
        for k in range(3):
            low, high = (part[k * 40 : (k + 1) * 40, :] for part in parts)
            cols[k * 64 : (k + 1) * 64, :] = jnp.concatenate(
                [low[0:24], low[24:40] + high[0:16], high[16:40]], axis=0
            )
        yield
        placed = mm(pick, cols[...].astype(BF), 1, 1)
        y = wide & 63
        keep = in_crop & (y >= 9) & (y < 9 + SHARE)
        yield
        here = pl.ds(aligned((left >> 3) * 8 + GRAD_PAD, 8), CROP + 8)
        grads[here, :] = grads[here, :] + jnp.where(keep, placed, 0.0)

    count, seen, turn = jnp.int32(0), jnp.int32(0), (me // FAR) & 1
    for q in range(CROPS):
        y0 = first_row - anchor(q, 0)
        shared = ((owner_of(q) ^ me) & (COLS - 2 - FAR)) == 0
        shared = (shared & (y0 < CROP) & (y0 + SHARE > 0)).astype(jnp.int32)
        jobs[count] = q
        count = count + shared * ((seen & 1) == turn).astype(jnp.int32)
        seen = seen + shared

    sets = tuple(zip(x_all, pre, act, two, cols))

    def crops(first, number):
        running = [job(jobs[first + k], *sets[k]) for k in range(number)]
        while running:
            running = [g for g in running if next(g, STOP) is not STOP]

    def four_crops(k, carry):
        crops(4 * k, 4)
        return carry

    lax.fori_loop(0, count >> 2, four_crops, 0)

    @pl.when((count & 2) == 2)
    def _():
        crops((count >> 2) * 4, 2)

    @pl.when((count & 1) == 1)
    def _():
        crops(count - 1, 1)

    def pack(k, carry):
        block = grads[pl.ds(aligned(k * TW, 32), 48), :][GRAD_PAD - 2 : GRAD_PAD + 38]
        a, b = block[:, 0:128], block[:, 128:256]
        out[k] = jnp.where(
            lane < 40,
            pltpu.roll(a, 128 - 9, 1),
            jnp.where(lane < 80, pltpu.roll(a, 128 - 33, 1), pltpu.roll(b, 71, 1)),
        ).astype(BF)
        return carry

    lax.fori_loop(0, COLS, pack, 0, unroll=4)


def finish_kernel(
    meta, parts, lpips, slope, feats_slope, w, w1, out, turned, planes, px, bm
):
    r, c = meta[0], meta[1]
    col_ok = column_mask(c * TW - 2)
    planes[...] = jnp.zeros(planes.shape, F32)
    for half in range(2):
        total = parts[half].astype(F32)
        for k in range(1, COLS // 2):
            total = total + parts[2 * k + half].astype(F32)
        turned[...] = taller(total).T
        for k in range(3):
            planes[pl.ds(half * SHARE * 8 + k, 40, stride=8), :] = turned[k * 40 : (k + 1) * 40, :]

    def gather(i, carry):
        at = pl.ds(aligned(i * 32, 32), 32)
        ok = planar_inside(r * TH - 2 + i * 4, c * TW - 2, 0, 36, 4, 4)
        px[pl.ds(aligned(i * WIDE, 16), WIDE), :] = patch_tile(
            jnp.where(ok, lpips[at, :] + planes[at, :], 0.0)
        )
        return carry

    lax.fori_loop(0, 17, gather, 0, unroll=True)
    px[17 * WIDE :, :] = jnp.zeros((WIDE, 128), BF)

    def middle(tile, count):
        v = from_colours(px, tile, count, w1)
        for j in range(count):
            for k in range(4):
                n = (tile + j) * 4 + k
                x = v[j * WIDE : (j + 1) * WIDE, k * 128 : (k + 1) * 128]
                x = keep_inside(x * slope[n].astype(F32), r * TH - 1 + n, 1, col_ok)
                bm[pl.ds(aligned(n * WIDE, 16), WIDE), :] = x.astype(BF)

    def middle_group(i, carry):
        middle(i * 4, 4)
        return carry

    lax.fori_loop(0, 4, middle_group, 0, unroll=True)
    middle(16, 1)

    def last(i, carry):
        v = conv_rows(bm, i * 8, 8, w[...], transposed=True, shift=2)
        v = v.reshape(8, WIDE, 128)[:, 0:TW, :]
        at = pl.ds(i * 8, 8)
        out[at] = (v * feats_slope[at].astype(F32)).astype(BF)
        return carry

    lax.fori_loop(0, TH // 8, last, 0, unroll=True)


def call(kernel, outs, scratch, args, scalars=1, unused=0, lists=(), vmem=VMEM):
    specs = [pl.BlockSpec(memory_space=pltpu.SMEM)] * scalars
    specs += [pl.BlockSpec(memory_space=pltpu.VMEM)] * (len(args) - scalars - unused)
    specs += [pl.BlockSpec(memory_space=pl.ANY)] * unused
    return pl.pallas_call(
        kernel,
        in_specs=specs,
        out_specs=jax.tree.map(lambda _: pl.BlockSpec(memory_space=pltpu.VMEM), outs),
        out_shape=outs,
        scratch_shapes=[pltpu.VMEM(s, t) for s, t in scratch] + list(lists),
        compiler_params=pltpu.CompilerParams(vmem_limit_bytes=vmem),
        interpret=INTERPRET,
    )(*args)


INTERPRET = False


def shape(dims, kind):
    return jax.ShapeDtypeStruct(dims, kind)


def colour_first(w):
    w = jnp.pad(w.astype(F32), ((0, 0), (0, 1), (0, 5), (0, 128 - w.shape[-1])))
    return w.reshape(3, 32, 128)


def decode(meta, top, mid, bot, left, right, conv_mid, small):
    return call(
        decode_kernel,
        (
            shape((COLS, TW // 4, 640), BF),
            shape((1024, 128), F32),
            pltpu.HBM((68, WIDE, 128), BF),
        ),
        [((90 * WIDE, 128), BF), ((98 * WIDE, 128), BF), ((384, 384), BF), ((384, 384), BF)],
        (meta, top, mid, bot, left, right, conv_mid, small),
    )


def percept(meta, dec, tall, left, right, small, vgg_second, weights):
    scaled = jnp.pad(2.0 * LOSS_SCALE * weights, (0, 64)).reshape(1, 128)
    return call(
        percept_kernel,
        (
            pltpu.HBM((72 * WIDE, 128), BF),
            pltpu.HBM((76 * WIDE, 128), BF),
            shape((8, 128), F32),
        ),
        [
            ((80 * 8, 128), F32),
            ((20 * WIDE, 128), BF),
            ((76 * WIDE, 128), BF),
            ((256, 512), BF),
            ((384, 384), BF),
        ],
        (meta, dec, tall, left, right, small, vgg_second, scaled),
    )


def percept_back(meta, feat, slope_one, small, vgg_second, feats, conv_mid, out_small):
    return call(
        percept_back_kernel,
        (
            shape((80 * 8, 128), F32),
            shape((TH, TW, 128), BF),
            shape((384, 384), BF),
            shape((256, 512), BF),
        ),
        [((82 * WIDE, 128), BF), ((384, 384), BF), ((384, 384), BF)],
        (meta, feat, slope_one, small, vgg_second, feats, conv_mid, out_small),
    )


def critic_weights(first, second, score):
    w = jnp.pad(first, ((0, 0), (0, 0), (0, 1), (0, 0)))
    w = jnp.transpose(w, (1, 0, 2, 3)).reshape(4, 16, 64)
    w = jnp.concatenate(
        [jnp.pad(w, ((2, 0), (0, 0), (0, 0))), jnp.pad(w, ((0, 2), (0, 0), (0, 0)))], -1
    ).reshape(96, 128)
    score = jnp.pad(score[None], ((0, 15), (0, 0)))
    return jnp.concatenate([second.reshape(1024, 128), w, score], 0)


def critics(meta, strip, weights, after):
    pair = [
        ((96, LANES), BF),
        ((128, LANES), F32),
        ((128, LANES), BF),
        ((384, (STEPS + 2) * 128), BF),
        ((256, 384), F32),
    ]
    return call(
        critic_kernel,
        shape((COLS, 40, 128), BF),
        [
            ((IMG_W + 8, 256), F32),
            ((IMG_W + 24, 256), F32),
            ((4, 128, 128), BF),
            ((4, 96, 128), BF),
            ((4, 2, 384, 256), BF),
            ((4, 256, 768), BF),
            ((4, 128, 128), F32),
            ((CROP + 8, 384), F32),
            ((TILES * 16, 128), F32),
            ((128, TILES * 16), F32),
        ]
        + [buffer for buffer in pair for _ in range(4)],
        (meta, strip, *weights, after),
        unused=1,
        lists=[pltpu.SMEM((CROPS,), jnp.int32)],
        vmem=30 * 1024 * 1024,
    )


def finish(meta, parts, lpips, slope, feats_slope, w, w1):
    return call(
        finish_kernel,
        shape((TH, TW, 128), BF),
        [
            ((128, 128), F32),
            ((80 * 8, 128), F32),
            ((18 * WIDE, 128), BF),
            ((68 * WIDE, 128), BF),
        ],
        (meta, parts, lpips, slope, feats_slope, w, w1),
    )


def in_hbm(x):
    return pltpu.with_memory_space_constraint(x, pltpu.HBM)


def exchange(low, high, axis):
    count = lax.axis_size(axis)
    forward = [(i, i + 1) for i in range(count - 1)]
    backward = [(target, source) for source, target in forward]
    return lax.ppermute(low, axis, forward), lax.ppermute(high, axis, backward)


def local(
    features, conv_mid, conv_out, target, vgg_first, vgg_second, perceptual_weights,
    crop_anchors, crop_owner, critic_first, critic_second, critic_score,
):
    meta = jnp.concatenate(
        [
            jnp.stack([lax.axis_index("row"), lax.axis_index("col")]).astype(jnp.int32),
            crop_anchors.reshape(2 * CROPS),
            crop_owner.reshape(CROPS),
        ]
    )
    feats = features[0]
    planar = jnp.transpose(target[0], (2, 1, 0))

    low, high, own = call(
        pack_rows_kernel,
        (shape((FEAT_HALO + 1, TW, 128), BF),) * 2 + (shape((3, TW, 128), BF),),
        [],
        (in_hbm(feats), in_hbm(planar)),
        scalars=0,
    )
    top, bot = exchange(low, high, "row")
    side_l, side_r, tall = call(
        pack_sides_kernel,
        (shape((2 * FEAT_HALO + TH + 3, COL_HALO, 128), BF),) * 2 + (shape((3, TW, 128), BF),),
        [],
        (feats, own, top, bot),
        scalars=0,
    )
    left, right = exchange(side_l, side_r, "col")
    out_small = colour_first(jnp.transpose(conv_out, (0, 1, 3, 2)))
    vgg_small = colour_first(vgg_first)
    mine = critic_weights(critic_first[0], critic_second[0], critic_score[0])
    left, right, sent, meta, out_small = lax.optimization_barrier(
        (left, right, mine, meta, out_small)
    )
    far = lax.ppermute(sent, "col", [(i, i ^ FAR) for i in range(COLS)])
    pay, dec, slope = decode(meta, top, feats, bot, left, right, conv_mid, out_small)
    pay, far = lax.optimization_barrier((pay, far))
    strip = lax.all_to_all(pay, "col", split_axis=0, concat_axis=0, tiled=True)
    other = lax.ppermute(mine, "col", [(i, i ^ 1) for i in range(COLS)])
    far_other = lax.ppermute(far, "col", [(i, i ^ 1) for i in range(COLS)])
    feat, slope_one, done = percept(
        meta, dec, tall, left, right, vgg_small, vgg_second, perceptual_weights
    )
    grads = critics(meta, strip, (mine, other, far, in_hbm(far_other)), done)
    parts = lax.all_to_all(grads, "col", split_axis=0, concat_axis=0, tiled=True)
    lpips, *made = percept_back(
        meta, in_hbm(feat), in_hbm(slope_one), vgg_small, vgg_second, feats, conv_mid, out_small
    )
    return finish(meta, parts, lpips, slope, *made)[None]


def solution(mesh):
    placed = (
        P(None, "row", "col", None),
        P(),
        P(),
        P(None, "row", "col", None),
        P(),
        P(),
        P(),
        P(),
        P(),
        P("col", None, None, None, None),
        P("col", None, None, None, None),
        P("col", None),
    )
    return jax.shard_map(
        local, mesh=mesh, in_specs=placed, out_specs=P(None, "row", "col", None), check_vma=False
    )
```

```python
import jax
import jax.numpy as jnp
import numpy as np
from jax import lax
from jax.experimental import pallas as pl
from jax.experimental.pallas import tpu as pltpu
from jax.sharding import PartitionSpec as P

BF = jnp.bfloat16
F32 = jnp.float32

LOSS_SCALE = 32.0
EPSILON = 1e-06
CROP = 256
TH, TW = 64, 32
IMG_H, IMG_W = 512, 1024
ROWS, COLS = 8, 32
CROPS = 64
DEC_HALO = 11
FEAT_HALO = 13
COL_HALO = 8
WIDE = TW + 2 * COL_HALO
TGT_HALO = 6
GRAD_PAD = 8
SHARE = 34
SPAN = 52
VMEM = 20 * 1024 * 1024


def sigmoid(v):
    return 0.5 * jnp.tanh(0.5 * v) + 0.5


def silu_parts(v):
    sig = sigmoid(v)
    act = v * sig
    return act, sig + act * (1.0 - sig)


def mm(a, b, ca=1, cb=0):
    return lax.dot_general(a, b, (((ca,), (cb,)), ((), ())), preferred_element_type=F32)


def iota(shape, dim):
    return lax.broadcasted_iota(jnp.int32, shape, dim)


def aligned(start, unit):
    return pl.multiple_of(start, unit) if not isinstance(start, int) else start


def conv_rows(src, row0, rows, weight, transposed=False, shift=0):
    n = rows * WIDE
    lhs = jnp.concatenate(
        [src[pl.ds(aligned((row0 + dy) * WIDE, 16), n), :] for dy in range(3)], axis=1
    )
    z = mm(lhs, weight, 1, 1 if transposed else 0)
    parts = []
    for dx in range(3):
        amount = (1 - dx - shift) % n
        part = z[:, dx * 128 : (dx + 1) * 128]
        parts.append(pltpu.roll(part, amount, 0) if amount else part)
    return parts[0] + parts[1] + parts[2]


def column_mask(col_first):
    x = col_first + iota((1, WIDE, 128), 1)
    return ((x >= 0) & (x < IMG_W)).astype(F32)


def keep_inside(v, row_first, rows, col_ok):
    y = row_first + iota((rows, 1, 128), 0)
    row_ok = ((y >= 0) & (y < IMG_H)).astype(F32)
    return (v.reshape(rows, WIDE, 128) * (col_ok * row_ok)).reshape(rows * WIDE, 128)


def planar_inside(row_first, col_first, low, high, rows, limit):
    lane = iota((rows * 8, 128), 1)
    row = iota((rows * 8, 128), 0) >> 3
    x = col_first + lane
    y = row_first + row
    ok = (x >= 0) & (x < IMG_W) & (lane >= low) & (lane < high) & (y >= 0) & (y < IMG_H)
    return ok & (row < limit)


def wider(v):
    return jnp.concatenate([v, jnp.zeros((v.shape[0], 128 - v.shape[1]), F32)], axis=1)


def taller(v):
    return jnp.concatenate([v, jnp.zeros((128 - v.shape[0], 128), F32)], axis=0)


def colour_weights(w, small):
    k = iota((32, 384), 0)
    n = iota((32, 384), 1)
    copies = (((n >> 7) * 8 + (n & 7)) == k).astype(F32).astype(BF)
    for dy in range(3):
        w[dy * 128 : (dy + 1) * 128, :] = mm(small(dy).astype(BF), copies, 0, 0).astype(BF)


def to_colours(src, first, w):
    group = iota((WIDE, 128), 1) >> 3
    tile = jnp.zeros((WIDE, 128), F32)
    for half in range(2):
        v = conv_rows(src, first + half * 8, 8, w[...])
        for k in range(8):
            tile = jnp.where(group == half * 8 + k, v[k * WIDE : (k + 1) * WIDE], tile)
    return taller(tile).T


def patch_tile(v):
    after, before = pltpu.roll(v, 1, 1), pltpu.roll(v, 127, 1)
    none = jnp.zeros((8, 128), F32)
    parts = []
    for k in range(4):
        at = slice(k * 8, (k + 1) * 8)
        parts += [after[at], v[at], before[at], none]
    return jnp.concatenate(parts, axis=0).T[0:WIDE].astype(BF)


def patch_weights(w, small):
    w[...] = jnp.zeros(w.shape, BF)
    for k in range(4):
        for dy in range(3):
            w[(k + dy) * 32 : (k + dy + 1) * 32, k * 128 : (k + 1) * 128] = small(dy).astype(BF)


def from_colours(px, tile, count, w):
    at = [pl.ds(aligned((tile + k) * WIDE, 16), count * WIDE) for k in range(2)]
    return mm(jnp.concatenate([px[at[0], :], px[at[1], :]], axis=1), w[...])


def pack_rows_kernel(feats, target, low, high, own):
    lane = iota((TW, 128), 1)
    n = TGT_HALO
    colours = [wider(target[k].astype(F32)) for k in range(3)]
    for k in range(3):
        own[k] = colours[k].astype(BF)
    for out, y0, t0 in ((low, TH - FEAT_HALO, TH - n), (high, 0, 0)):
        extra = jnp.zeros((TW, 128), F32)
        for k in range(3):
            amount = (n * k - t0) % 128
            moved = pltpu.roll(colours[k], amount, 1) if amount else colours[k]
            extra = jnp.where((lane >= n * k) & (lane < n * k + n), moved, extra)
        out[0:FEAT_HALO] = feats[y0 : y0 + FEAT_HALO]
        out[FEAT_HALO] = extra.astype(BF)


def pack_sides_kernel(feats, own, top, bot, side_l, side_r, tall):
    lane = iota((TW, 128), 1)
    n = TGT_HALO
    above, below = top[FEAT_HALO].astype(F32), bot[FEAT_HALO].astype(F32)
    colours = []
    for k in range(3):
        first = pltpu.roll(above, 128 - n * k, 1) if k else above
        last = pltpu.roll(below, n + TH - n * k, 1)
        v = jnp.where(lane < n, first, pltpu.roll(own[k].astype(F32), n, 1))
        v = jnp.where(lane < n + TH, v, jnp.where(lane < 2 * n + TH, last, 0.0))
        tall[k] = v.astype(BF)
        colours.append(v)
    parts = (
        (0, top[0:FEAT_HALO]),
        (FEAT_HALO, feats[...]),
        (FEAT_HALO + TH, bot[0:FEAT_HALO]),
        (2 * FEAT_HALO + TH, jnp.stack(colours)),
    )
    for y, v in parts:
        v = v.astype(F32)
        for out, x0 in ((side_l, TW - COL_HALO), (side_r, 0)):
            out[y : y + v.shape[0]] = v[:, x0 : x0 + COL_HALO, :].astype(BF)


def decode_kernel(
    meta, top, mid, bot, left, right, w_mid, w_out, pay, dec, slope_out, s1, s2, w, w3
):
    r, c = meta[0], meta[1]
    for dy in range(3):
        for dx in range(3):
            w[dy * 128 : (dy + 1) * 128, dx * 128 : (dx + 1) * 128] = w_mid[dy, dx]
    colour_weights(w3, lambda dy: w_out[dy])

    def fill(first, rows, centre):
        n = rows * WIDE
        parts = [left[pl.ds(first, rows)], centre, right[pl.ds(first, rows)]]
        v = jnp.concatenate([p.astype(F32) for p in parts], axis=1).reshape(n, 128)
        s1[pl.ds(aligned(first * WIDE, 16), n), :] = (v * sigmoid(v)).astype(BF)

    fill(0, FEAT_HALO, top[0:FEAT_HALO])
    fill(FEAT_HALO + TH, FEAT_HALO, bot[0:FEAT_HALO])

    def fill_mid(i, carry):
        fill(FEAT_HALO + i * 8, 8, mid[pl.ds(i * 8, 8)])
        return carry

    lax.fori_loop(0, TH // 8, fill_mid, 0, unroll=2)
    col_ok = column_mask(c * TW - COL_HALO)

    def middle(i, carry):
        v = conv_rows(s1, i * 8, 8, w[...])
        act, slope = silu_parts(v)
        act = keep_inside(act, r * TH - 12 + i * 8, 8, col_ok)
        s2[pl.ds(aligned(i * 8 * WIDE, 16), 8 * WIDE), :] = act.astype(BF)
        slope = pltpu.roll(slope, 8 * WIDE - 6, 0).reshape(8, WIDE, 128).astype(BF)
        first, last = max(i * 8, 11), min(i * 8 + 8, 79)
        if first < last:
            slope_out[first - 11 : last - 11] = slope[first - i * 8 : last - i * 8]
        return carry

    for i in range(11):
        middle(i, 0)
    s2[88 * WIDE :, :] = jnp.zeros((10 * WIDE, 128), BF)
    dec[768:, :] = jnp.zeros((256, 128), F32)

    def colours(i, carry):
        v = to_colours(s2, i * 16, w3)
        ok = planar_inside(
            r * TH - DEC_HALO + i * 16, c * TW - COL_HALO, 2, WIDE - 2, 16, 86 - i * 16
        )
        dec[pl.ds(aligned(i * 128, 128), 128), :] = jnp.where(ok, v, 0.0).astype(BF).astype(F32)
        return carry

    lax.fori_loop(0, 6, colours, 0, unroll=True)
    planes = [
        dec[pl.ds(k, 128, stride=8), :].T[COL_HALO : COL_HALO + TW, :] for k in range(3)
    ]
    lane = iota((8, 128), 1)
    for half in range(2):
        tiles = [jnp.zeros((8, 128), F32) for _ in range(5)]
        for g in range(4):
            for k in range(3):
                piece = planes[k][g * 8 : (g + 1) * 8]
                if half:
                    piece = pltpu.roll(piece, 128 - SHARE, 1)
                piece = jnp.where(lane < SPAN, piece, 0.0)
                at, off = divmod((g * 3 + k) * SPAN, 128)
                if off:
                    piece = pltpu.roll(piece, off, 1)
                tiles[at] = tiles[at] + jnp.where(lane >= off, piece, 0.0)
                if off + SPAN > 128:
                    tiles[at + 1] = tiles[at + 1] + jnp.where(lane < off, piece, 0.0)
        packed = jnp.concatenate(tiles, axis=1).astype(BF)
        for k in range(COLS // 2):
            pay[2 * k + half] = packed


def percept_kernel(
    meta, dec, tall, left, right, v_first, v_second, weights, feat, slope_one, done,
    planes, px, one, w1, w2,
):
    r, c = meta[0], meta[1]
    col_first = c * TW - COL_HALO
    col_ok = column_mask(col_first)

    def first_small(dy):
        v = v_first[dy]
        return v + pltpu.roll(pltpu.roll(v, 3, 0), 64, 1)

    patch_weights(w1, first_small)
    for dy in range(3):
        for dx in range(3):
            v = v_second[dy, dx].astype(F32)
            v = jnp.concatenate([v, jnp.zeros((64, 64), F32)], axis=1)
            u = pltpu.roll(v, 64, 1)
            w2[dy * 128 : (dy + 1) * 128, dx * 128 : (dx + 1) * 128] = jnp.concatenate(
                [v, u], axis=0
            ).astype(BF)

    planes[...] = jnp.zeros(planes.shape, F32)
    for k in range(3):
        v = jnp.concatenate(
            [a.astype(F32) for a in (left[90 + k], tall[k], right[90 + k])], axis=0
        )
        planes[pl.ds(3 + k, 80, stride=8), :] = taller(v).T[0:80]

    done[...] = jnp.zeros((8, 128), F32)

    def gather(i, carry):
        v = dec[pl.ds(aligned(i * 32 + 40, 8), 32), :] + planes[pl.ds(aligned(i * 32, 32), 32), :]
        px[pl.ds(aligned(i * WIDE, 16), WIDE), :] = patch_tile(v)
        return carry

    lax.fori_loop(0, 19, gather, 0, unroll=True)
    px[19 * WIDE :, :] = jnp.zeros((WIDE, 128), BF)

    def first(tile, count):
        v = from_colours(px, tile, count, w1)
        for j in range(count):
            for k in range(4):
                p = (tile + j) * 4 + k
                x = v[j * WIDE : (j + 1) * WIDE, k * 128 : (k + 1) * 128]
                act, slope = silu_parts(x)
                act = keep_inside(act, r * TH - 5 + p, 1, col_ok)
                slope_one[pl.ds(aligned(p * WIDE, 16), WIDE), :] = slope.astype(BF)
                one[pl.ds(aligned(p * WIDE, 16), WIDE), :] = act.astype(BF)

    def first_group(i, carry):
        first(i * 4, 4)
        return carry

    lax.fori_loop(0, 4, first_group, 0, unroll=True)
    first(16, 3)
    ones = ((iota((128, 128), 0) >> 6) == (iota((128, 128), 1) >> 6)).astype(F32).astype(BF)

    def half_sum(v):
        return mm(v.astype(BF), ones)

    def second(i, carry):
        v = conv_rows(one, i * 8, 8, w2[...])
        f, slope = silu_parts(v)
        scale = lax.rsqrt(half_sum(f * f) + EPSILON)
        unit = f * scale
        weighted = weights[...] * (unit - pltpu.roll(unit, 64, 1))
        g = scale * (weighted - unit * half_sum(weighted * unit)) * slope
        g = keep_inside(g, r * TH - 4 + i * 8, 8, col_ok)
        feat[pl.ds(aligned(i * 8 * WIDE, 16), 8 * WIDE), :] = g.astype(BF)
        return carry

    lax.fori_loop(0, 9, second, 0, unroll=3)


def percept_back_kernel(
    meta, feat, slope_one, v_first, v_second, feats, w_mid, out, feats_slope, w,
    bv, w3, w4,
):
    r, c = meta[0], meta[1]
    col_ok = column_mask(c * TW - COL_HALO)

    def last_small(dy):
        parts = [v_first[2 - dy, (2 - dx) * 8 : (3 - dx) * 8, :] for dx in range(3)]
        return jnp.concatenate(parts + [jnp.zeros((8, 128), F32)], axis=0)

    colour_weights(w4, last_small)
    for dy in range(3):
        for dx in range(3):
            w[dx * 128 : (dx + 1) * 128, dy * 128 : (dy + 1) * 128] = w_mid[2 - dy, 2 - dx]

    def feature_slope(i, carry):
        at = pl.ds(i * 8, 8)
        feats_slope[at] = silu_parts(feats[at].astype(F32))[1].astype(BF)
        return carry

    lax.fori_loop(0, TH // 8, feature_slope, 0, unroll=2)
    for dy in range(3):
        for dx in range(3):
            v = v_second[dy, dx].astype(F32)
            v = jnp.concatenate([v, jnp.zeros((64, 64), F32)], axis=1)
            w3[(2 - dx) * 128 : (3 - dx) * 128, (2 - dy) * 128 : (3 - dy) * 128] = jnp.concatenate(
                [v, jnp.zeros((64, 128), F32)], axis=0
            ).astype(BF)

    def back(i, carry):
        v = conv_rows(feat, i * 10, 10, w3[...], transposed=True)
        x = slope_one[pl.ds(aligned((i * 10 + 2) * WIDE, 16), 10 * WIDE), :]
        v = keep_inside(v * x.astype(F32), r * TH - 3 + i * 10, 10, col_ok)
        bv[pl.ds(aligned(i * 10 * WIDE, 16), 10 * WIDE), :] = v.astype(BF)
        return carry

    lax.fori_loop(0, 7, back, 0, unroll=True)
    bv[70 * WIDE :, :] = jnp.zeros((12 * WIDE, 128), BF)

    def colours(i, carry):
        v = to_colours(bv, i * 16, w4)
        out[pl.ds(aligned(i * 128, 128), 128), :] = pltpu.roll(v, 122, 1)
        return carry

    lax.fori_loop(0, 5, colours, 0, unroll=True)


STOP = object()
FAR = 16
STEPS = 6
HALF = STEPS + 1
TILES = 2 * HALF
LANES = TILES * 128
EVEN = HALF * 128


def critic_kernel(
    meta, strip, mine, other, far, far_other, _, out,
    strip32, grads, w_pre, w_one, w_two, w_back, score, distance, row_gap, row_gap_back, *rest,
):
    x_all, pre, act, two, cols = (rest[k * 4 : (k + 1) * 4] for k in range(5))
    jobs = rest[20]
    r, me = meta[0], meta[1]
    first_row = r * TH - 2 + SHARE * (me & 1)
    lane = iota((1, 128), 1)
    upper = lane >= 64
    first_x = (lane & 63) == 0
    last_x = (lane & 63) == 63

    def unpack(k, carry):
        v = strip[k].astype(F32)

        def piece(g, j, place):
            at, off = divmod((g * 3 + j) * SPAN, 128)
            amount = (place - off) % 128
            parts = [v[:, at * 128 : (at + 1) * 128]]
            if off + SPAN > 128:
                parts.append(v[:, (at + 1) * 128 : (at + 2) * 128])
            parts = [pltpu.roll(p, amount, 1) if amount else p for p in parts]
            if len(parts) == 1:
                return parts[0]
            return jnp.where(lane < place + 128 - off, parts[0], parts[1])

        for g in range(4):
            both = jnp.where(upper, piece(g, 1, 64), piece(g, 0, 0))
            row = jnp.concatenate([both, piece(g, 2, 0)], axis=1)
            strip32[pl.ds(aligned(k * TW + g * 8, 8), 8), :] = row
        return carry

    lax.fori_loop(0, COLS, unpack, 0, unroll=16)
    strip32[IMG_W:, :] = jnp.zeros((8, 256), F32)
    grads[...] = jnp.zeros(grads.shape, F32)
    w_back[...] = jnp.zeros(w_back.shape, BF)
    for g, source in enumerate((mine, other, far, far_other)):
        w_one[g] = source[1024:1120, :]
        w_pre[g] = (0.5 * taller(source[1024:1120, :].astype(F32))).T.astype(BF)
        score[g] = taller(source[1120:1136, :].astype(F32)).T
        for i in range(4):
            first, second = (
                source[i * 256 + k * 128 : i * 256 + (k + 1) * 128, :].astype(F32).T
                for k in range(2)
            )
            at = slice((i // 2) * 128, (i // 2 + 1) * 128)
            w_two[g, i % 2, 0:128, at] = jnp.where(upper, first, second).astype(BF)
            w_two[g, i % 2, 128:256, at] = jnp.where(upper, 0.0, first).astype(BF)
            w_two[g, i % 2, 256:384, at] = jnp.where(upper, second, 0.0).astype(BF)
        for par in range(2):
            for p in range(2):
                for t in range(2):
                    i = par + 2 * t
                    for kind, j in ((0, 1 + p), (1 + p, 3 - 3 * p)):
                        w_back[
                            g,
                            (par * 2 + 1 - p) * 64 : (par * 2 + 2 - p) * 64,
                            (t * 3 + kind) * 128 : (t * 3 + kind + 1) * 128,
                        ] = 0.5 * source[i * 256 + j * 64 : i * 256 + (j + 1) * 64, :]
    for t in two:
        t[:, 0:128] = jnp.zeros((384, 128), BF)
        t[:, (STEPS + 1) * 128 :] = jnp.zeros((384, 128), BF)
    for t in cols:
        t[192:, :] = jnp.zeros((64, 384), F32)
    x, n = iota((CROP + 8, 384), 0), iota((CROP + 8, 384), 1)
    wanted = 4 * (n & 63) + (n >> 6) - 1
    wanted_ok = (wanted >= 0) & (wanted < CROP)
    distance[...] = jnp.where(wanted_ok, x - wanted, -1).astype(F32)

    def gap(dims, rho, n):
        tile, i, k = rho >> 4, (rho >> 2) & 3, rho & 3
        u = 2 * jnp.where(tile >= HALF, tile - HALF, tile) + jnp.where(tile >= HALF, 1, 0)
        return jnp.where(k < 3, n - (k * 40 + 2 * u + i), -1).astype(F32)

    dims = (TILES * 16, 128)
    row_gap[...] = gap(dims, iota(dims, 0), iota(dims, 1))
    dims = (128, TILES * 16)
    row_gap_back[...] = gap(dims, iota(dims, 1), iota(dims, 0))
    wide = iota((1, 256), 1)

    def anchor(q, k):
        return meta[2 + 2 * q + k]

    def owner_of(q):
        return meta[2 + 2 * CROPS + q]

    def job(q, x_all, pre, act, two, cols):
        top, left, apart = anchor(q, 0), anchor(q, 1), owner_of(q) ^ me
        g = (apart & 1) + 2 * ((apart // FAR) & 1)
        y0 = first_row - top
        v0 = lax.shift_right_arithmetic(y0 - 3, 2)
        e = 4 * v0 - y0 + 6
        crop_row = y0 - 9 + (wide & 63)
        in_crop = (crop_row >= 0) & (crop_row < CROP) & (wide < 192)
        here = pl.ds(aligned((left >> 3) * 8, 8), CROP + 8)
        window = jnp.where(in_crop, strip32[here, :], 0.0).astype(BF)
        pick = jnp.where(distance[...] == (left & 7).astype(F32), 1.0, 0.0).astype(BF)
        cols_of = mm(window, pick, 0, 0)
        none = jnp.zeros((8, 384), F32)
        halves = [
            jnp.concatenate(
                [cols_of[k * 64 + 24 * h : k * 64 + 24 * h + 40, :] for k in range(3)] + [none],
                axis=0,
            )
            for h in range(2)
        ]
        mixed = []
        for m in range(6):
            tile = slice((m // 2) * 128, (m // 2 + 1) * 128)
            low, high = halves[0][:, tile], halves[1][:, tile]
            if m % 2 == 0:
                high = pltpu.roll(high, 64, 1)
            else:
                low = pltpu.roll(low, 64, 1)
            mixed.append(jnp.where(upper, high, low))
        yield
        chosen = jnp.where(row_gap[...] == e.astype(F32), 1.0, 0.0).astype(BF)
        patches = mm(chosen, jnp.concatenate(mixed, axis=1).astype(BF)).astype(BF)
        for t in range(TILES):
            for m in range(6):
                x_all[m * 16 : (m + 1) * 16, t * 128 : (t + 1) * 128] = patches[
                    t * 16 : (t + 1) * 16, m * 128 : (m + 1) * 128
                ]
        yield
        weight = w_pre[g][:, 0:96]
        for t0 in range(0, TILES, 2):
            at = slice(t0 * 128, (t0 + 2) * 128)
            value = mm(weight, x_all[:, at])
            for t in range(t0, t0 + 2):
                at = slice(t * 128, (t + 1) * 128)
                n = 2 * (t % HALF) + t // HALF + jnp.where(upper, 2 * STEPS, 0)
                u = 2 * v0 - 1 + n
                ok = ((u >= 0) & (u < CROP // 2)).astype(F32)
                half = value[:, (t - t0) * 128 : (t - t0 + 1) * 128]
                rise = jnp.tanh(half) + 1.0
                kept = rise * ok
                pre[:, at] = kept * (1.0 + half * (2.0 - rise))
                act[:, at] = (half * kept).astype(BF)
            yield
        column = score[g][:, 0:1]
        for t0 in range(0, STEPS, 2):
            value = 0.0
            for par in range(2):
                at = par * EVEN + t0 * 128
                taps = jnp.concatenate(
                    [act[:, at : at + 256], act[:, at + 128 : at + 384]], axis=0
                )
                value = value + mm(w_two[g, par], taps)
            for t in range(t0, t0 + 2):
                at = slice((t - t0) * 128, (t - t0 + 1) * 128)
                f = value[0:128, at]
                f = f + jnp.where(first_x, 0.0, pltpu.roll(value[128:256, at], 1, 1))
                f = f + jnp.where(last_x, 0.0, pltpu.roll(value[256:384, at], 127, 1))
                f, slope = silu_parts(f)
                logit = jnp.sum(f * column, axis=0, keepdims=True)
                v = v0 + t + jnp.where(upper, STEPS, 0)
                ok = (v >= 0) & (v < CROP // 4)
                grad = jnp.where(ok, -LOSS_SCALE * sigmoid(-logit), 0.0)
                b = grad * (column * slope)
                at = slice((t + 1) * 128, (t + 2) * 128)
                two[0:128, at] = b.astype(BF)
                two[128:256, at] = jnp.where(first_x, 0.0, pltpu.roll(b, 1, 1)).astype(BF)
                two[256:384, at] = jnp.where(last_x, 0.0, pltpu.roll(b, 127, 1)).astype(BF)
            yield
        for s0 in range(0, HALF, 2):
            n = min(2, HALF - s0) * 128
            at = s0 * 128
            both = jnp.concatenate([two[:, 128 + at : 128 + at + n], two[:, at : at + n]], axis=0)
            up = mm(w_back[g], both)
            for par in range(2):
                here = slice(par * EVEN + at, par * EVEN + at + n)
                one = (up[par * 128 : (par + 1) * 128] * pre[:, here]).astype(BF)
                x_all[:, here] = mm(w_one[g], one).astype(BF)
            yield
        spread = jnp.concatenate(
            [
                jnp.concatenate(
                    [
                        x_all[m * 16 : (m + 1) * 16, t * 128 : (t + 1) * 128]
                        for t in range(TILES)
                    ],
                    axis=0,
                )
                for m in range(6)
            ],
            axis=1,
        )
        chosen = jnp.where(row_gap_back[...] == e.astype(F32), 1.0, 0.0).astype(BF)
        back = mm(chosen, spread)
        yield
        parts = []
        for h in range(2):
            tiles = []
            for k in range(3):
                low = back[:, 2 * k * 128 : (2 * k + 1) * 128]
                high = back[:, (2 * k + 1) * 128 : (2 * k + 2) * 128]
                if h == 0:
                    high = pltpu.roll(high, 64, 1)
                else:
                    low = pltpu.roll(low, 64, 1)
                tiles.append(jnp.where(upper, high, low))
            parts.append(jnp.concatenate(tiles, axis=1))
        for k in range(3):
            low, high = (part[k * 40 : (k + 1) * 40, :] for part in parts)
            cols[k * 64 : (k + 1) * 64, :] = jnp.concatenate(
                [low[0:24], low[24:40] + high[0:16], high[16:40]], axis=0
            )
        yield
        placed = mm(pick, cols[...].astype(BF), 1, 1)
        y = wide & 63
        keep = in_crop & (y >= 9) & (y < 9 + SHARE)
        yield
        here = pl.ds(aligned((left >> 3) * 8 + GRAD_PAD, 8), CROP + 8)
        grads[here, :] = grads[here, :] + jnp.where(keep, placed, 0.0)

    count, seen, turn = jnp.int32(0), jnp.int32(0), (me // FAR) & 1
    for q in range(CROPS):
        y0 = first_row - anchor(q, 0)
        shared = ((owner_of(q) ^ me) & (COLS - 2 - FAR)) == 0
        shared = (shared & (y0 < CROP) & (y0 + SHARE > 0)).astype(jnp.int32)
        jobs[count] = q
        count = count + shared * ((seen & 1) == turn).astype(jnp.int32)
        seen = seen + shared

    sets = tuple(zip(x_all, pre, act, two, cols))

    def crops(first, number):
        running = [job(jobs[first + k], *sets[k]) for k in range(number)]
        while running:
            running = [g for g in running if next(g, STOP) is not STOP]

    def four_crops(k, carry):
        crops(4 * k, 4)
        return carry

    lax.fori_loop(0, count >> 2, four_crops, 0)

    @pl.when((count & 2) == 2)
    def _():
        crops((count >> 2) * 4, 2)

    @pl.when((count & 1) == 1)
    def _():
        crops(count - 1, 1)

    def pack(k, carry):
        block = grads[pl.ds(aligned(k * TW, 32), 48), :][GRAD_PAD - 2 : GRAD_PAD + 38]
        a, b = block[:, 0:128], block[:, 128:256]
        out[k] = jnp.where(
            lane < 40,
            pltpu.roll(a, 128 - 9, 1),
            jnp.where(lane < 80, pltpu.roll(a, 128 - 33, 1), pltpu.roll(b, 71, 1)),
        ).astype(BF)
        return carry

    lax.fori_loop(0, COLS, pack, 0, unroll=8)


def finish_kernel(
    meta, parts, lpips, slope, feats_slope, w, w_out, out, turned, planes, px, bm, w1
):
    r, c = meta[0], meta[1]
    def small(dy):
        flipped = [w_out[2 - dy, (2 - dx) * 8 : (3 - dx) * 8, :] for dx in range(3)]
        return jnp.concatenate(flipped + [jnp.zeros((8, 128), F32)], axis=0)

    patch_weights(w1, small)
    col_ok = column_mask(c * TW - 2)
    planes[...] = jnp.zeros(planes.shape, F32)
    for half in range(2):
        total = parts[half].astype(F32)
        for k in range(1, COLS // 2):
            total = total + parts[2 * k + half].astype(F32)
        turned[...] = taller(total).T
        for k in range(3):
            planes[pl.ds(half * SHARE * 8 + k, 40, stride=8), :] = turned[k * 40 : (k + 1) * 40, :]

    def gather(i, carry):
        at = pl.ds(aligned(i * 32, 32), 32)
        ok = planar_inside(r * TH - 2 + i * 4, c * TW - 2, 0, 36, 4, 4)
        px[pl.ds(aligned(i * WIDE, 16), WIDE), :] = patch_tile(
            jnp.where(ok, lpips[at, :] + planes[at, :], 0.0)
        )
        return carry

    lax.fori_loop(0, 17, gather, 0, unroll=True)
    px[17 * WIDE :, :] = jnp.zeros((WIDE, 128), BF)

    def middle(tile, count):
        v = from_colours(px, tile, count, w1)
        for j in range(count):
            for k in range(4):
                n = (tile + j) * 4 + k
                x = v[j * WIDE : (j + 1) * WIDE, k * 128 : (k + 1) * 128]
                x = keep_inside(x * slope[n].astype(F32), r * TH - 1 + n, 1, col_ok)
                bm[pl.ds(aligned(n * WIDE, 16), WIDE), :] = x.astype(BF)

    def middle_group(i, carry):
        middle(i * 4, 4)
        return carry

    lax.fori_loop(0, 4, middle_group, 0, unroll=True)
    middle(16, 1)

    def last(i, carry):
        v = conv_rows(bm, i * 8, 8, w[...], transposed=True, shift=2)
        v = v.reshape(8, WIDE, 128)[:, 0:TW, :]
        at = pl.ds(i * 8, 8)
        out[at] = (v * feats_slope[at].astype(F32)).astype(BF)
        return carry

    lax.fori_loop(0, TH // 8, last, 0, unroll=True)


def call(kernel, outs, scratch, args, scalars=1, unused=0, lists=(), vmem=VMEM):
    specs = [pl.BlockSpec(memory_space=pltpu.SMEM)] * scalars
    specs += [pl.BlockSpec(memory_space=pltpu.VMEM)] * (len(args) - scalars - unused)
    specs += [pl.BlockSpec(memory_space=pl.ANY)] * unused
    return pl.pallas_call(
        kernel,
        in_specs=specs,
        out_specs=jax.tree.map(lambda _: pl.BlockSpec(memory_space=pltpu.VMEM), outs),
        out_shape=outs,
        scratch_shapes=[pltpu.VMEM(s, t) for s, t in scratch] + list(lists),
        compiler_params=pltpu.CompilerParams(vmem_limit_bytes=vmem),
        interpret=INTERPRET,
    )(*args)


INTERPRET = False


def shape(dims, kind):
    return jax.ShapeDtypeStruct(dims, kind)


def colour_first(w):
    w = jnp.pad(w.astype(F32), ((0, 0), (0, 1), (0, 5), (0, 128 - w.shape[-1])))
    return w.reshape(3, 32, 128)


def decode(meta, top, mid, bot, left, right, conv_mid, small):
    return call(
        decode_kernel,
        (
            shape((COLS, TW // 4, 640), BF),
            shape((1024, 128), F32),
            pltpu.HBM((68, WIDE, 128), BF),
        ),
        [((90 * WIDE, 128), BF), ((98 * WIDE, 128), BF), ((384, 384), BF), ((384, 384), BF)],
        (meta, top, mid, bot, left, right, conv_mid, small),
    )


def percept(meta, dec, tall, left, right, small, vgg_second, weights):
    scaled = jnp.pad(2.0 * LOSS_SCALE * weights, (0, 64)).reshape(1, 128)
    return call(
        percept_kernel,
        (
            pltpu.HBM((72 * WIDE, 128), BF),
            pltpu.HBM((76 * WIDE, 128), BF),
            shape((8, 128), F32),
        ),
        [
            ((80 * 8, 128), F32),
            ((20 * WIDE, 128), BF),
            ((76 * WIDE, 128), BF),
            ((256, 512), BF),
            ((384, 384), BF),
        ],
        (meta, dec, tall, left, right, small, vgg_second, scaled),
    )


def percept_back(meta, feat, slope_one, small, vgg_second, feats, conv_mid):
    return call(
        percept_back_kernel,
        (
            shape((80 * 8, 128), F32),
            shape((TH, TW, 128), BF),
            shape((384, 384), BF),
        ),
        [((82 * WIDE, 128), BF), ((384, 384), BF), ((384, 384), BF)],
        (meta, feat, slope_one, small, vgg_second, feats, conv_mid),
    )


def critic_weights(first, second, score):
    w = jnp.pad(first, ((0, 0), (0, 0), (0, 1), (0, 0)))
    w = jnp.transpose(w, (1, 0, 2, 3)).reshape(4, 16, 64)
    w = jnp.concatenate(
        [jnp.pad(w, ((2, 0), (0, 0), (0, 0))), jnp.pad(w, ((0, 2), (0, 0), (0, 0)))], -1
    ).reshape(96, 128)
    score = jnp.pad(score[None], ((0, 15), (0, 0)))
    return jnp.concatenate([second.reshape(1024, 128), w, score], 0)


def critics(meta, strip, weights, after):
    pair = [
        ((96, LANES), BF),
        ((128, LANES), F32),
        ((128, LANES), BF),
        ((384, (STEPS + 2) * 128), BF),
        ((256, 384), F32),
    ]
    return call(
        critic_kernel,
        shape((COLS, 40, 128), BF),
        [
            ((IMG_W + 8, 256), F32),
            ((IMG_W + 24, 256), F32),
            ((4, 128, 128), BF),
            ((4, 96, 128), BF),
            ((4, 2, 384, 256), BF),
            ((4, 256, 768), BF),
            ((4, 128, 128), F32),
            ((CROP + 8, 384), F32),
            ((TILES * 16, 128), F32),
            ((128, TILES * 16), F32),
        ]
        + [buffer for buffer in pair for _ in range(4)],
        (meta, strip, *weights, after),
        unused=1,
        lists=[pltpu.SMEM((CROPS,), jnp.int32)],
        vmem=30 * 1024 * 1024,
    )


def finish(meta, parts, lpips, slope, feats_slope, w, small):
    return call(
        finish_kernel,
        shape((TH, TW, 128), BF),
        [
            ((128, 128), F32),
            ((80 * 8, 128), F32),
            ((18 * WIDE, 128), BF),
            ((68 * WIDE, 128), BF),
            ((256, 512), BF),
        ],
        (meta, parts, lpips, slope, feats_slope, w, small),
    )


def in_hbm(x):
    return pltpu.with_memory_space_constraint(x, pltpu.HBM)


def exchange(low, high, axis):
    count = lax.axis_size(axis)
    forward = [(i, i + 1) for i in range(count - 1)]
    backward = [(target, source) for source, target in forward]
    return lax.ppermute(low, axis, forward), lax.ppermute(high, axis, backward)


def local(
    features, conv_mid, conv_out, target, vgg_first, vgg_second, perceptual_weights,
    crop_anchors, crop_owner, critic_first, critic_second, critic_score,
):
    meta = jnp.concatenate(
        [
            jnp.stack([lax.axis_index("row"), lax.axis_index("col")]).astype(jnp.int32),
            crop_anchors.reshape(2 * CROPS),
            crop_owner.reshape(CROPS),
        ]
    )
    feats = features[0]
    planar = jnp.transpose(target[0], (2, 1, 0))

    low, high, own = call(
        pack_rows_kernel,
        (shape((FEAT_HALO + 1, TW, 128), BF),) * 2 + (shape((3, TW, 128), BF),),
        [],
        (in_hbm(feats), in_hbm(planar)),
        scalars=0,
    )
    top, bot = exchange(low, high, "row")
    side_l, side_r, tall = call(
        pack_sides_kernel,
        (shape((2 * FEAT_HALO + TH + 3, COL_HALO, 128), BF),) * 2 + (shape((3, TW, 128), BF),),
        [],
        (feats, own, top, bot),
        scalars=0,
    )
    left, right = exchange(side_l, side_r, "col")
    out_small = colour_first(jnp.transpose(conv_out, (0, 1, 3, 2)))
    vgg_small = colour_first(vgg_first)
    mine = critic_weights(critic_first[0], critic_second[0], critic_score[0])
    left, right, sent, meta, out_small = lax.optimization_barrier(
        (left, right, mine, meta, out_small)
    )
    far = lax.ppermute(sent, "col", [(i, i ^ FAR) for i in range(COLS)])
    pay, dec, slope = decode(meta, top, feats, bot, left, right, conv_mid, out_small)
    pay, far = lax.optimization_barrier((pay, far))
    strip = lax.all_to_all(pay, "col", split_axis=0, concat_axis=0, tiled=True)
    other = lax.ppermute(mine, "col", [(i, i ^ 1) for i in range(COLS)])
    far_other = lax.ppermute(far, "col", [(i, i ^ 1) for i in range(COLS)])
    feat, slope_one, done = percept(
        meta, dec, tall, left, right, vgg_small, vgg_second, perceptual_weights
    )
    grads = critics(meta, strip, (mine, other, far, in_hbm(far_other)), done)
    parts = lax.all_to_all(grads, "col", split_axis=0, concat_axis=0, tiled=True)
    lpips, *made = percept_back(
        meta, in_hbm(feat), in_hbm(slope_one), vgg_small, vgg_second, feats, conv_mid
    )
    return finish(meta, parts, lpips, slope, *made, out_small)[None]


def solution(mesh):
    placed = (
        P(None, "row", "col", None),
        P(),
        P(),
        P(None, "row", "col", None),
        P(),
        P(),
        P(),
        P(),
        P(),
        P("col", None, None, None, None),
        P("col", None, None, None, None),
        P("col", None),
    )
    return jax.shard_map(
        local, mesh=mesh, in_specs=placed, out_specs=P(None, "row", "col", None), check_vma=False
    )
```

```python
import jax
import jax.numpy as jnp
import numpy as np
from jax import lax
from jax.experimental import pallas as pl
from jax.experimental.pallas import tpu as pltpu
from jax.sharding import PartitionSpec as P

BF = jnp.bfloat16
F32 = jnp.float32

LOSS_SCALE = 32.0
EPSILON = 1e-06
CROP = 256
TH, TW = 64, 32
IMG_H, IMG_W = 512, 1024
ROWS, COLS = 8, 32
CROPS = 64
DEC_HALO = 11
FEAT_HALO = 13
COL_HALO = 8
WIDE = TW + 2 * COL_HALO
TGT_HALO = 6
GRAD_PAD = 8
SHARE = 34
SPAN = 52
VMEM = 20 * 1024 * 1024


def sigmoid(v):
    return 0.5 * jnp.tanh(0.5 * v) + 0.5


def silu_parts(v):
    sig = sigmoid(v)
    act = v * sig
    return act, sig + act * (1.0 - sig)


def mm(a, b, ca=1, cb=0):
    return lax.dot_general(a, b, (((ca,), (cb,)), ((), ())), preferred_element_type=F32)


def iota(shape, dim):
    return lax.broadcasted_iota(jnp.int32, shape, dim)


def aligned(start, unit):
    return pl.multiple_of(start, unit) if not isinstance(start, int) else start


def conv_rows(src, row0, rows, weight, transposed=False, shift=0):
    n = rows * WIDE
    lhs = jnp.concatenate(
        [src[pl.ds(aligned((row0 + dy) * WIDE, 16), n), :] for dy in range(3)], axis=1
    )
    z = mm(lhs, weight, 1, 1 if transposed else 0)
    parts = []
    for dx in range(3):
        amount = (1 - dx - shift) % n
        part = z[:, dx * 128 : (dx + 1) * 128]
        parts.append(pltpu.roll(part, amount, 0) if amount else part)
    return parts[0] + parts[1] + parts[2]


def column_mask(col_first):
    x = col_first + iota((1, WIDE, 128), 1)
    return ((x >= 0) & (x < IMG_W)).astype(F32)


def keep_inside(v, row_first, rows, col_ok):
    y = row_first + iota((rows, 1, 128), 0)
    row_ok = ((y >= 0) & (y < IMG_H)).astype(F32)
    return (v.reshape(rows, WIDE, 128) * (col_ok * row_ok)).reshape(rows * WIDE, 128)


def planar_inside(row_first, col_first, low, high, rows, limit):
    lane = iota((rows * 8, 128), 1)
    row = iota((rows * 8, 128), 0) >> 3
    x = col_first + lane
    y = row_first + row
    ok = (x >= 0) & (x < IMG_W) & (lane >= low) & (lane < high) & (y >= 0) & (y < IMG_H)
    return ok & (row < limit)


def wider(v):
    return jnp.concatenate([v, jnp.zeros((v.shape[0], 128 - v.shape[1]), F32)], axis=1)


def taller(v):
    return jnp.concatenate([v, jnp.zeros((128 - v.shape[0], 128), F32)], axis=0)


def colour_weights(w, small):
    k = iota((32, 384), 0)
    n = iota((32, 384), 1)
    copies = (((n >> 7) * 8 + (n & 7)) == k).astype(F32).astype(BF)
    for dy in range(3):
        w[dy * 128 : (dy + 1) * 128, :] = mm(small(dy).astype(BF), copies, 0, 0).astype(BF)


def to_colours(src, first, w):
    group = iota((WIDE, 128), 1) >> 3
    tile = jnp.zeros((WIDE, 128), F32)
    for half in range(2):
        v = conv_rows(src, first + half * 8, 8, w[...])
        for k in range(8):
            tile = jnp.where(group == half * 8 + k, v[k * WIDE : (k + 1) * WIDE], tile)
    return taller(tile).T


def patch_tile(v):
    after, before = pltpu.roll(v, 1, 1), pltpu.roll(v, 127, 1)
    none = jnp.zeros((8, 128), F32)
    parts = []
    for k in range(4):
        at = slice(k * 8, (k + 1) * 8)
        parts += [after[at], v[at], before[at], none]
    return jnp.concatenate(parts, axis=0).T[0:WIDE].astype(BF)


def patch_weights(w, small):
    w[...] = jnp.zeros(w.shape, BF)
    for k in range(4):
        for dy in range(3):
            w[(k + dy) * 32 : (k + dy + 1) * 32, k * 128 : (k + 1) * 128] = small(dy).astype(BF)


def from_colours(px, tile, count, w):
    at = [pl.ds(aligned((tile + k) * WIDE, 16), count * WIDE) for k in range(2)]
    return mm(jnp.concatenate([px[at[0], :], px[at[1], :]], axis=1), w[...])


def pack_rows_kernel(feats, target, low, high, own):
    lane = iota((TW, 128), 1)
    n = TGT_HALO
    colours = [wider(target[k].astype(F32)) for k in range(3)]
    for k in range(3):
        own[k] = colours[k].astype(BF)
    for out, y0, t0 in ((low, TH - FEAT_HALO, TH - n), (high, 0, 0)):
        extra = jnp.zeros((TW, 128), F32)
        for k in range(3):
            amount = (n * k - t0) % 128
            moved = pltpu.roll(colours[k], amount, 1) if amount else colours[k]
            extra = jnp.where((lane >= n * k) & (lane < n * k + n), moved, extra)
        out[0:FEAT_HALO] = feats[y0 : y0 + FEAT_HALO]
        out[FEAT_HALO] = extra.astype(BF)


def pack_sides_kernel(feats, own, top, bot, side_l, side_r, tall):
    lane = iota((TW, 128), 1)
    n = TGT_HALO
    above, below = top[FEAT_HALO].astype(F32), bot[FEAT_HALO].astype(F32)
    colours = []
    for k in range(3):
        first = pltpu.roll(above, 128 - n * k, 1) if k else above
        last = pltpu.roll(below, n + TH - n * k, 1)
        v = jnp.where(lane < n, first, pltpu.roll(own[k].astype(F32), n, 1))
        v = jnp.where(lane < n + TH, v, jnp.where(lane < 2 * n + TH, last, 0.0))
        tall[k] = v.astype(BF)
        colours.append(v)
    parts = (
        (0, top[0:FEAT_HALO]),
        (FEAT_HALO, feats[...]),
        (FEAT_HALO + TH, bot[0:FEAT_HALO]),
        (2 * FEAT_HALO + TH, jnp.stack(colours)),
    )
    for y, v in parts:
        v = v.astype(F32)
        for out, x0 in ((side_l, TW - COL_HALO), (side_r, 0)):
            out[y : y + v.shape[0]] = v[:, x0 : x0 + COL_HALO, :].astype(BF)


def decode_kernel(
    meta, top, mid, bot, left, right, w_mid, w_out, pay, dec, slope_out, s1, s2, w, w3
):
    r, c = meta[0], meta[1]
    for dy in range(3):
        for dx in range(3):
            w[dy * 128 : (dy + 1) * 128, dx * 128 : (dx + 1) * 128] = w_mid[dy, dx]
    colour_weights(w3, lambda dy: w_out[dy])

    def fill(first, rows, centre):
        n = rows * WIDE
        parts = [left[pl.ds(first, rows)], centre, right[pl.ds(first, rows)]]
        v = jnp.concatenate([p.astype(F32) for p in parts], axis=1).reshape(n, 128)
        s1[pl.ds(aligned(first * WIDE, 16), n), :] = (v * sigmoid(v)).astype(BF)

    fill(0, FEAT_HALO, top[0:FEAT_HALO])
    fill(FEAT_HALO + TH, FEAT_HALO, bot[0:FEAT_HALO])

    def fill_mid(i, carry):
        fill(FEAT_HALO + i * 8, 8, mid[pl.ds(i * 8, 8)])
        return carry

    lax.fori_loop(0, TH // 8, fill_mid, 0, unroll=True)
    col_ok = column_mask(c * TW - COL_HALO)

    def middle(i, carry):
        v = conv_rows(s1, i * 8, 8, w[...])
        act, slope = silu_parts(v)
        act = keep_inside(act, r * TH - 12 + i * 8, 8, col_ok)
        s2[pl.ds(aligned(i * 8 * WIDE, 16), 8 * WIDE), :] = act.astype(BF)
        slope = pltpu.roll(slope, 8 * WIDE - 6, 0).reshape(8, WIDE, 128).astype(BF)
        first, last = max(i * 8, 11), min(i * 8 + 8, 79)
        if first < last:
            slope_out[first - 11 : last - 11] = slope[first - i * 8 : last - i * 8]
        return carry

    for i in range(11):
        middle(i, 0)
    s2[88 * WIDE :, :] = jnp.zeros((10 * WIDE, 128), BF)
    dec[768:, :] = jnp.zeros((256, 128), F32)

    def colours(i, carry):
        v = to_colours(s2, i * 16, w3)
        ok = planar_inside(
            r * TH - DEC_HALO + i * 16, c * TW - COL_HALO, 2, WIDE - 2, 16, 86 - i * 16
        )
        dec[pl.ds(aligned(i * 128, 128), 128), :] = jnp.where(ok, v, 0.0).astype(BF).astype(F32)
        return carry

    lax.fori_loop(0, 6, colours, 0, unroll=True)
    planes = [
        dec[pl.ds(k, 128, stride=8), :].T[COL_HALO : COL_HALO + TW, :] for k in range(3)
    ]
    lane = iota((8, 128), 1)
    for half in range(2):
        tiles = [jnp.zeros((8, 128), F32) for _ in range(5)]
        for g in range(4):
            for k in range(3):
                piece = planes[k][g * 8 : (g + 1) * 8]
                if half:
                    piece = pltpu.roll(piece, 128 - SHARE, 1)
                piece = jnp.where(lane < SPAN, piece, 0.0)
                at, off = divmod((g * 3 + k) * SPAN, 128)
                if off:
                    piece = pltpu.roll(piece, off, 1)
                tiles[at] = tiles[at] + jnp.where(lane >= off, piece, 0.0)
                if off + SPAN > 128:
                    tiles[at + 1] = tiles[at + 1] + jnp.where(lane < off, piece, 0.0)
        packed = jnp.concatenate(tiles, axis=1).astype(BF)
        for k in range(COLS // 2):
            pay[2 * k + half] = packed


def percept_kernel(
    meta, dec, tall, left, right, v_first, v_second, weights, feat, slope_one, done,
    planes, px, one, w1, w2,
):
    r, c = meta[0], meta[1]
    col_first = c * TW - COL_HALO
    col_ok = column_mask(col_first)

    def first_small(dy):
        v = v_first[dy]
        return v + pltpu.roll(pltpu.roll(v, 3, 0), 64, 1)

    patch_weights(w1, first_small)
    for dy in range(3):
        for dx in range(3):
            v = v_second[dy, dx].astype(F32)
            v = jnp.concatenate([v, jnp.zeros((64, 64), F32)], axis=1)
            u = pltpu.roll(v, 64, 1)
            w2[dy * 128 : (dy + 1) * 128, dx * 128 : (dx + 1) * 128] = jnp.concatenate(
                [v, u], axis=0
            ).astype(BF)

    planes[...] = jnp.zeros(planes.shape, F32)
    for k in range(3):
        v = jnp.concatenate(
            [a.astype(F32) for a in (left[90 + k], tall[k], right[90 + k])], axis=0
        )
        planes[pl.ds(3 + k, 80, stride=8), :] = taller(v).T[0:80]

    done[...] = jnp.zeros((8, 128), F32)

    def gather(i, carry):
        v = dec[pl.ds(aligned(i * 32 + 40, 8), 32), :] + planes[pl.ds(aligned(i * 32, 32), 32), :]
        px[pl.ds(aligned(i * WIDE, 16), WIDE), :] = patch_tile(v)
        return carry

    lax.fori_loop(0, 19, gather, 0, unroll=True)
    px[19 * WIDE :, :] = jnp.zeros((WIDE, 128), BF)

    def first(tile, count):
        v = from_colours(px, tile, count, w1)
        for j in range(count):
            for k in range(4):
                p = (tile + j) * 4 + k
                x = v[j * WIDE : (j + 1) * WIDE, k * 128 : (k + 1) * 128]
                act, slope = silu_parts(x)
                act = keep_inside(act, r * TH - 5 + p, 1, col_ok)
                slope_one[pl.ds(aligned(p * WIDE, 16), WIDE), :] = slope.astype(BF)
                one[pl.ds(aligned(p * WIDE, 16), WIDE), :] = act.astype(BF)

    def first_group(i, carry):
        first(i * 4, 4)
        return carry

    lax.fori_loop(0, 4, first_group, 0, unroll=True)
    first(16, 3)
    ones = ((iota((128, 128), 0) >> 6) == (iota((128, 128), 1) >> 6)).astype(F32).astype(BF)

    def half_sum(v):
        return mm(v.astype(BF), ones)

    def second(i, carry):
        v = conv_rows(one, i * 8, 8, w2[...])
        f, slope = silu_parts(v)
        scale = lax.rsqrt(half_sum(f * f) + EPSILON)
        unit = f * scale
        weighted = weights[...] * (unit - pltpu.roll(unit, 64, 1))
        g = scale * (weighted - unit * half_sum(weighted * unit)) * slope
        g = keep_inside(g, r * TH - 4 + i * 8, 8, col_ok)
        feat[pl.ds(aligned(i * 8 * WIDE, 16), 8 * WIDE), :] = g.astype(BF)
        return carry

    lax.fori_loop(0, 9, second, 0, unroll=True)


def percept_back_kernel(
    meta, feat, slope_one, v_first, v_second, feats, w_mid, out, feats_slope, w,
    bv, w3, w4,
):
    r, c = meta[0], meta[1]
    col_ok = column_mask(c * TW - COL_HALO)

    def last_small(dy):
        parts = [v_first[2 - dy, (2 - dx) * 8 : (3 - dx) * 8, :] for dx in range(3)]
        return jnp.concatenate(parts + [jnp.zeros((8, 128), F32)], axis=0)

    colour_weights(w4, last_small)
    for dy in range(3):
        for dx in range(3):
            w[dx * 128 : (dx + 1) * 128, dy * 128 : (dy + 1) * 128] = w_mid[2 - dy, 2 - dx]

    def feature_slope(i, carry):
        at = pl.ds(i * 8, 8)
        feats_slope[at] = silu_parts(feats[at].astype(F32))[1].astype(BF)
        return carry

    lax.fori_loop(0, TH // 8, feature_slope, 0, unroll=2)
    for dy in range(3):
        for dx in range(3):
            v = v_second[dy, dx].astype(F32)
            v = jnp.concatenate([v, jnp.zeros((64, 64), F32)], axis=1)
            w3[(2 - dx) * 128 : (3 - dx) * 128, (2 - dy) * 128 : (3 - dy) * 128] = jnp.concatenate(
                [v, jnp.zeros((64, 128), F32)], axis=0
            ).astype(BF)

    def back(i, carry):
        v = conv_rows(feat, i * 10, 10, w3[...], transposed=True)
        x = slope_one[pl.ds(aligned((i * 10 + 2) * WIDE, 16), 10 * WIDE), :]
        v = keep_inside(v * x.astype(F32), r * TH - 3 + i * 10, 10, col_ok)
        bv[pl.ds(aligned(i * 10 * WIDE, 16), 10 * WIDE), :] = v.astype(BF)
        return carry

    lax.fori_loop(0, 7, back, 0, unroll=True)
    bv[70 * WIDE :, :] = jnp.zeros((12 * WIDE, 128), BF)

    def colours(i, carry):
        v = to_colours(bv, i * 16, w4)
        out[pl.ds(aligned(i * 128, 128), 128), :] = pltpu.roll(v, 122, 1)
        return carry

    lax.fori_loop(0, 5, colours, 0, unroll=True)


STOP = object()
FAR = 16
STEPS = 6
HALF = STEPS + 1
TILES = 2 * HALF
LANES = TILES * 128
EVEN = HALF * 128


def critic_kernel(
    meta, strip, mine, other, far, far_other, _, out,
    strip32, grads, w_pre, w_one, w_two, w_back, score, distance, row_gap, row_gap_back, *rest,
):
    x_all, pre, act, two, cols = (rest[k * 4 : (k + 1) * 4] for k in range(5))
    jobs = rest[20]
    r, me = meta[0], meta[1]
    first_row = r * TH - 2 + SHARE * (me & 1)
    lane = iota((1, 128), 1)
    upper = lane >= 64
    first_x = (lane & 63) == 0
    last_x = (lane & 63) == 63

    def unpack(k, carry):
        v = strip[k].astype(F32)

        def piece(g, j, place):
            at, off = divmod((g * 3 + j) * SPAN, 128)
            amount = (place - off) % 128
            parts = [v[:, at * 128 : (at + 1) * 128]]
            if off + SPAN > 128:
                parts.append(v[:, (at + 1) * 128 : (at + 2) * 128])
            parts = [pltpu.roll(p, amount, 1) if amount else p for p in parts]
            if len(parts) == 1:
                return parts[0]
            return jnp.where(lane < place + 128 - off, parts[0], parts[1])

        for g in range(4):
            both = jnp.where(upper, piece(g, 1, 64), piece(g, 0, 0))
            row = jnp.concatenate([both, piece(g, 2, 0)], axis=1)
            strip32[pl.ds(aligned(k * TW + g * 8, 8), 8), :] = row
        return carry

    lax.fori_loop(0, COLS, unpack, 0, unroll=True)
    strip32[IMG_W:, :] = jnp.zeros((8, 256), F32)
    grads[...] = jnp.zeros(grads.shape, F32)
    w_back[...] = jnp.zeros(w_back.shape, BF)
    for g, source in enumerate((mine, other, far, far_other)):
        w_one[g] = source[1024:1120, :]
        w_pre[g] = (0.5 * taller(source[1024:1120, :].astype(F32))).T.astype(BF)
        score[g] = taller(source[1120:1136, :].astype(F32)).T
        for i in range(4):
            first, second = (
                source[i * 256 + k * 128 : i * 256 + (k + 1) * 128, :].astype(F32).T
                for k in range(2)
            )
            at = slice((i // 2) * 128, (i // 2 + 1) * 128)
            w_two[g, i % 2, 0:128, at] = jnp.where(upper, first, second).astype(BF)
            w_two[g, i % 2, 128:256, at] = jnp.where(upper, 0.0, first).astype(BF)
            w_two[g, i % 2, 256:384, at] = jnp.where(upper, second, 0.0).astype(BF)
        for par in range(2):
            for p in range(2):
                for t in range(2):
                    i = par + 2 * t
                    for kind, j in ((0, 1 + p), (1 + p, 3 - 3 * p)):
                        w_back[
                            g,
                            (par * 2 + 1 - p) * 64 : (par * 2 + 2 - p) * 64,
                            (t * 3 + kind) * 128 : (t * 3 + kind + 1) * 128,
                        ] = 0.5 * source[i * 256 + j * 64 : i * 256 + (j + 1) * 64, :]
    for t in two:
        t[:, 0:128] = jnp.zeros((384, 128), BF)
        t[:, (STEPS + 1) * 128 :] = jnp.zeros((384, 128), BF)
    for t in cols:
        t[192:, :] = jnp.zeros((64, 384), F32)
    x, n = iota((CROP + 8, 384), 0), iota((CROP + 8, 384), 1)
    wanted = 4 * (n & 63) + (n >> 6) - 1
    wanted_ok = (wanted >= 0) & (wanted < CROP)
    distance[...] = jnp.where(wanted_ok, x - wanted, -1).astype(F32)

    def gap(dims, rho, n):
        tile, i, k = rho >> 4, (rho >> 2) & 3, rho & 3
        u = 2 * jnp.where(tile >= HALF, tile - HALF, tile) + jnp.where(tile >= HALF, 1, 0)
        return jnp.where(k < 3, n - (k * 40 + 2 * u + i), -1).astype(F32)

    dims = (TILES * 16, 128)
    row_gap[...] = gap(dims, iota(dims, 0), iota(dims, 1))
    dims = (128, TILES * 16)
    row_gap_back[...] = gap(dims, iota(dims, 1), iota(dims, 0))
    wide = iota((1, 256), 1)

    def anchor(q, k):
        return meta[2 + 2 * q + k]

    def owner_of(q):
        return meta[2 + 2 * CROPS + q]

    def job(q, x_all, pre, act, two, cols):
        top, left, apart = anchor(q, 0), anchor(q, 1), owner_of(q) ^ me
        g = (apart & 1) + 2 * ((apart // FAR) & 1)
        y0 = first_row - top
        v0 = lax.shift_right_arithmetic(y0 - 3, 2)
        e = 4 * v0 - y0 + 6
        crop_row = y0 - 9 + (wide & 63)
        in_crop = (crop_row >= 0) & (crop_row < CROP) & (wide < 192)
        here = pl.ds(aligned((left >> 3) * 8, 8), CROP + 8)
        window = jnp.where(in_crop, strip32[here, :], 0.0).astype(BF)
        pick = jnp.where(distance[...] == (left & 7).astype(F32), 1.0, 0.0).astype(BF)
        cols_of = mm(window, pick, 0, 0)
        none = jnp.zeros((8, 384), F32)
        halves = [
            jnp.concatenate(
                [cols_of[k * 64 + 24 * h : k * 64 + 24 * h + 40, :] for k in range(3)] + [none],
                axis=0,
            )
            for h in range(2)
        ]
        mixed = []
        for m in range(6):
            tile = slice((m // 2) * 128, (m // 2 + 1) * 128)
            low, high = halves[0][:, tile], halves[1][:, tile]
            if m % 2 == 0:
                high = pltpu.roll(high, 64, 1)
            else:
                low = pltpu.roll(low, 64, 1)
            mixed.append(jnp.where(upper, high, low))
        yield
        chosen = jnp.where(row_gap[...] == e.astype(F32), 1.0, 0.0).astype(BF)
        patches = mm(chosen, jnp.concatenate(mixed, axis=1).astype(BF)).astype(BF)
        for t in range(TILES):
            for m in range(6):
                x_all[m * 16 : (m + 1) * 16, t * 128 : (t + 1) * 128] = patches[
                    t * 16 : (t + 1) * 16, m * 128 : (m + 1) * 128
                ]
        yield
        weight = w_pre[g][:, 0:96]
        for t0 in range(0, TILES, 2):
            at = slice(t0 * 128, (t0 + 2) * 128)
            value = mm(weight, x_all[:, at])
            for t in range(t0, t0 + 2):
                at = slice(t * 128, (t + 1) * 128)
                n = 2 * (t % HALF) + t // HALF + jnp.where(upper, 2 * STEPS, 0)
                u = 2 * v0 - 1 + n
                ok = ((u >= 0) & (u < CROP // 2)).astype(F32)
                half = value[:, (t - t0) * 128 : (t - t0 + 1) * 128]
                rise = jnp.tanh(half) + 1.0
                kept = rise * ok
                pre[:, at] = kept * (1.0 + half * (2.0 - rise))
                act[:, at] = (half * kept).astype(BF)
            yield
        column = score[g][:, 0:1]
        for t0 in range(0, STEPS, 2):
            value = 0.0
            for par in range(2):
                at = par * EVEN + t0 * 128
                taps = jnp.concatenate(
                    [act[:, at : at + 256], act[:, at + 128 : at + 384]], axis=0
                )
                value = value + mm(w_two[g, par], taps)
            for t in range(t0, t0 + 2):
                at = slice((t - t0) * 128, (t - t0 + 1) * 128)
                f = value[0:128, at]
                f = f + jnp.where(first_x, 0.0, pltpu.roll(value[128:256, at], 1, 1))
                f = f + jnp.where(last_x, 0.0, pltpu.roll(value[256:384, at], 127, 1))
                f, slope = silu_parts(f)
                logit = jnp.sum(f * column, axis=0, keepdims=True)
                v = v0 + t + jnp.where(upper, STEPS, 0)
                ok = (v >= 0) & (v < CROP // 4)
                grad = jnp.where(ok, -LOSS_SCALE * sigmoid(-logit), 0.0)
                b = grad * (column * slope)
                at = slice((t + 1) * 128, (t + 2) * 128)
                two[0:128, at] = b.astype(BF)
                two[128:256, at] = jnp.where(first_x, 0.0, pltpu.roll(b, 1, 1)).astype(BF)
                two[256:384, at] = jnp.where(last_x, 0.0, pltpu.roll(b, 127, 1)).astype(BF)
            yield
        for s0 in range(0, HALF, 2):
            n = min(2, HALF - s0) * 128
            at = s0 * 128
            both = jnp.concatenate([two[:, 128 + at : 128 + at + n], two[:, at : at + n]], axis=0)
            up = mm(w_back[g], both)
            for par in range(2):
                here = slice(par * EVEN + at, par * EVEN + at + n)
                one = (up[par * 128 : (par + 1) * 128] * pre[:, here]).astype(BF)
                x_all[:, here] = mm(w_one[g], one).astype(BF)
            yield
        spread = jnp.concatenate(
            [
                jnp.concatenate(
                    [
                        x_all[m * 16 : (m + 1) * 16, t * 128 : (t + 1) * 128]
                        for t in range(TILES)
                    ],
                    axis=0,
                )
                for m in range(6)
            ],
            axis=1,
        )
        chosen = jnp.where(row_gap_back[...] == e.astype(F32), 1.0, 0.0).astype(BF)
        back = mm(chosen, spread)
        yield
        parts = []
        for h in range(2):
            tiles = []
            for k in range(3):
                low = back[:, 2 * k * 128 : (2 * k + 1) * 128]
                high = back[:, (2 * k + 1) * 128 : (2 * k + 2) * 128]
                if h == 0:
                    high = pltpu.roll(high, 64, 1)
                else:
                    low = pltpu.roll(low, 64, 1)
                tiles.append(jnp.where(upper, high, low))
            parts.append(jnp.concatenate(tiles, axis=1))
        for k in range(3):
            low, high = (part[k * 40 : (k + 1) * 40, :] for part in parts)
            cols[k * 64 : (k + 1) * 64, :] = jnp.concatenate(
                [low[0:24], low[24:40] + high[0:16], high[16:40]], axis=0
            )
        yield
        placed = mm(pick, cols[...].astype(BF), 1, 1)
        y = wide & 63
        keep = in_crop & (y >= 9) & (y < 9 + SHARE)
        yield
        here = pl.ds(aligned((left >> 3) * 8 + GRAD_PAD, 8), CROP + 8)
        grads[here, :] = grads[here, :] + jnp.where(keep, placed, 0.0)

    count, seen, turn = jnp.int32(0), jnp.int32(0), (me // FAR) & 1
    for q in range(CROPS):
        y0 = first_row - anchor(q, 0)
        shared = ((owner_of(q) ^ me) & (COLS - 2 - FAR)) == 0
        shared = (shared & (y0 < CROP) & (y0 + SHARE > 0)).astype(jnp.int32)
        jobs[count] = q
        count = count + shared * ((seen & 1) == turn).astype(jnp.int32)
        seen = seen + shared

    sets = tuple(zip(x_all, pre, act, two, cols))

    def crops(first, number):
        running = [job(jobs[first + k], *sets[k]) for k in range(number)]
        while running:
            running = [g for g in running if next(g, STOP) is not STOP]

    def four_crops(k, carry):
        crops(4 * k, 4)
        return carry

    lax.fori_loop(0, count >> 2, four_crops, 0)

    @pl.when((count & 2) == 2)
    def _():
        crops((count >> 2) * 4, 2)

    @pl.when((count & 1) == 1)
    def _():
        crops(count - 1, 1)

    def pack(k, carry):
        block = grads[pl.ds(aligned(k * TW, 32), 48), :][GRAD_PAD - 2 : GRAD_PAD + 38]
        a, b = block[:, 0:128], block[:, 128:256]
        out[k] = jnp.where(
            lane < 40,
            pltpu.roll(a, 128 - 9, 1),
            jnp.where(lane < 80, pltpu.roll(a, 128 - 33, 1), pltpu.roll(b, 71, 1)),
        ).astype(BF)
        return carry

    lax.fori_loop(0, COLS, pack, 0, unroll=True)


def finish_kernel(
    meta, parts, lpips, slope, feats_slope, w, w_out, out, turned, planes, px, bm, w1
):
    r, c = meta[0], meta[1]
    def small(dy):
        flipped = [w_out[2 - dy, (2 - dx) * 8 : (3 - dx) * 8, :] for dx in range(3)]
        return jnp.concatenate(flipped + [jnp.zeros((8, 128), F32)], axis=0)

    patch_weights(w1, small)
    col_ok = column_mask(c * TW - 2)
    planes[...] = jnp.zeros(planes.shape, F32)
    for half in range(2):
        total = parts[half].astype(F32)
        for k in range(1, COLS // 2):
            total = total + parts[2 * k + half].astype(F32)
        turned[...] = taller(total).T
        for k in range(3):
            planes[pl.ds(half * SHARE * 8 + k, 40, stride=8), :] = turned[k * 40 : (k + 1) * 40, :]

    def gather(i, carry):
        at = pl.ds(aligned(i * 32, 32), 32)
        ok = planar_inside(r * TH - 2 + i * 4, c * TW - 2, 0, 36, 4, 4)
        px[pl.ds(aligned(i * WIDE, 16), WIDE), :] = patch_tile(
            jnp.where(ok, lpips[at, :] + planes[at, :], 0.0)
        )
        return carry

    lax.fori_loop(0, 17, gather, 0, unroll=True)
    px[17 * WIDE :, :] = jnp.zeros((WIDE, 128), BF)

    def middle(tile, count):
        v = from_colours(px, tile, count, w1)
        for j in range(count):
            for k in range(4):
                n = (tile + j) * 4 + k
                x = v[j * WIDE : (j + 1) * WIDE, k * 128 : (k + 1) * 128]
                x = keep_inside(x * slope[n].astype(F32), r * TH - 1 + n, 1, col_ok)
                bm[pl.ds(aligned(n * WIDE, 16), WIDE), :] = x.astype(BF)

    def middle_group(i, carry):
        middle(i * 4, 4)
        return carry

    lax.fori_loop(0, 4, middle_group, 0, unroll=True)
    middle(16, 1)

    def last(i, carry):
        v = conv_rows(bm, i * 8, 8, w[...], transposed=True, shift=2)
        v = v.reshape(8, WIDE, 128)[:, 0:TW, :]
        at = pl.ds(i * 8, 8)
        out[at] = (v * feats_slope[at].astype(F32)).astype(BF)
        return carry

    lax.fori_loop(0, TH // 8, last, 0, unroll=True)


def call(kernel, outs, scratch, args, scalars=1, unused=0, lists=(), vmem=VMEM):
    specs = [pl.BlockSpec(memory_space=pltpu.SMEM)] * scalars
    specs += [pl.BlockSpec(memory_space=pltpu.VMEM)] * (len(args) - scalars - unused)
    specs += [pl.BlockSpec(memory_space=pl.ANY)] * unused
    return pl.pallas_call(
        kernel,
        in_specs=specs,
        out_specs=jax.tree.map(lambda _: pl.BlockSpec(memory_space=pltpu.VMEM), outs),
        out_shape=outs,
        scratch_shapes=[pltpu.VMEM(s, t) for s, t in scratch] + list(lists),
        compiler_params=pltpu.CompilerParams(vmem_limit_bytes=vmem),
        interpret=INTERPRET,
    )(*args)


INTERPRET = False


def shape(dims, kind):
    return jax.ShapeDtypeStruct(dims, kind)


def colour_first(w):
    w = jnp.pad(w.astype(F32), ((0, 0), (0, 1), (0, 5), (0, 128 - w.shape[-1])))
    return w.reshape(3, 32, 128)


def decode(meta, top, mid, bot, left, right, conv_mid, small):
    return call(
        decode_kernel,
        (
            shape((COLS, TW // 4, 640), BF),
            shape((1024, 128), F32),
            pltpu.HBM((68, WIDE, 128), BF),
        ),
        [((90 * WIDE, 128), BF), ((98 * WIDE, 128), BF), ((384, 384), BF), ((384, 384), BF)],
        (meta, top, mid, bot, left, right, conv_mid, small),
    )


def percept(meta, dec, tall, left, right, small, vgg_second, weights):
    scaled = jnp.pad(2.0 * LOSS_SCALE * weights, (0, 64)).reshape(1, 128)
    return call(
        percept_kernel,
        (
            pltpu.HBM((72 * WIDE, 128), BF),
            pltpu.HBM((76 * WIDE, 128), BF),
            shape((8, 128), F32),
        ),
        [
            ((80 * 8, 128), F32),
            ((20 * WIDE, 128), BF),
            ((76 * WIDE, 128), BF),
            ((256, 512), BF),
            ((384, 384), BF),
        ],
        (meta, dec, tall, left, right, small, vgg_second, scaled),
    )


def percept_back(meta, feat, slope_one, small, vgg_second, feats, conv_mid):
    return call(
        percept_back_kernel,
        (
            shape((80 * 8, 128), F32),
            shape((TH, TW, 128), BF),
            shape((384, 384), BF),
        ),
        [((82 * WIDE, 128), BF), ((384, 384), BF), ((384, 384), BF)],
        (meta, feat, slope_one, small, vgg_second, feats, conv_mid),
    )


def critic_weights(first, second, score):
    w = jnp.pad(first, ((0, 0), (0, 0), (0, 1), (0, 0)))
    w = jnp.transpose(w, (1, 0, 2, 3)).reshape(4, 16, 64)
    w = jnp.concatenate(
        [jnp.pad(w, ((2, 0), (0, 0), (0, 0))), jnp.pad(w, ((0, 2), (0, 0), (0, 0)))], -1
    ).reshape(96, 128)
    score = jnp.pad(score[None], ((0, 15), (0, 0)))
    return jnp.concatenate([second.reshape(1024, 128), w, score], 0)


def critics(meta, strip, weights, after):
    pair = [
        ((96, LANES), BF),
        ((128, LANES), F32),
        ((128, LANES), BF),
        ((384, (STEPS + 2) * 128), BF),
        ((256, 384), F32),
    ]
    return call(
        critic_kernel,
        shape((COLS, 40, 128), BF),
        [
            ((IMG_W + 8, 256), F32),
            ((IMG_W + 24, 256), F32),
            ((4, 128, 128), BF),
            ((4, 96, 128), BF),
            ((4, 2, 384, 256), BF),
            ((4, 256, 768), BF),
            ((4, 128, 128), F32),
            ((CROP + 8, 384), F32),
            ((TILES * 16, 128), F32),
            ((128, TILES * 16), F32),
        ]
        + [buffer for buffer in pair for _ in range(4)],
        (meta, strip, *weights, after),
        unused=1,
        lists=[pltpu.SMEM((CROPS,), jnp.int32)],
        vmem=30 * 1024 * 1024,
    )


def finish(meta, parts, lpips, slope, feats_slope, w, small):
    return call(
        finish_kernel,
        shape((TH, TW, 128), BF),
        [
            ((128, 128), F32),
            ((80 * 8, 128), F32),
            ((18 * WIDE, 128), BF),
            ((68 * WIDE, 128), BF),
            ((256, 512), BF),
        ],
        (meta, parts, lpips, slope, feats_slope, w, small),
    )


def in_hbm(x):
    return pltpu.with_memory_space_constraint(x, pltpu.HBM)


def exchange(low, high, axis):
    count = lax.axis_size(axis)
    forward = [(i, i + 1) for i in range(count - 1)]
    backward = [(target, source) for source, target in forward]
    return lax.ppermute(low, axis, forward), lax.ppermute(high, axis, backward)


def local(
    features, conv_mid, conv_out, target, vgg_first, vgg_second, perceptual_weights,
    crop_anchors, crop_owner, critic_first, critic_second, critic_score,
):
    meta = jnp.concatenate(
        [
            jnp.stack([lax.axis_index("row"), lax.axis_index("col")]).astype(jnp.int32),
            crop_anchors.reshape(2 * CROPS),
            crop_owner.reshape(CROPS),
        ]
    )
    feats = features[0]
    planar = jnp.transpose(target[0], (2, 1, 0))

    low, high, own = call(
        pack_rows_kernel,
        (shape((FEAT_HALO + 1, TW, 128), BF),) * 2 + (shape((3, TW, 128), BF),),
        [],
        (in_hbm(feats), in_hbm(planar)),
        scalars=0,
    )
    top, bot = exchange(low, high, "row")
    side_l, side_r, tall = call(
        pack_sides_kernel,
        (shape((2 * FEAT_HALO + TH + 3, COL_HALO, 128), BF),) * 2 + (shape((3, TW, 128), BF),),
        [],
        (feats, own, top, bot),
        scalars=0,
    )
    left, right = exchange(side_l, side_r, "col")
    out_small = colour_first(jnp.transpose(conv_out, (0, 1, 3, 2)))
    vgg_small = colour_first(vgg_first)
    mine = critic_weights(critic_first[0], critic_second[0], critic_score[0])
    left, right, sent, meta, out_small = lax.optimization_barrier(
        (left, right, mine, meta, out_small)
    )
    far = lax.ppermute(sent, "col", [(i, i ^ FAR) for i in range(COLS)])
    pay, dec, slope = decode(meta, top, feats, bot, left, right, conv_mid, out_small)
    pay, far = lax.optimization_barrier((pay, far))
    strip = lax.all_to_all(pay, "col", split_axis=0, concat_axis=0, tiled=True)
    other = lax.ppermute(mine, "col", [(i, i ^ 1) for i in range(COLS)])
    far_other = lax.ppermute(far, "col", [(i, i ^ 1) for i in range(COLS)])
    feat, slope_one, done = percept(
        meta, dec, tall, left, right, vgg_small, vgg_second, perceptual_weights
    )
    grads = critics(meta, strip, (mine, other, far, in_hbm(far_other)), done)
    parts = lax.all_to_all(grads, "col", split_axis=0, concat_axis=0, tiled=True)
    lpips, *made = percept_back(
        meta, in_hbm(feat), in_hbm(slope_one), vgg_small, vgg_second, feats, conv_mid
    )
    return finish(meta, parts, lpips, slope, *made, out_small)[None]


def solution(mesh):
    placed = (
        P(None, "row", "col", None),
        P(),
        P(),
        P(None, "row", "col", None),
        P(),
        P(),
        P(),
        P(),
        P(),
        P("col", None, None, None, None),
        P("col", None, None, None, None),
        P("col", None),
    )
    return jax.shard_map(
        local, mesh=mesh, in_specs=placed, out_specs=P(None, "row", "col", None), check_vma=False
    )
```
